32 devices in a mesh: section: 2 (over x), dp: 4 (over y, core), rep: 4 (over z).
Axes of the slice: x: 2, y: 2, z: 4, core: 2. Of those that a mesh axis runs over, the one named last changes fastest.
Arguments:
- query_input: bfloat16 [64, 256, 768], P(('dp', 'rep')), may hold values from -6 to 6
- key_input: bfloat16 [64, 256, 768], P(('dp', 'rep')), may hold values from -6 to 6
- query_lengths: int32 [64], P(('dp', 'rep')), may hold values from 64 to 256, as said below
- key_lengths: int32 [64], P(('dp', 'rep')), may hold values from 64 to 256, as said below
- cotangent: bfloat16 [64, 256, 768], P(('dp', 'rep')), may hold values from -8 to 8
- w_qkv: bfloat16 [2, 2, 768, 2304], P('section'), may hold values from -0.21875 to 0.21875
- w_out: bfloat16 [2, 2, 768, 768], P('section'), may hold values from -1.25 to 1.25
- w_up: bfloat16 [2, 2, 768, 3072], P('section'), may hold values from -0.21875 to 0.21875
- w_down: bfloat16 [2, 2, 3072, 768], P('section'), may hold values from -0.109375 to 0.109375
- b_up: float32 [2, 2, 3072], P('section'), may hold values from -1.5 to 1.5
- biases: float32 [2, 2, 6, 768], P('section'), may hold values from -1.5 to 1.5
- gains: float32 [2, 2, 2, 768], P('section'), may hold values from 0.25 to 1.75
Outputs:
- pooled_query: float32 [2, 64, 768], P('section')
- pooled_key: float32 [2, 64, 768], P('section')
- input_grad: float32 [2, 64, 256, 768], P('section', ('dp', 'rep'))
- grad_qkv: float32 [2, 768, 2304], P('section')
- grad_out: float32 [2, 768, 768], P('section')
- grad_up: float32 [2, 768, 3072], P('section')
- grad_down: float32 [2, 3072, 768], P('section')
- grad_b_up: float32 [2, 3072], P('section')
- grad_biases: float32 [2, 6, 768], P('section')
- grad_gains: float32 [2, 2, 768], P('section')
The draws below stay inside these ranges and needn't reach their ends.
Inputs may be any that keep to these rules, and one draw needn't show every extreme that they name: `query_lengths`: positions before a crop's length are tokens, the rest padding; in every draw some crop has length 256 and some crop has length 64. `key_lengths`: as for query_lengths, drawn independently.
All inputs are finite; a program needn't handle non-finite values.
Results may differ from the reference program's by a relative error of at most 0.018.
Values may be sent and summed in bfloat16 or wider, within the bound.
No kernel may reach another device: no remote copies, remote signals or barrier semaphores. Data moves between devices by JAX's collectives and lax.ppermute only.
A program may use at most 384 MiB of HBM per device.

```python
import math
import jax
import jax.numpy as jnp
from jax import lax

D = 768
HEADS = 12
HEAD = 64
FF = 3072
CROP = 256
MINLEN = 64
CROPS = 64


def skewed_lengths(key):
    span = CROP - MINLEN
    parts = jax.random.split(key, 4)
    alpha = jax.random.randint(parts[0], (CROPS,), 0, span + 1)
    beta = jax.random.randint(parts[1], (CROPS,), 0, span + 1)
    lengths = MINLEN + alpha * (span + beta) // (2 * span)
    longest = jax.random.randint(parts[2], (), 0, CROPS)
    offset = jax.random.randint(parts[3], (), 1, CROPS)
    shortest = (longest + offset) % CROPS
    lengths = lengths.at[longest].set(CROP).at[shortest].set(MINLEN)
    return lengths.astype(jnp.int32)


def draw_query_lengths(key, part):
    key = jax.random.fold_in(key, 11)
    return skewed_lengths(key)


def draw_key_lengths(key, part):
    key = jax.random.fold_in(key, 12)
    return skewed_lengths(key)


def draw_cotangent(key, part):
    key = jax.random.fold_in(key, 23)
    parts = jax.random.split(key, 1)
    rising = 3.0 ** (jnp.arange(CROPS, dtype=jnp.float32) / CROPS)
    noise = jax.random.normal(parts[0], (CROPS, CROP, D), jnp.float32)
    return (jnp.clip(noise, -4.0, 4.0) * rising[:, None, None] / 1.5).astype(jnp.bfloat16)


def shard_levels(key, shape, pieces, low, top_value):
    factor_of = 1.0
    for position, blocks in pieces:
        heights = jax.random.uniform(jax.random.fold_in(jax.random.fold_in(key, 6), position), (blocks,), jnp.float32, low / len(pieces), top_value / len(pieces))
        factor_of = factor_of * jnp.repeat(jnp.exp(heights), shape[position] // blocks).reshape((-1,) + (1,) * (len(shape) - 1 - position))
    return factor_of


def gaussian(stream_key, extent, scale, bound, cuts=(), kind=jnp.bfloat16):
    entries = jax.random.normal(stream_key, extent, jnp.float32) * scale
    if len(cuts) > 0:
        entries = shard_levels(stream_key, extent, cuts, -0.22, 0.18) * entries
    return jnp.clip(entries, min=-bound, max=bound).astype(kind)


def setup_inputs(seed: int = 0) -> dict:
    splits = jax.random.split(jax.random.key(seed), 13)
    return {
        "query_input": gaussian(splits[0], (CROPS, CROP, D), 1.0, 6.0, ((0, 16),)),
        "key_input": gaussian(splits[1], (CROPS, CROP, D), 1.0, 6.0, ((0, 16),)),
        "query_lengths": draw_query_lengths(jax.random.fold_in(splits[12], 71), 0),
        "key_lengths": draw_key_lengths(jax.random.fold_in(splits[12], 71), 0),
        "cotangent": draw_cotangent(jax.random.fold_in(splits[12], 71), 0),
        "w_qkv": gaussian(splits[5], (2, 2, D, 3 * D), D ** -0.5, 0.21875, ((0, 2),)),
        "w_out": gaussian(splits[6], (2, 2, D, D), (D // 32) ** -0.5, 1.25, ((0, 2),)),
        "w_up": gaussian(splits[7], (2, 2, D, FF), D ** -0.5, 0.21875, ((0, 2),)),
        "w_down": gaussian(splits[8], (2, 2, FF, D), FF ** -0.5, 0.109375, ((0, 2),)),
        "b_up": gaussian(splits[9], (2, 2, FF), 0.3, 1.5, ((0, 2),), jnp.float32),
        "biases": gaussian(splits[10], (2, 2, 6, D), 0.3, 1.5, ((0, 2),), jnp.float32),
        "gains": jnp.clip(1.0 + 0.15 * jax.random.normal(splits[11], (2, 2, 2, D), jnp.float32), 0.25, 1.75),
    }


@jax.custom_vjp
def low(v):
    return lax.optimization_barrier(v.astype(jnp.bfloat16)).astype(jnp.float32)

@jax.custom_vjp
def low_back(v):
    return v

def low_keep(v):
    return (low(v), None)

def low_pass(kept, grad):
    return (grad,)

def back_keep(v):
    return (v, None)

def back_low(kept, grad):
    return (low(grad),)
low.defvjp(low_keep, low_pass)
low_back.defvjp(back_keep, back_low)
EPS = 1e-06
NEG = -1000000000.0

def rounded_both(values):
    return low(low_back(values))

def layer_norm(hidden, norm_gain, norm_shift):
    centred = hidden - lax.optimization_barrier(jnp.mean(hidden, -1, keepdims=True))
    inverse = lax.rsqrt(lax.optimization_barrier(jnp.mean(centred * centred, -1, keepdims=True)) + EPS)
    return centred * inverse * norm_gain + norm_shift

def block(inputs, valid, weights):
    w_qkv, w_out, w_up, w_down, b_up, biases, gains = weights
    crop_count, crop_len, model_width = inputs.shape
    heads_shape = (crop_count, crop_len, HEADS, HEAD)
    highest = lax.Precision.HIGHEST
    projected = jnp.einsum('cld,de->cle', low(inputs), w_qkv, precision=highest)
    queries = rounded_both(projected[..., :model_width] + biases[0]).reshape(heads_shape)
    key_heads = rounded_both(projected[..., model_width:2 * model_width]).reshape(heads_shape)
    values = rounded_both(projected[..., 2 * model_width:] + biases[1]).reshape(heads_shape)
    scores = low_back(jnp.einsum('cqhe,ckhe->chqk', queries, key_heads, precision=highest) * HEAD ** (-0.5))
    scores = jnp.where(valid[:, None, None, :], scores, NEG)
    attention = low(jax.nn.softmax(scores, axis=-1))
    mixture = rounded_both(jnp.einsum('chqk,ckhe->cqhe', attention, values, precision=highest).reshape(crop_count, crop_len, model_width))
    attended = low_back(jnp.einsum('cld,de->cle', mixture, w_out, precision=highest) + biases[2])
    after_attn = layer_norm(inputs + attended, gains[0], biases[3])
    pre_active = low_back(jnp.einsum('cld,df->clf', low(after_attn), w_up, precision=highest) + b_up)
    active = low(jax.nn.gelu(pre_active, approximate=False))
    branch = low_back(jnp.einsum('clf,fd->cld', active, w_down, precision=highest) + biases[4])
    return layer_norm(after_attn + branch, gains[1], biases[5])

def pooled_of(block_out, weights_mask, lengths):
    return lax.optimization_barrier(jnp.sum(block_out * weights_mask[..., None], 1)) / lengths.astype(block_out.dtype)[:, None]

def reference(query_input, key_input, query_lengths, key_lengths, cotangent, w_qkv, w_out, w_up, w_down, b_up, biases, gains):
    arrays = [source.astype(jnp.float32) for source in (w_qkv, w_out, w_up, w_down, b_up, biases, gains)]

    def select_block(section_number, member):
        return tuple((source[section_number, member] for source in arrays))
    group_size = math.gcd(CROPS, 16)
    group_count = CROPS // group_size

    def grouped(source):
        return source.reshape((group_count, group_size) + source.shape[1:])
    positions = jnp.arange(CROP, dtype=jnp.int32)
    query_valid = positions[None, :] < query_lengths[:, None]
    key_valid = positions[None, :] < key_lengths[:, None]
    query_float = query_input.astype(jnp.float32)
    key_float = key_input.astype(jnp.float32)
    cot_float = cotangent.astype(jnp.float32)
    boundary = jnp.zeros_like(query_float)

    def query_loss(inputs, shift_term, lower_weights, upper_weights):

        def group_step(carry, items):
            inputs_part, shift_part, valid_part, length_part, cot_part = items
            lower_out = block(inputs_part, valid_part, lower_weights)
            upper_in = low_back(low(lower_out) + shift_part)
            upper_out = block(upper_in, valid_part, upper_weights)
            weights_mask = valid_part.astype(inputs_part.dtype)
            loss_part = jnp.sum(cot_part * weights_mask[..., None] * upper_out)
            return (carry + loss_part, (pooled_of(lower_out, weights_mask, length_part), pooled_of(upper_out, weights_mask, length_part)))
        loss_total, pools = lax.scan(jax.checkpoint(group_step), jnp.zeros((), jnp.float32), (grouped(inputs), grouped(shift_term), grouped(query_valid), grouped(query_lengths), grouped(cot_float)))
        return (loss_total, pools)
    loss_value, back_fn, query_pools = jax.vjp(query_loss, query_float, boundary, select_block(0, 0), select_block(1, 0), has_aux=True)
    input_lower, input_upper, grads_lower, grads_upper = back_fn(jnp.ones((), loss_value.dtype))
    key_lower_w = select_block(0, 1)
    key_upper_w = select_block(1, 1)

    def key_step(carry, items):
        inputs_part, valid_part, length_part = items
        lower_out = block(inputs_part, valid_part, key_lower_w)
        upper_out = block(low(lower_out), valid_part, key_upper_w)
        weights_mask = valid_part.astype(inputs_part.dtype)
        return (carry, (pooled_of(lower_out, weights_mask, length_part), pooled_of(upper_out, weights_mask, length_part)))
    unused_carry, key_pools = lax.scan(key_step, jnp.zeros((), jnp.float32), (grouped(key_float), grouped(key_valid), grouped(key_lengths)))
    width = query_input.shape[2]
    pooled_query = jnp.stack([query_pools[0].reshape(CROPS, width), query_pools[1].reshape(CROPS, width)])
    pooled_key = jnp.stack([key_pools[0].reshape(CROPS, width), key_pools[1].reshape(CROPS, width)])
    input_grad = jnp.stack([input_lower, input_upper])
    stacked = [jnp.stack([grads_lower[number], grads_upper[number]]) for number in range(7)]
    return (pooled_query, pooled_key, input_grad, stacked[0], stacked[1], stacked[2], stacked[3], stacked[4], stacked[5], stacked[6])
```

```python
import functools
import math

import jax
import jax.numpy as jnp
from jax import lax
from jax.experimental import pallas as pl
from jax.experimental.pallas import tpu as pltpu
from jax.sharding import PartitionSpec as P

HEAD = 64
EPS = 1e-06
NEG = -1000000000.0
CHUNK = 256
VMEM_LIMIT = 60 * 1024 * 1024
NT = (((1,), (1,)), ((), ()))
TN = (((0,), (0,)), ((), ()))
F32 = jnp.float32
BF16 = jnp.bfloat16
ANY = pl.BlockSpec(memory_space=pl.ANY)
SMEM = pl.BlockSpec(memory_space=pltpu.SMEM)


def mm(left, right, dims=(((1,), (0,)), ((), ()))):
    return lax.dot_general(left, right, dims, preferred_element_type=F32)


def row_variants(crop_len):
    return [crop_len]


def gelu_pair(values):
    cdf = 0.5 + 0.5 * lax.erf(values * (2.0**-0.5))
    density = jnp.exp(-0.5 * values * values) * (2.0 * math.pi) ** -0.5
    return values * cdf, cdf + values * density


def norm_forward(hidden):
    centred = hidden - jnp.mean(hidden, -1, keepdims=True)
    inverse = lax.rsqrt(jnp.mean(centred * centred, -1, keepdims=True) + EPS)
    return centred * inverse, inverse


def norm_backward(scaled, normed, inverse):
    return (
        scaled
        - jnp.mean(scaled, -1, keepdims=True)
        - normed * jnp.mean(scaled * normed, -1, keepdims=True)
    ) * inverse


def dispatch(length, crop_len, body):
    lower = 0
    for rows in row_variants(crop_len):
        pl.when((length > lower) & (length <= rows))(functools.partial(body, rows))
        lower = rows


def save_shapes(crops, crop_len, width, hidden):
    heads = width // HEAD
    return {
        "xs": ((crops, crop_len, width), BF16),
        "qkv": ((crops, crop_len, 3 * width), BF16),
        "att": ((crops, heads, crop_len, crop_len), BF16),
        "mix": ((crops, crop_len, width), BF16),
        "n1": ((crops, crop_len, width), F32),
        "low": ((crops, crop_len, width), BF16),
        "act": ((crops, crop_len, hidden), BF16),
        "gp": ((crops, crop_len, hidden), BF16),
        "n2": ((crops, crop_len, width), F32),
        "inv": ((crops, crop_len, 128), F32),
    }


def forward_kernel(member, names, first, n_alias, info, own, *refs):
    recv, refs = (None, refs) if first else (refs[0], refs[1:])
    wqkv, wout, wup, wdown, bup, biases, gains = refs[:7]
    refs = refs[7 + n_alias :]
    y_ref, pool_ref = refs[:2]
    saved = dict(zip(names, refs[2 : 2 + len(names)]))
    (bx, bwqkv, bwout, bwup, bwdown, bqkv, batt, bmix, blow, bact, bgp, bn1, bn2, binv, by, wsem, xsem, osem) = refs[2 + len(names) :]
    crop_len, width = by.shape
    hidden = bact.shape[1]
    heads = width // HEAD
    live, crop, length, section = info[0], info[1], info[2], info[3]

    def weight_copy(number):
        source = (wqkv, wout, wup, wdown)[number]
        return pltpu.make_async_copy(source.at[0, member], (bwqkv, bwout, bwup, bwdown)[number], wsem.at[number])

    def out_copy(number, name, buffer):
        return pltpu.make_async_copy(buffer, saved[name].at[crop], osem.at[number])

    def body(rows):
        keys = -(-rows // 128) * 128
        started = []

        def finish(number, name, buffer):
            if rows < crop_len:
                if name == "att":
                    pass
                else:
                    buffer[rows:, :] = jnp.zeros((crop_len - rows, buffer.shape[1]), buffer.dtype)
            if name in saved:
                copy = out_copy(number, name, buffer)
                copy.start()
                started.append(copy)

        weight_copy(0).wait()
        weight_copy(1).start()
        weight_copy(2).start()
        x = bx[:rows, :]
        finish(0, "xs", bx)
        bias_of = {0: biases[0, member, 0:1, :], 2: biases[0, member, 1:2, :]}
        for segment in range(3):
            for start in range(0, width, CHUNK):
                cols = slice(segment * width + start, segment * width + start + CHUNK)
                part = mm(x, bwqkv[:, cols])
                if segment in bias_of:
                    part = part + bias_of[segment][:, start : start + CHUNK]
                bqkv[:rows, cols] = part.astype(BF16)
        weight_copy(3).start()
        finish(1, "qkv", bqkv)
        lane = lax.broadcasted_iota(jnp.int32, (1, 128), 1)
        masks = (lane < HEAD, lane >= HEAD)
        key_valid = lax.broadcasted_iota(jnp.int32, (1, keys), 1) < length
        scale = HEAD**-0.5
        for pair in range(heads // 2):
            lo = pair * 128
            q2 = bqkv[:rows, lo : lo + 128]
            k2 = bqkv[:keys, width + lo : width + lo + 128]
            v2 = bqkv[:keys, 2 * width + lo : 2 * width + lo + 128]
            mixed = None
            for half in range(2):
                scores = mm(q2, jnp.where(masks[half], k2, 0), NT) * scale
                scores = jnp.where(key_valid, scores, NEG)
                weight = jnp.exp(scores - jnp.max(scores, -1, keepdims=True))
                weight = weight * (1.0 / jnp.sum(weight, -1, keepdims=True))
                weight = weight.astype(BF16)
                if "att" in saved:
                    batt[2 * pair + half, :rows, :keys] = weight
                part = mm(weight, jnp.where(masks[half], v2, 0))
                mixed = part if mixed is None else mixed + part
            bmix[:rows, lo : lo + 128] = mixed.astype(BF16)
        finish(2, "att", batt)
        finish(3, "mix", bmix)
        weight_copy(1).wait()
        attended = mm(bmix[:rows, :], bwout[...]) + biases[0, member, 2:3, :]
        n1, inv1 = norm_forward(x.astype(F32) + attended)
        bn1[:rows, :] = n1
        finish(4, "n1", bn1)
        after = n1 * gains[0, member, 0:1, :] + biases[0, member, 3:4, :]
        low = after.astype(BF16)
        blow[:rows, :] = low
        finish(5, "low", blow)
        weight_copy(2).wait()
        weight_copy(3).wait()
        branch = None
        for start in range(0, hidden, CHUNK):
            cols = slice(start, start + CHUNK)
            pre = mm(low, bwup[:, cols]) + bup[0, member : member + 1, cols]
            act, slope = gelu_pair(pre)
            act = act.astype(BF16)
            bact[:rows, cols] = act
            if "gp" in saved:
                bgp[:rows, cols] = slope.astype(BF16)
            part = mm(act, bwdown[cols, :])
            branch = part if branch is None else branch + part
        finish(6, "act", bact)
        finish(7, "gp", bgp)
        n2, inv2 = norm_forward(after + branch + biases[0, member, 4:5, :])
        bn2[:rows, :] = n2
        finish(8, "n2", bn2)
        if "inv" in saved:
            wide = lax.broadcasted_iota(jnp.int32, (1, 128), 1)
            binv[:rows, :] = jnp.where(wide == 0, inv1, inv2)
            finish(9, "inv", binv)
        out = n2 * gains[0, member, 1:2, :] + biases[0, member, 5:6, :]
        by[:rows, :] = out.astype(BF16)
        if rows < crop_len:
            by[rows:, :] = jnp.zeros((crop_len - rows, width), BF16)
        ycopy = pltpu.make_async_copy(by, y_ref, osem.at[10])
        ycopy.start()
        valid = lax.broadcasted_iota(jnp.int32, (rows, 1), 0) < length
        total = jnp.sum(jnp.where(valid, out, 0.0), 0, keepdims=True)
        pool_ref[...] = total / length.astype(F32)
        for copy in started:
            copy.wait()
        ycopy.wait()

    @pl.when(live == 1)
    def _():
        @pl.when(section == 0)
        def _():
            pltpu.make_async_copy(own.at[crop], bx, xsem).start()

        if recv is not None:

            @pl.when(section != 0)
            def _():
                pltpu.make_async_copy(recv, bx, xsem).start()

        weight_copy(0).start()
        pltpu.make_async_copy(own.at[crop], bx, xsem).wait()

        dispatch(length, crop_len, body)


def forward_call(member, info, own, recv, weights, state, save, order=()):
    wqkv, wout, wup, wdown, bup, biases, gains = weights
    crops, crop_len, width = own.shape
    hidden = wup.shape[-1]
    heads = width // HEAD
    shapes = save_shapes(crops, crop_len, width, hidden)
    names = tuple(shapes) if save else ()
    aliased = [state[name] for name in names] if state else []
    order = list(order)
    arrived = [] if recv is None else [recv]
    operands = [info, own, *arrived, *weights, *order, *aliased]
    whole = lambda a: pl.BlockSpec(a.shape, lambda n=len(a.shape): (0,) * n)
    in_specs = [SMEM, ANY] + [ANY] * len(arrived) + [ANY] * 4 + [whole(bup), whole(biases), whole(gains)]
    in_specs += [ANY] * (len(order) + len(aliased))
    out_shape = [
        jax.ShapeDtypeStruct((crop_len, width), BF16),
        jax.ShapeDtypeStruct((1, width), F32),
    ] + [jax.ShapeDtypeStruct(*shapes[name]) for name in names]
    first = 9 + len(arrived) + len(order)
    tokens = crop_len
    cost = pl.CostEstimate(
        flops=2 * tokens * (wqkv[0, 0].size + wout[0, 0].size + 2 * wup[0, 0].size),
        bytes_accessed=20_000_000,
        transcendentals=0,
    )
    outs = pl.pallas_call(
        functools.partial(forward_kernel, member, names, recv is None, len(order) + len(aliased)),
        out_shape=out_shape,
        in_specs=in_specs,
        out_specs=[ANY, pl.BlockSpec((1, width), lambda: (0, 0))] + [ANY] * len(names),
        input_output_aliases={first + i: 2 + i for i in range(len(aliased))},
        scratch_shapes=[
            pltpu.VMEM((crop_len, width), BF16),
            pltpu.VMEM((width, 3 * width), BF16),
            pltpu.VMEM((width, width), BF16),
            pltpu.VMEM((width, hidden), BF16),
            pltpu.VMEM((hidden, width), BF16),
            pltpu.VMEM((crop_len, 3 * width), BF16),
            pltpu.VMEM((heads, crop_len, crop_len) if save else (1, 16, 128), BF16),
            pltpu.VMEM((crop_len, width), BF16),
            pltpu.VMEM((crop_len, width), BF16),
            pltpu.VMEM((crop_len, hidden), BF16),
            pltpu.VMEM((crop_len, hidden), BF16),
            pltpu.VMEM((crop_len, width), F32),
            pltpu.VMEM((crop_len, width), F32),
            pltpu.VMEM((crop_len, 128), F32),
            pltpu.VMEM((crop_len, width), BF16),
            pltpu.SemaphoreType.DMA((4,)),
            pltpu.SemaphoreType.DMA,
            pltpu.SemaphoreType.DMA((11,)),
        ],
        compiler_params=pltpu.CompilerParams(vmem_limit_bytes=VMEM_LIMIT),
        cost_estimate=cost,
        name="forward_crop",
    )(*operands)
    return outs[0], outs[1], dict(zip(names, outs[2:]))


BACK_READ = ("qkv", "att", "n1", "gp", "n2", "inv")


def backward_kernel(first, n_alias, info, cot, *refs):
    recv, refs = (None, refs) if first else (refs[0], refs[1:])
    wqkv, wout, wup, wdown, biases, gains = refs[:6]
    refs = refs[6:]
    saved = dict(zip(BACK_READ, refs[: len(BACK_READ)]))
    refs = refs[len(BACK_READ) + n_alias :]
    dx_ref, vec_ref, ig_ref, bg_ref, ug_ref, ag_ref, qg_ref = refs[:7]
    (bg_in, bwqkv, bwout, bwup, bwdown, bqkv, batt, bn1, bgp, bn2, binv, bbg, bug, bag, bqg, bmg, bxg, bdx, wsem, ssem, gsem, osem) = refs[7:]
    crop_len, width = bbg.shape
    hidden = bug.shape[1]
    heads = width // HEAD
    live, crop, length, section = info[0], info[1], info[2], info[3]

    def weight_copy(number):
        source = (wup, wout, wqkv)[number]
        return pltpu.make_async_copy(source.at[0, 0], (bwup, bwout, bwqkv)[number], wsem.at[number])

    def down_copy(part):
        size = hidden // 4
        return pltpu.make_async_copy(
            wdown.at[0, 0, pl.ds(part * size, size)], bwdown.at[pl.ds(part * size, size)], wsem.at[3 + part]
        )

    def state_copy(name):
        buffers = {"qkv": bqkv, "att": batt, "n1": bn1, "gp": bgp, "n2": bn2, "inv": binv}
        return pltpu.make_async_copy(saved[name].at[crop], buffers[name], ssem.at[BACK_READ.index(name)])

    def body(rows):
        keys = -(-rows // 128) * 128
        started = []

        def finish(number, buffer, target):
            if rows < crop_len:
                buffer[rows:, :] = jnp.zeros((crop_len - rows, buffer.shape[1]), buffer.dtype)
            copy = pltpu.make_async_copy(buffer, target, osem.at[number])
            copy.start()
            started.append(copy)

        def column(values):
            return jnp.sum(values, 0, keepdims=True)

        valid = lax.broadcasted_iota(jnp.int32, (rows, 1), 0) < length
        g = jnp.where(valid, bg_in[:rows, :].astype(F32), 0.0)
        state_copy("n2").wait()
        state_copy("inv").wait()
        n2 = bn2[:rows, :]
        inv1 = binv[:rows, 0:1]
        inv2 = binv[:rows, 1:2]
        base = hidden // width
        vec_ref[base + 5 : base + 6, :] = column(g)
        vec_ref[base + 7 : base + 8, :] = column(g * n2)
        sum_two = norm_backward(g * gains[0, 0, 1:2, :], n2, inv2)
        bg = sum_two.astype(BF16)
        bbg[:rows, :] = bg
        finish(0, bbg, bg_ref.at[crop])
        vec_ref[base + 4 : base + 5, :] = column(bg.astype(F32))
        weight_copy(0).start()
        state_copy("gp").wait()
        for start in range(0, hidden, CHUNK):
            cols = slice(start, start + CHUNK)
            if start % (hidden // 4) == 0:
                down_copy(start // (hidden // 4)).wait()
            grad = mm(bg, bwdown[cols, :], NT) * bgp[:rows, cols].astype(F32)
            grad = grad.astype(BF16)
            bug[:rows, cols] = grad
            vec_ref[start // width : start // width + 1, start % width : start % width + CHUNK] = column(grad.astype(F32))
        weight_copy(0).wait()
        weight_copy(1).start()
        state_copy("n1").start()
        state_copy("qkv").start()
        state_copy("att").start()
        weight_copy(2).start()
        side = sum_two + mm(bug[:rows, :], bwup[...], NT)
        finish(1, bug, ug_ref.at[crop])
        state_copy("n1").wait()
        n1 = bn1[:rows, :]
        vec_ref[base + 3 : base + 4, :] = column(side)
        vec_ref[base + 6 : base + 7, :] = column(side * n1)
        sum_one = norm_backward(side * gains[0, 0, 0:1, :], n1, inv1)
        ag = sum_one.astype(BF16)
        bag[:rows, :] = ag
        finish(2, bag, ag_ref.at[crop])
        vec_ref[base + 2 : base + 3, :] = column(ag.astype(F32))
        weight_copy(1).wait()
        bmg[:rows, :] = mm(ag, bwout[...], NT).astype(BF16)
        state_copy("qkv").wait()
        state_copy("att").wait()
        lane = lax.broadcasted_iota(jnp.int32, (1, 128), 1)
        masks = (lane < HEAD, lane >= HEAD)
        scale = HEAD**-0.5
        zero = jnp.zeros((), BF16)
        for pair in range(heads // 2):
            lo = pair * 128
            q2 = bqkv[:rows, lo : lo + 128]
            k2 = bqkv[:keys, width + lo : width + lo + 128]
            v2 = bqkv[:keys, 2 * width + lo : 2 * width + lo + 128]
            m2 = bmg[:rows, lo : lo + 128]
            dq = dk = dv = None
            for half in range(2):
                weight = batt[2 * pair + half, :rows, :keys]
                wide = weight.astype(F32)
                grad = mm(m2, jnp.where(masks[half], v2, zero), NT)
                mean = jnp.sum(wide * grad, -1, keepdims=True)
                score = (wide * (grad - mean)).astype(BF16)
                parts = (
                    mm(score, jnp.where(masks[half], k2, zero)),
                    mm(score, jnp.where(masks[half], q2, zero), TN),
                    mm(weight, jnp.where(masks[half], m2, zero), TN),
                )
                dq, dk, dv = parts if dq is None else (dq + parts[0], dk + parts[1], dv + parts[2])
            dq = (dq * scale).astype(BF16)
            dk = (dk[:rows] * scale).astype(BF16)
            dv = dv[:rows].astype(BF16)
            bqg[:rows, lo : lo + 128] = dq
            bqg[:rows, width + lo : width + lo + 128] = dk
            bqg[:rows, 2 * width + lo : 2 * width + lo + 128] = dv
            vec_ref[base : base + 1, lo : lo + 128] = column(dq.astype(F32))
            vec_ref[base + 1 : base + 2, lo : lo + 128] = column(dv.astype(F32))
        finish(3, bqg, qg_ref.at[crop])
        weight_copy(2).wait()
        xg = sum_one + mm(bqg[:rows, :], bwqkv[...], NT)
        dx = xg.astype(BF16)
        bdx[:rows, :] = dx
        finish(4, bdx, dx_ref)
        bxg[:rows, :] = jnp.where(section == 0, xg, dx.astype(F32))
        finish(5, bxg, ig_ref.at[crop])
        for copy in started:
            copy.wait()

    @pl.when(live != 1)
    def _():
        vec_ref[...] = jnp.zeros(vec_ref.shape, F32)

    @pl.when(live == 1)
    def _():
        if recv is not None:

            @pl.when(section == 0)
            def _():
                pltpu.make_async_copy(recv, bg_in, gsem).start()

        @pl.when(section != 0)
        def _():
            pltpu.make_async_copy(cot.at[crop], bg_in, gsem).start()

        state_copy("n2").start()
        state_copy("inv").start()
        for part in range(4):
            down_copy(part).start()
        state_copy("gp").start()
        pltpu.make_async_copy(cot.at[crop], bg_in, gsem).wait()
        dispatch(length, crop_len, body)


def backward_call(info, cot, recv, weights, state, grads):
    wqkv, wout, wup, wdown, bup, biases, gains = weights
    crops, crop_len, width = cot.shape
    hidden = wup.shape[-1]
    heads = width // HEAD
    shapes = {
        "ig": ((crops, crop_len, width), F32),
        "bg": ((crops, crop_len, width), BF16),
        "ug": ((crops, crop_len, hidden), BF16),
        "ag": ((crops, crop_len, width), BF16),
        "qg": ((crops, crop_len, 3 * width), BF16),
    }
    names = tuple(shapes)
    aliased = [grads[name] for name in names] if grads else []
    arrived = [] if recv is None else [recv]
    operands = [info, cot, *arrived, wqkv, wout, wup, wdown, biases, gains]
    operands += [state[name] for name in BACK_READ] + aliased
    whole = lambda a: pl.BlockSpec(a.shape, lambda n=len(a.shape): (0,) * n)
    in_specs = [SMEM, ANY] + [ANY] * (len(arrived) + 4) + [whole(biases), whole(gains)]
    in_specs += [ANY] * (len(BACK_READ) + len(aliased))
    first = 8 + len(arrived) + len(BACK_READ)
    rows = hidden // width + 8
    cost = pl.CostEstimate(
        flops=2 * crop_len * (wqkv[0, 0].size + wout[0, 0].size + 2 * wup[0, 0].size),
        bytes_accessed=20_000_000,
        transcendentals=0,
    )
    outs = pl.pallas_call(
        functools.partial(backward_kernel, recv is None, len(aliased)),
        out_shape=[
            jax.ShapeDtypeStruct((crop_len, width), BF16),
            jax.ShapeDtypeStruct((rows, width), F32),
        ]
        + [jax.ShapeDtypeStruct(*shapes[name]) for name in names],
        in_specs=in_specs,
        out_specs=[ANY, pl.BlockSpec((rows, width), lambda: (0, 0))] + [ANY] * len(names),
        input_output_aliases={first + i: 2 + i for i in range(len(aliased))},
        scratch_shapes=[
            pltpu.VMEM((crop_len, width), BF16),
            pltpu.VMEM((width, 3 * width), BF16),
            pltpu.VMEM((width, width), BF16),
            pltpu.VMEM((width, hidden), BF16),
            pltpu.VMEM((hidden, width), BF16),
            pltpu.VMEM((crop_len, 3 * width), BF16),
            pltpu.VMEM((heads, crop_len, crop_len), BF16),
            pltpu.VMEM((crop_len, width), F32),
            pltpu.VMEM((crop_len, hidden), BF16),
            pltpu.VMEM((crop_len, width), F32),
            pltpu.VMEM((crop_len, 128), F32),
            pltpu.VMEM((crop_len, width), BF16),
            pltpu.VMEM((crop_len, hidden), BF16),
            pltpu.VMEM((crop_len, width), BF16),
            pltpu.VMEM((crop_len, 3 * width), BF16),
            pltpu.VMEM((crop_len, width), BF16),
            pltpu.VMEM((crop_len, width), F32),
            pltpu.VMEM((crop_len, width), BF16),
            pltpu.SemaphoreType.DMA((7,)),
            pltpu.SemaphoreType.DMA((len(BACK_READ),)),
            pltpu.SemaphoreType.DMA,
            pltpu.SemaphoreType.DMA((6,)),
        ],
        compiler_params=pltpu.CompilerParams(vmem_limit_bytes=VMEM_LIMIT),
        cost_estimate=cost,
        name="backward_crop",
    )(*operands)
    return outs[0], outs[1], dict(zip(names, outs[2:]))


def weight_kernel(info, left, right, out):
    out[...] = mm(left[...], right[...], TN).astype(BF16)


def weight_call(info, left, right, mine):
    left = left.reshape(-1, left.shape[-1])
    right = right.reshape(-1, right.shape[-1])
    tokens, rows, columns = left.shape[0], left.shape[1] // 2, right.shape[1]
    if rows >= columns:
        tile, count = rows // (rows // 384), rows // 384
        spec_left = pl.BlockSpec((tokens, tile), lambda i, info: (0, (info[0] if mine else 1 - info[0]) * count + i))
        spec_right = pl.BlockSpec((tokens, columns), lambda i, info: (0, 0))
        spec_out = pl.BlockSpec((tile, columns), lambda i, info: (i, 0))
    else:
        tile = 768
        count = columns // tile
        spec_left = pl.BlockSpec((tokens, rows), lambda i, info: (0, info[0] if mine else 1 - info[0]))
        spec_right = pl.BlockSpec((tokens, tile), lambda i, info: (0, i))
        spec_out = pl.BlockSpec((rows, tile), lambda i, info: (0, i))
    return pl.pallas_call(
        weight_kernel,
        out_shape=jax.ShapeDtypeStruct((rows, columns), BF16),
        grid_spec=pltpu.PrefetchScalarGridSpec(
            num_scalar_prefetch=1, grid=(count,), in_specs=[spec_left, spec_right], out_specs=spec_out
        ),
        compiler_params=pltpu.CompilerParams(vmem_limit_bytes=VMEM_LIMIT, dimension_semantics=("arbitrary",)),
        cost_estimate=pl.CostEstimate(flops=2 * tokens * rows * columns, bytes_accessed=2 * tokens * (rows + columns) + 2 * rows * columns, transcendentals=0),
        name="weight_half",
    )(info, left, right)


def last_weight_kernel(info, left, right, left_out, right_out, out):
    step = pl.program_id(0)

    @pl.when(step < pl.num_programs(0) - 1)
    def _():
        out[...] = mm(left[...], right[...], TN).astype(BF16)

    @pl.when(step == pl.num_programs(0) - 1)
    def _():
        out[...] = mm(left_out[...], right_out[...], TN).astype(BF16)


def last_weight_call(info, left, right, left_out, right_out, mine):
    left, right, left_out, right_out = (a.reshape(-1, a.shape[-1]) for a in (left, right, left_out, right_out))
    tokens, width = left.shape
    rows, parts = width // 2, right.shape[1] // width
    half = lambda info: info[0] if mine else 1 - info[0]
    return pl.pallas_call(
        last_weight_kernel,
        out_shape=jax.ShapeDtypeStruct((rows, (parts + 1) * width), BF16),
        grid_spec=pltpu.PrefetchScalarGridSpec(
            num_scalar_prefetch=1,
            grid=(parts + 1,),
            in_specs=[
                pl.BlockSpec((tokens, rows), lambda i, info: (0, half(info))),
                pl.BlockSpec((tokens, width), lambda i, info: (0, jnp.minimum(i, parts - 1))),
                pl.BlockSpec((tokens, rows), lambda i, info: (0, half(info))),
                pl.BlockSpec((tokens, width), lambda i, info: (0, 0)),
            ],
            out_specs=pl.BlockSpec((rows, width), lambda i, info: (0, i)),
        ),
        compiler_params=pltpu.CompilerParams(vmem_limit_bytes=VMEM_LIMIT),
        cost_estimate=pl.CostEstimate(flops=2 * tokens * rows * width * (parts + 1), bytes_accessed=12_000_000, transcendentals=0),
        name="weight_half_two",
    )(info, left, right, left_out, right_out)


def ring_plan(dp, rep):
    chips = [(0, z) for z in range(rep)] + [(1, z) for z in reversed(range(rep))]
    count = len(chips)
    position = [0] * (dp * rep)
    pairs = []
    for core in range(2):
        order = chips if core == 0 else chips[::-1]
        index = [(2 * y + core) * rep + z for y, z in order]
        for place, device in enumerate(index):
            position[device] = place
            pairs.append((device, index[(place + 1) % count]))
    return count, position, pairs


def sum_over_ring(halves, place, count, pairs):
    own, other = (a.reshape(count, -1, a.shape[-1]) for a in halves)

    def block(number):
        number = jnp.mod(number, count)
        take = lambda a: lax.dynamic_index_in_dim(a, number, 0, keepdims=False).astype(F32)
        return take(own) + take(other)

    moving = block(place).astype(BF16)
    for step in range(1, count):
        moving = lax.ppermute(moving, AXES, pairs)
        moving = (moving.astype(F32) + block(place - step)).astype(BF16)
        yield None
    result = jnp.zeros(own.shape, BF16)
    for step in range(count):
        if step > 0:
            moving = lax.ppermute(moving, AXES, pairs)
        result = lax.dynamic_update_index_in_dim(result, moving, jnp.mod(place + 1 - step, count), 0)
        yield None
    yield result.reshape(halves[0].shape)


AXES = ("dp", "rep")


def on_device(
    query_input,
    key_input,
    query_lengths,
    key_lengths,
    cotangent,
    w_qkv,
    w_out,
    w_up,
    w_down,
    b_up,
    biases,
    gains,
):
    section = lax.axis_index("section")
    dp, rep = lax.axis_size("dp"), lax.axis_size("rep")
    crops, crop_len, width = query_input.shape
    hidden = w_up.shape[-1]
    weights = (w_qkv, w_out, w_up, w_down, b_up, biases, gains)

    def info_of(crop, lengths):
        live = (crop >= 0) & (crop < crops)
        slot = jnp.clip(crop, 0, crops - 1)
        length = lax.dynamic_index_in_dim(lengths, slot, 0, keepdims=False)
        return jnp.stack([live.astype(jnp.int32), slot, length, section]).astype(jnp.int32)

    def up(value):
        return lax.ppermute(value, "section", [(0, 1)])

    def down(value):
        return lax.ppermute(value, "section", [(1, 0)])

    def picked(rows, first):
        return lax.dynamic_slice_in_dim(jnp.concatenate(rows), first, crops, 0)

    state, grads = {}, {}
    pools, vectors = [], []
    arrived = returned = None
    for slot in range(crops + 1):
        sent, pooled, state = forward_call(
            0, info_of(slot - section, query_lengths), query_input, arrived, weights, state, True, vectors[-1:]
        )
        pools.append(pooled)
        if slot < crops:
            arrived = up(sent)
        if slot >= 1:
            back, vector, grads = backward_call(
                info_of(slot - 2 + section, query_lengths), cotangent, returned, weights, state, grads
            )
            vectors.append(vector)
            returned = down(back)
    back, vector, grads = backward_call(
        info_of(crops - 1 + section, query_lengths), cotangent, returned, weights, state, grads
    )
    vectors.append(vector)

    core = jnp.mod(lax.axis_index("dp"), 2)
    core_info = core.astype(jnp.int32)[None]
    swap = [(d * rep + z, (d ^ 1) * rep + z) for d in range(dp) for z in range(rep)]
    products = (
        lambda mine: weight_call(core_info, state["act"], grads["bg"], mine),
        lambda mine: weight_call(core_info, state["low"], grads["ug"], mine),
        lambda mine: last_weight_call(core_info, state["xs"], grads["qg"], state["mix"], grads["ag"], mine),
    )
    halves = []
    for product in products:
        theirs = product(False)
        halves.append((product(True), lax.ppermute(theirs, AXES, swap), theirs))

    pooled_query = lax.all_gather(picked(pools, section), AXES, axis=0, tiled=True)
    small = lax.psum(sum(vectors), AXES)

    key_pools = []
    arrived = None
    for slot in range(crops + 1):
        sent, pooled, _ = forward_call(
            1, info_of(slot - section, key_lengths), key_input, arrived, weights, {}, False, [halves[-1][0]]
        )
        key_pools.append(pooled)
        if slot < crops:
            arrived = up(sent)
    pooled_key = lax.all_gather(picked(key_pools, section), AXES, axis=0, tiled=True)

    def joined(half, other):
        both = jnp.where(core == 0, jnp.stack([half, other]), jnp.stack([other, half]))
        return both.reshape(-1, half.shape[-1])

    if dp == 4:
        count, position, pairs = ring_plan(dp, rep)
        place = jnp.asarray(position, jnp.int32)[lax.axis_index(AXES)]
        rings = [sum_over_ring(half[:2], place, count, pairs) for half in halves]
        for step in range(2 * count):
            results = [next(ring) for ring in rings]
        totals = [joined(half, lax.ppermute(half, AXES, swap)) for half in results]
    else:
        totals = [lax.psum(joined(mine, theirs), AXES) for mine, _, theirs in halves]
    totals = [total.astype(F32) for total in totals]
    ratio = hidden // width
    return (
        pooled_query[None],
        pooled_key[None],
        grads["ig"][None],
        totals[2][None, :, : 3 * width],
        totals[2][None, :, 3 * width :],
        totals[1][None],
        totals[0][None],
        small[:ratio].reshape(1, hidden),
        small[None, ratio : ratio + 6],
        small[None, ratio + 6 : ratio + 8],
    )


def solution(mesh):
    placed = (
        P(("dp", "rep"), None, None),
        P(("dp", "rep"), None, None),
        P(("dp", "rep")),
        P(("dp", "rep")),
        P(("dp", "rep"), None, None),
        P("section", None, None, None),
        P("section", None, None, None),
        P("section", None, None, None),
        P("section", None, None, None),
        P("section", None, None),
        P("section", None, None, None),
        P("section", None, None, None),
    )
    return jax.shard_map(
        on_device,
        mesh=mesh,
        in_specs=placed,
        out_specs=(
            P("section", None, None),
            P("section", None, None),
            P("section", ("dp", "rep"), None, None),
            P("section", None, None),
            P("section", None, None),
            P("section", None, None),
            P("section", None, None),
            P("section", None),
            P("section", None, None),
            P("section", None, None),
        ),
        check_vma=False,
    )
```

```python
import functools
import math

import jax
import jax.numpy as jnp
from jax import lax
from jax.experimental import pallas as pl
from jax.experimental.pallas import tpu as pltpu
from jax.sharding import PartitionSpec as P

HEAD = 64
EPS = 1e-06
NEG = -1000000000.0
CHUNK = 256
VMEM_LIMIT = 60 * 1024 * 1024
NT = (((1,), (1,)), ((), ()))
TN = (((0,), (0,)), ((), ()))
F32 = jnp.float32
BF16 = jnp.bfloat16
ANY = pl.BlockSpec(memory_space=pl.ANY)
SMEM = pl.BlockSpec(memory_space=pltpu.SMEM)


def mm(left, right, dims=(((1,), (0,)), ((), ()))):
    return lax.dot_general(left, right, dims, preferred_element_type=F32)


def row_variants(crop_len):
    return [crop_len]


def gelu_pair(values):
    cdf = 0.5 + 0.5 * lax.erf(values * (2.0**-0.5))
    density = jnp.exp(-0.5 * values * values) * (2.0 * math.pi) ** -0.5
    return values * cdf, cdf + values * density


def norm_forward(hidden):
    centred = hidden - jnp.mean(hidden, -1, keepdims=True)
    inverse = lax.rsqrt(jnp.mean(centred * centred, -1, keepdims=True) + EPS)
    return centred * inverse, inverse


def norm_backward(scaled, normed, inverse):
    return (
        scaled
        - jnp.mean(scaled, -1, keepdims=True)
        - normed * jnp.mean(scaled * normed, -1, keepdims=True)
    ) * inverse


def dispatch(length, crop_len, body):
    lower = 0
    for rows in row_variants(crop_len):
        pl.when((length > lower) & (length <= rows))(functools.partial(body, rows))
        lower = rows


def save_shapes(crops, crop_len, width, hidden):
    heads = width // HEAD
    return {
        "xs": ((crops, crop_len, width), BF16),
        "qkv": ((crops, crop_len, 3 * width), BF16),
        "att": ((crops, heads, crop_len, crop_len), BF16),
        "mix": ((crops, crop_len, width), BF16),
        "n1": ((crops, crop_len, width), F32),
        "low": ((crops, crop_len, width), BF16),
        "act": ((crops, crop_len, hidden), BF16),
        "gp": ((crops, crop_len, hidden), BF16),
        "n2": ((crops, crop_len, width), F32),
        "inv": ((crops, crop_len, 128), F32),
    }


def forward_kernel(member, names, call, first, n_alias, info, own, *refs):
    recv, refs = (None, refs) if first else (refs[0], refs[1:])
    wqkv, wout, wup, wdown, bup, biases, gains = refs[:7]
    refs = refs[7 + n_alias :]
    y_ref, pool_ref = refs[:2]
    saved = dict(zip(names, refs[2 : 2 + len(names)]))
    (bx, bwqkv, bwout, bwup, bwdown, bqkv, batt, bmix, blow, bact, bgp, bn1, bn2, binv, by, wsem, xsem, osem) = refs[2 + len(names) :]
    crop_len, width = by.shape
    hidden = bact.shape[1]
    heads = width // HEAD
    live, crop, length, section = (info[call, number] for number in range(4))

    def weight_copy(number):
        source = (wqkv, wout, wup, wdown)[number]
        return pltpu.make_async_copy(source.at[0, member], (bwqkv, bwout, bwup, bwdown)[number], wsem.at[number])

    def out_copy(number, name, buffer):
        return pltpu.make_async_copy(buffer, saved[name].at[crop], osem.at[number])

    def body(rows):
        keys = -(-rows // 128) * 128
        started = []

        def finish(number, name, buffer):
            if rows < crop_len:
                if name == "att":
                    pass
                else:
                    buffer[rows:, :] = jnp.zeros((crop_len - rows, buffer.shape[1]), buffer.dtype)
            if name in saved:
                copy = out_copy(number, name, buffer)
                copy.start()
                started.append(copy)

        weight_copy(0).wait()
        weight_copy(1).start()
        weight_copy(2).start()
        x = bx[:rows, :]
        finish(0, "xs", bx)
        bias_of = {0: biases[0, member, 0:1, :], 2: biases[0, member, 1:2, :]}
        for segment in range(3):
            for start in range(0, width, CHUNK):
                cols = slice(segment * width + start, segment * width + start + CHUNK)
                part = mm(x, bwqkv[:, cols])
                if segment in bias_of:
                    part = part + bias_of[segment][:, start : start + CHUNK]
                bqkv[:rows, cols] = part.astype(BF16)
        weight_copy(3).start()
        finish(1, "qkv", bqkv)
        lane = lax.broadcasted_iota(jnp.int32, (1, 128), 1)
        masks = (lane < HEAD, lane >= HEAD)
        key_valid = lax.broadcasted_iota(jnp.int32, (1, keys), 1) < length
        scale = HEAD**-0.5
        for pair in range(heads // 2):
            lo = pair * 128
            q2 = bqkv[:rows, lo : lo + 128]
            k2 = bqkv[:keys, width + lo : width + lo + 128]
            v2 = bqkv[:keys, 2 * width + lo : 2 * width + lo + 128]
            mixed = None
            for half in range(2):
                scores = mm(q2, jnp.where(masks[half], k2, 0), NT) * scale
                scores = jnp.where(key_valid, scores, NEG)
                weight = jnp.exp(scores - jnp.max(scores, -1, keepdims=True))
                weight = weight * (1.0 / jnp.sum(weight, -1, keepdims=True))
                weight = weight.astype(BF16)
                if "att" in saved:
                    batt[2 * pair + half, :rows, :keys] = weight
                part = mm(weight, jnp.where(masks[half], v2, 0))
                mixed = part if mixed is None else mixed + part
            bmix[:rows, lo : lo + 128] = mixed.astype(BF16)
        finish(2, "att", batt)
        finish(3, "mix", bmix)
        weight_copy(1).wait()
        attended = mm(bmix[:rows, :], bwout[...]) + biases[0, member, 2:3, :]
        n1, inv1 = norm_forward(x.astype(F32) + attended)
        bn1[:rows, :] = n1
        finish(4, "n1", bn1)
        after = n1 * gains[0, member, 0:1, :] + biases[0, member, 3:4, :]
        low = after.astype(BF16)
        blow[:rows, :] = low
        finish(5, "low", blow)
        weight_copy(2).wait()
        weight_copy(3).wait()
        branch = None
        for start in range(0, hidden, CHUNK):
            cols = slice(start, start + CHUNK)
            pre = mm(low, bwup[:, cols]) + bup[0, member : member + 1, cols]
            act, slope = gelu_pair(pre)
            act = act.astype(BF16)
            bact[:rows, cols] = act
            if "gp" in saved:
                bgp[:rows, cols] = slope.astype(BF16)
            part = mm(act, bwdown[cols, :])
            branch = part if branch is None else branch + part
        finish(6, "act", bact)
        finish(7, "gp", bgp)
        n2, inv2 = norm_forward(after + branch + biases[0, member, 4:5, :])
        bn2[:rows, :] = n2
        finish(8, "n2", bn2)
        if "inv" in saved:
            wide = lax.broadcasted_iota(jnp.int32, (1, 128), 1)
            binv[:rows, :] = jnp.where(wide == 0, inv1, inv2)
            finish(9, "inv", binv)
        out = n2 * gains[0, member, 1:2, :] + biases[0, member, 5:6, :]
        by[:rows, :] = out.astype(BF16)
        if rows < crop_len:
            by[rows:, :] = jnp.zeros((crop_len - rows, width), BF16)
        ycopy = pltpu.make_async_copy(by, y_ref, osem.at[10])
        ycopy.start()
        valid = lax.broadcasted_iota(jnp.int32, (rows, 1), 0) < length
        total = jnp.sum(jnp.where(valid, out, 0.0), 0, keepdims=True)
        pool_ref[...] = total / length.astype(F32)
        for copy in started:
            copy.wait()
        ycopy.wait()

    @pl.when(live == 1)
    def _():
        @pl.when(section == 0)
        def _():
            pltpu.make_async_copy(own.at[crop], bx, xsem).start()

        if recv is not None:

            @pl.when(section != 0)
            def _():
                pltpu.make_async_copy(recv, bx, xsem).start()

        weight_copy(0).start()
        pltpu.make_async_copy(own.at[crop], bx, xsem).wait()

        dispatch(length, crop_len, body)


def forward_call(member, info, call, own, recv, weights, state, save, order=()):
    wqkv, wout, wup, wdown, bup, biases, gains = weights
    crops, crop_len, width = own.shape
    hidden = wup.shape[-1]
    heads = width // HEAD
    shapes = save_shapes(crops, crop_len, width, hidden)
    names = tuple(shapes) if save else ()
    aliased = [state[name] for name in names] if state else []
    order = list(order)
    arrived = [] if recv is None else [recv]
    operands = [info, own, *arrived, *weights, *order, *aliased]
    whole = lambda a: pl.BlockSpec(a.shape, lambda n=len(a.shape): (0,) * n)
    in_specs = [SMEM, ANY] + [ANY] * len(arrived) + [ANY] * 4 + [whole(bup), whole(biases), whole(gains)]
    in_specs += [ANY] * (len(order) + len(aliased))
    out_shape = [
        jax.ShapeDtypeStruct((crop_len, width), BF16),
        jax.ShapeDtypeStruct((1, width), F32),
    ] + [jax.ShapeDtypeStruct(*shapes[name]) for name in names]
    first = 9 + len(arrived) + len(order)
    tokens = crop_len
    cost = pl.CostEstimate(
        flops=2 * tokens * (wqkv[0, 0].size + wout[0, 0].size + 2 * wup[0, 0].size),
        bytes_accessed=20_000_000,
        transcendentals=0,
    )
    outs = pl.pallas_call(
        functools.partial(forward_kernel, member, names, call, recv is None, len(order) + len(aliased)),
        out_shape=out_shape,
        in_specs=in_specs,
        out_specs=[ANY, pl.BlockSpec((1, width), lambda: (0, 0))] + [ANY] * len(names),
        input_output_aliases={first + i: 2 + i for i in range(len(aliased))},
        scratch_shapes=[
            pltpu.VMEM((crop_len, width), BF16),
            pltpu.VMEM((width, 3 * width), BF16),
            pltpu.VMEM((width, width), BF16),
            pltpu.VMEM((width, hidden), BF16),
            pltpu.VMEM((hidden, width), BF16),
            pltpu.VMEM((crop_len, 3 * width), BF16),
            pltpu.VMEM((heads, crop_len, crop_len) if save else (1, 16, 128), BF16),
            pltpu.VMEM((crop_len, width), BF16),
            pltpu.VMEM((crop_len, width), BF16),
            pltpu.VMEM((crop_len, hidden), BF16),
            pltpu.VMEM((crop_len, hidden), BF16),
            pltpu.VMEM((crop_len, width), F32),
            pltpu.VMEM((crop_len, width), F32),
            pltpu.VMEM((crop_len, 128), F32),
            pltpu.VMEM((crop_len, width), BF16),
            pltpu.SemaphoreType.DMA((4,)),
            pltpu.SemaphoreType.DMA,
            pltpu.SemaphoreType.DMA((11,)),
        ],
        compiler_params=pltpu.CompilerParams(vmem_limit_bytes=VMEM_LIMIT),
        cost_estimate=cost,
        name="forward_crop",
    )(*operands)
    return outs[0], outs[1], dict(zip(names, outs[2:]))


BACK_READ = ("qkv", "att", "n1", "gp", "n2", "inv")


def backward_kernel(call, first, n_alias, info, cot, *refs):
    recv, refs = (None, refs) if first else (refs[0], refs[1:])
    wqkv, wout, wup, wdown, biases, gains = refs[:6]
    refs = refs[6:]
    saved = dict(zip(BACK_READ, refs[: len(BACK_READ)]))
    refs = refs[len(BACK_READ) + n_alias :]
    dx_ref, vec_ref, ig_ref, bg_ref, ug_ref, ag_ref, qg_ref = refs[:7]
    (bg_in, bwqkv, bwout, bwup, bwdown, bqkv, batt, bn1, bgp, bn2, binv, bbg, bug, bag, bqg, bmg, bxg, bdx, wsem, ssem, gsem, osem) = refs[7:]
    crop_len, width = bbg.shape
    hidden = bug.shape[1]
    heads = width // HEAD
    live, crop, length, section = (info[call, number] for number in range(4))

    def weight_copy(number):
        source = (wup, wout, wqkv)[number]
        return pltpu.make_async_copy(source.at[0, 0], (bwup, bwout, bwqkv)[number], wsem.at[number])

    def down_copy(part):
        size = hidden // 4
        return pltpu.make_async_copy(
            wdown.at[0, 0, pl.ds(part * size, size)], bwdown.at[pl.ds(part * size, size)], wsem.at[3 + part]
        )

    def state_copy(name):
        buffers = {"qkv": bqkv, "att": batt, "n1": bn1, "gp": bgp, "n2": bn2, "inv": binv}
        return pltpu.make_async_copy(saved[name].at[crop], buffers[name], ssem.at[BACK_READ.index(name)])

    def body(rows):
        keys = -(-rows // 128) * 128
        started = []

        def finish(number, buffer, target):
            if rows < crop_len:
                buffer[rows:, :] = jnp.zeros((crop_len - rows, buffer.shape[1]), buffer.dtype)
            copy = pltpu.make_async_copy(buffer, target, osem.at[number])
            copy.start()
            started.append(copy)

        def column(values):
            return jnp.sum(values, 0, keepdims=True)

        valid = lax.broadcasted_iota(jnp.int32, (rows, 1), 0) < length
        g = jnp.where(valid, bg_in[:rows, :].astype(F32), 0.0)
        state_copy("n2").wait()
        state_copy("inv").wait()
        n2 = bn2[:rows, :]
        inv1 = binv[:rows, 0:1]
        inv2 = binv[:rows, 1:2]
        base = hidden // width
        vec_ref[base + 5 : base + 6, :] = column(g)
        vec_ref[base + 7 : base + 8, :] = column(g * n2)
        sum_two = norm_backward(g * gains[0, 0, 1:2, :], n2, inv2)
        bg = sum_two.astype(BF16)
        bbg[:rows, :] = bg
        finish(0, bbg, bg_ref.at[crop])
        vec_ref[base + 4 : base + 5, :] = column(bg.astype(F32))
        weight_copy(0).start()
        state_copy("gp").wait()
        for start in range(0, hidden, CHUNK):
            cols = slice(start, start + CHUNK)
            if start % (hidden // 4) == 0:
                down_copy(start // (hidden // 4)).wait()
            grad = mm(bg, bwdown[cols, :], NT) * bgp[:rows, cols].astype(F32)
            grad = grad.astype(BF16)
            bug[:rows, cols] = grad
            vec_ref[start // width : start // width + 1, start % width : start % width + CHUNK] = column(grad.astype(F32))
        weight_copy(0).wait()
        weight_copy(1).start()
        state_copy("n1").start()
        state_copy("qkv").start()
        state_copy("att").start()
        weight_copy(2).start()
        side = sum_two + mm(bug[:rows, :], bwup[...], NT)
        finish(1, bug, ug_ref.at[crop])
        state_copy("n1").wait()
        n1 = bn1[:rows, :]
        vec_ref[base + 3 : base + 4, :] = column(side)
        vec_ref[base + 6 : base + 7, :] = column(side * n1)
        sum_one = norm_backward(side * gains[0, 0, 0:1, :], n1, inv1)
        ag = sum_one.astype(BF16)
        bag[:rows, :] = ag
        finish(2, bag, ag_ref.at[crop])
        vec_ref[base + 2 : base + 3, :] = column(ag.astype(F32))
        weight_copy(1).wait()
        bmg[:rows, :] = mm(ag, bwout[...], NT).astype(BF16)
        state_copy("qkv").wait()
        state_copy("att").wait()
        lane = lax.broadcasted_iota(jnp.int32, (1, 128), 1)
        masks = (lane < HEAD, lane >= HEAD)
        scale = HEAD**-0.5
        zero = jnp.zeros((), BF16)
        for pair in range(heads // 2):
            lo = pair * 128
            q2 = bqkv[:rows, lo : lo + 128]
            k2 = bqkv[:keys, width + lo : width + lo + 128]
            v2 = bqkv[:keys, 2 * width + lo : 2 * width + lo + 128]
            m2 = bmg[:rows, lo : lo + 128]
            dq = dk = dv = None
            for half in range(2):
                weight = batt[2 * pair + half, :rows, :keys]
                wide = weight.astype(F32)
                grad = mm(m2, jnp.where(masks[half], v2, zero), NT)
                mean = jnp.sum(wide * grad, -1, keepdims=True)
                score = (wide * (grad - mean)).astype(BF16)
                parts = (
                    mm(score, jnp.where(masks[half], k2, zero)),
                    mm(score, jnp.where(masks[half], q2, zero), TN),
                    mm(weight, jnp.where(masks[half], m2, zero), TN),
                )
                dq, dk, dv = parts if dq is None else (dq + parts[0], dk + parts[1], dv + parts[2])
            dq = (dq * scale).astype(BF16)
            dk = (dk[:rows] * scale).astype(BF16)
            dv = dv[:rows].astype(BF16)
            bqg[:rows, lo : lo + 128] = dq
            bqg[:rows, width + lo : width + lo + 128] = dk
            bqg[:rows, 2 * width + lo : 2 * width + lo + 128] = dv
            vec_ref[base : base + 1, lo : lo + 128] = column(dq.astype(F32))
            vec_ref[base + 1 : base + 2, lo : lo + 128] = column(dv.astype(F32))
        finish(3, bqg, qg_ref.at[crop])
        weight_copy(2).wait()
        xg = sum_one + mm(bqg[:rows, :], bwqkv[...], NT)
        dx = xg.astype(BF16)
        bdx[:rows, :] = dx
        finish(4, bdx, dx_ref)
        bxg[:rows, :] = jnp.where(section == 0, xg, dx.astype(F32))
        finish(5, bxg, ig_ref.at[crop])
        for copy in started:
            copy.wait()

    @pl.when(live != 1)
    def _():
        vec_ref[...] = jnp.zeros(vec_ref.shape, F32)

    @pl.when(live == 1)
    def _():
        if recv is not None:

            @pl.when(section == 0)
            def _():
                pltpu.make_async_copy(recv, bg_in, gsem).start()

        @pl.when(section != 0)
        def _():
            pltpu.make_async_copy(cot.at[crop], bg_in, gsem).start()

        state_copy("n2").start()
        state_copy("inv").start()
        for part in range(4):
            down_copy(part).start()
        state_copy("gp").start()
        pltpu.make_async_copy(cot.at[crop], bg_in, gsem).wait()
        dispatch(length, crop_len, body)


def backward_call(info, call, cot, recv, weights, state, grads):
    wqkv, wout, wup, wdown, bup, biases, gains = weights
    crops, crop_len, width = cot.shape
    hidden = wup.shape[-1]
    heads = width // HEAD
    shapes = {
        "ig": ((crops, crop_len, width), F32),
        "bg": ((crops, crop_len, width), BF16),
        "ug": ((crops, crop_len, hidden), BF16),
        "ag": ((crops, crop_len, width), BF16),
        "qg": ((crops, crop_len, 3 * width), BF16),
    }
    names = tuple(shapes)
    aliased = [grads[name] for name in names] if grads else []
    arrived = [] if recv is None else [recv]
    operands = [info, cot, *arrived, wqkv, wout, wup, wdown, biases, gains]
    operands += [state[name] for name in BACK_READ] + aliased
    whole = lambda a: pl.BlockSpec(a.shape, lambda n=len(a.shape): (0,) * n)
    in_specs = [SMEM, ANY] + [ANY] * (len(arrived) + 4) + [whole(biases), whole(gains)]
    in_specs += [ANY] * (len(BACK_READ) + len(aliased))
    first = 8 + len(arrived) + len(BACK_READ)
    rows = hidden // width + 8
    cost = pl.CostEstimate(
        flops=2 * crop_len * (wqkv[0, 0].size + wout[0, 0].size + 2 * wup[0, 0].size),
        bytes_accessed=20_000_000,
        transcendentals=0,
    )
    outs = pl.pallas_call(
        functools.partial(backward_kernel, call, recv is None, len(aliased)),
        out_shape=[
            jax.ShapeDtypeStruct((crop_len, width), BF16),
            jax.ShapeDtypeStruct((rows, width), F32),
        ]
        + [jax.ShapeDtypeStruct(*shapes[name]) for name in names],
        in_specs=in_specs,
        out_specs=[ANY, pl.BlockSpec((rows, width), lambda: (0, 0))] + [ANY] * len(names),
        input_output_aliases={first + i: 2 + i for i in range(len(aliased))},
        scratch_shapes=[
            pltpu.VMEM((crop_len, width), BF16),
            pltpu.VMEM((width, 3 * width), BF16),
            pltpu.VMEM((width, width), BF16),
            pltpu.VMEM((width, hidden), BF16),
            pltpu.VMEM((hidden, width), BF16),
            pltpu.VMEM((crop_len, 3 * width), BF16),
            pltpu.VMEM((heads, crop_len, crop_len), BF16),
            pltpu.VMEM((crop_len, width), F32),
            pltpu.VMEM((crop_len, hidden), BF16),
            pltpu.VMEM((crop_len, width), F32),
            pltpu.VMEM((crop_len, 128), F32),
            pltpu.VMEM((crop_len, width), BF16),
            pltpu.VMEM((crop_len, hidden), BF16),
            pltpu.VMEM((crop_len, width), BF16),
            pltpu.VMEM((crop_len, 3 * width), BF16),
            pltpu.VMEM((crop_len, width), BF16),
            pltpu.VMEM((crop_len, width), F32),
            pltpu.VMEM((crop_len, width), BF16),
            pltpu.SemaphoreType.DMA((7,)),
            pltpu.SemaphoreType.DMA((len(BACK_READ),)),
            pltpu.SemaphoreType.DMA,
            pltpu.SemaphoreType.DMA((6,)),
        ],
        compiler_params=pltpu.CompilerParams(vmem_limit_bytes=VMEM_LIMIT),
        cost_estimate=cost,
        name="backward_crop",
    )(*operands)
    return outs[0], outs[1], dict(zip(names, outs[2:]))


def weight_kernel(info, left, right, out):
    out[...] = mm(left[...], right[...], TN).astype(BF16)


def weight_call(info, left, right, mine):
    left = left.reshape(-1, left.shape[-1])
    right = right.reshape(-1, right.shape[-1])
    tokens, rows, columns = left.shape[0], left.shape[1] // 2, right.shape[1]
    half = lambda info: info[0] if mine else 1 - info[0]
    if rows >= columns:
        count = rows // 384
        tile = rows // count
        spec_left = pl.BlockSpec((tokens, tile), lambda i, info: (0, half(info) * count + i))
        spec_right = pl.BlockSpec((tokens, columns), lambda i, info: (0, 0))
        spec_out = pl.BlockSpec((tile, columns), lambda i, info: (i, 0))
    else:
        tile = 768
        count = columns // tile
        spec_left = pl.BlockSpec((tokens, rows), lambda i, info: (0, half(info)))
        spec_right = pl.BlockSpec((tokens, tile), lambda i, info: (0, i))
        spec_out = pl.BlockSpec((rows, tile), lambda i, info: (0, i))
    return pl.pallas_call(
        weight_kernel,
        out_shape=jax.ShapeDtypeStruct((rows, columns), BF16),
        grid_spec=pltpu.PrefetchScalarGridSpec(
            num_scalar_prefetch=1, grid=(count,), in_specs=[spec_left, spec_right], out_specs=spec_out
        ),
        compiler_params=pltpu.CompilerParams(vmem_limit_bytes=VMEM_LIMIT),
        cost_estimate=pl.CostEstimate(flops=2 * tokens * rows * columns, bytes_accessed=2 * tokens * (rows + columns) + 2 * rows * columns, transcendentals=0),
        name="weight_half",
    )(info, left, right)


def last_weight_kernel(info, left, right, left_out, right_out, out):
    step = pl.program_id(0)

    @pl.when(step < pl.num_programs(0) - 1)
    def _():
        out[...] = mm(left[...], right[...], TN).astype(BF16)

    @pl.when(step == pl.num_programs(0) - 1)
    def _():
        out[...] = mm(left_out[...], right_out[...], TN).astype(BF16)


def last_weight_call(info, left, right, left_out, right_out, mine):
    left, right, left_out, right_out = (a.reshape(-1, a.shape[-1]) for a in (left, right, left_out, right_out))
    tokens, width = left.shape
    rows, parts = width // 2, right.shape[1] // width
    half = lambda info: info[0] if mine else 1 - info[0]
    return pl.pallas_call(
        last_weight_kernel,
        out_shape=jax.ShapeDtypeStruct((rows, (parts + 1) * width), BF16),
        grid_spec=pltpu.PrefetchScalarGridSpec(
            num_scalar_prefetch=1,
            grid=(parts + 1,),
            in_specs=[
                pl.BlockSpec((tokens, rows), lambda i, info: (0, half(info))),
                pl.BlockSpec((tokens, width), lambda i, info: (0, jnp.minimum(i, parts - 1))),
                pl.BlockSpec((tokens, rows), lambda i, info: (0, half(info))),
                pl.BlockSpec((tokens, width), lambda i, info: (0, 0)),
            ],
            out_specs=pl.BlockSpec((rows, width), lambda i, info: (0, i)),
        ),
        compiler_params=pltpu.CompilerParams(vmem_limit_bytes=VMEM_LIMIT),
        cost_estimate=pl.CostEstimate(flops=2 * tokens * rows * width * (parts + 1), bytes_accessed=12_000_000, transcendentals=0),
        name="weight_half_two",
    )(info, left, right, left_out, right_out)


def ring_plan(dp, rep):
    chips = [(0, z) for z in range(rep)] + [(1, z) for z in reversed(range(rep))]
    count = len(chips)
    position = [0] * (dp * rep)
    pairs = []
    for core in range(2):
        order = chips if core == 0 else chips[::-1]
        index = [(2 * y + core) * rep + z for y, z in order]
        for place, device in enumerate(index):
            position[device] = place
            pairs.append((device, index[(place + 1) % count]))
    return count, position, pairs


def tied(value, *others):
    return lax.optimization_barrier((value, *others))[0]


class RingSum:
    def __init__(self, own, other, core, place, plan, swap):
        self.count, _, self.pairs = plan
        self.own, self.other = (a.reshape(self.count, -1, a.shape[-1]) for a in (own, other))
        self.core, self.place, self.swap = core, place, swap
        self.moving = self.block(place).astype(BF16)
        self.step, self.half = 0, None

    def block(self, number):
        number = jnp.mod(number, self.count)
        take = lambda a: lax.dynamic_index_in_dim(a, number, 0, keepdims=False).astype(F32)
        return take(self.own) + take(self.other)

    def done(self):
        return self.step == 2 * self.count - 2

    def put(self, number):
        self.half = lax.dynamic_update_index_in_dim(self.half, self.moving, jnp.mod(number, self.count), 0)

    def advance(self, last):
        self.step += 1
        moving = tied(lax.ppermute(self.moving, AXES, self.pairs), last)
        if self.step < self.count:
            self.moving = (moving.astype(F32) + self.block(self.place - self.step)).astype(BF16)
            if self.step == self.count - 1:
                self.half = jnp.zeros(self.own.shape, BF16)
                self.put(self.place + 1)
            return
        self.moving = moving
        self.put(self.place - (self.step - self.count))

    def result(self):
        half = self.half.reshape(-1, self.own.shape[-1])
        other = lax.ppermute(half, AXES, self.swap)
        both = jnp.where(self.core == 0, jnp.stack([half, other]), jnp.stack([other, half]))
        return both.reshape(-1, half.shape[-1]).astype(F32)


class RingGather:
    def __init__(self, value, place, plan, swap):
        self.count, _, self.pairs = plan
        self.place, self.swap = place, swap
        self.moving = value
        self.parts = [value]

    def done(self):
        return len(self.parts) == self.count

    def advance(self, last):
        self.moving = tied(lax.ppermute(self.moving, AXES, self.pairs), last)
        self.parts.append(self.moving)

    def result(self, core, rep):
        count = self.count
        own = jnp.stack(self.parts[::-1])
        own = jnp.roll(own, self.place + 1, 0)
        other = lax.ppermute(own, AXES, self.swap)
        first = jnp.where(core == 0, own, other)
        second = jnp.where(core == 0, other, own)[::-1]
        both = jnp.stack([first, second], 1)
        low, high = both[: count // 2], both[count // 2 :][::-1]
        whole = jnp.stack([low, high])
        whole = jnp.moveaxis(whole, 1, 2)
        return whole.reshape((2 * 2, rep) + whole.shape[3:])


AXES = ("dp", "rep")


def on_device(
    query_input,
    key_input,
    query_lengths,
    key_lengths,
    cotangent,
    w_qkv,
    w_out,
    w_up,
    w_down,
    b_up,
    biases,
    gains,
):
    section = lax.axis_index("section")
    dp, rep = lax.axis_size("dp"), lax.axis_size("rep")
    crops, crop_len, width = query_input.shape
    hidden = w_up.shape[-1]
    weights = (w_qkv, w_out, w_up, w_down, b_up, biases, gains)

    slots = list(range(crops + 1))
    calls = [(slot, slot - 1) for slot in slots] + [(slot - 1, slot) for slot in slots]
    early = min(2, crops)
    key_calls = [(slot, -1) for slot in range(early)] + [(-1, slot) for slot in range(early)]
    key_calls += [(slot, slot - 1 if slot > early else -1) for slot in range(early, crops + 1)]
    table = jnp.asarray(calls + key_calls, jnp.int32)
    lives = jnp.where(section == 0, table[:, 0], table[:, 1])
    crop_of = jnp.clip(lives, 0, crops - 1)
    is_query = jnp.arange(len(calls) + len(key_calls)) < len(calls)
    lengths = jnp.where(is_query, query_lengths[crop_of], key_lengths[crop_of])
    info = jnp.stack(
        [(lives == crop_of).astype(jnp.int32), crop_of, lengths, jnp.full(lives.shape, section)], 1
    ).astype(jnp.int32)

    def up(value):
        return lax.ppermute(value, "section", [(0, 1)])

    def down(value):
        return lax.ppermute(value, "section", [(1, 0)])

    def picked(rows, first):
        return lax.dynamic_slice_in_dim(jnp.concatenate(rows), first, crops, 0)

    state, grads = {}, {}
    pools, vectors = [], []
    key_sent, key_pools = {}, [None] * len(key_calls)

    def key_crop(number, info):
        first, second = key_calls[number]
        arrived = key_sent.get(second)
        sent, key_pools[number], _ = forward_call(
            1, info, len(calls) + number, key_input, arrived, weights, {}, False
        )
        if 0 <= first < crops:
            key_sent[first] = up(sent)

    def key_pool():
        rows = []
        for crop in range(crops):
            first = [key_pools[n] for n, call in enumerate(key_calls) if call[0] == crop][0]
            second = [key_pools[n] for n, call in enumerate(key_calls) if call[1] == crop][0]
            rows.append(jnp.where(section == 0, first, second))
        return jnp.concatenate(rows)

    arrived = returned = None
    for slot in range(crops + 2):
        if slot <= crops:
            sent, pooled, state = forward_call(
                0, info, slot, query_input, arrived, weights, state, True, vectors[-1:]
            )
            pools.append(pooled)
        if slot < crops:
            arrived = up(sent)
        if slot == 1:
            key_crop(0, tied(info, pooled))
        if slot == crops:
            for number in range(1, early):
                key_crop(number, tied(info, pooled))
        if slot == crops + 1:
            for number in range(early, 2 * early):
                key_crop(number, tied(info, vectors[-1]))
        if slot >= 1:
            late = info
            if slot == 1:
                late = tied(info, key_pools[0])
            if slot == crops:
                late = tied(info, *key_pools[1:early])
            if slot == crops + 1:
                late = tied(info, *key_pools[early : 2 * early])
            back, vector, grads = backward_call(late, crops + slot, cotangent, returned, weights, state, grads)
            vectors.append(vector)
            returned = down(back)

    core = jnp.mod(lax.axis_index("dp"), 2)
    core_info = core.astype(jnp.int32)[None]
    swap = [(d * rep + z, (d ^ 1) * rep + z) for d in range(dp) for z in range(rep)]
    products = (
        lambda mine, core_info: weight_call(core_info, state["act"], grads["bg"], mine),
        lambda mine, core_info: weight_call(core_info, state["low"], grads["ug"], mine),
        lambda mine, core_info: last_weight_call(
            core_info, state["xs"], grads["qg"], state["mix"], grads["ag"], mine
        ),
    )
    vector = sum(vectors)
    late_keys = range(2 * early, len(key_calls))
    if dp == 4:
        plan = ring_plan(dp, rep)
        place = jnp.asarray(plan[1], jnp.int32)[lax.axis_index(AXES)]
        rings, last = [], vector

        def advance(last):
            for ring in rings:
                if not ring.done():
                    ring.advance(last)
                    last = ring.moving
            return last

        for product in products:
            theirs = product(False, tied(core_info, last))
            last = advance(theirs)
            other = lax.ppermute(theirs, AXES, swap)
            own = product(True, tied(core_info, last))
            last = advance(own)
            rings.append(RingSum(own, other, core, place, plan, swap))
        sums = list(rings)
        for number in late_keys:
            key_crop(number, tied(info, last))
            last = advance(key_pools[number])
        small = jnp.concatenate([vector, picked(pools, section), key_pool()])
        gather = RingGather(small, place, plan, swap)
        rings.insert(0, gather)
        while not all(ring.done() for ring in rings):
            last = advance(last)
        small = gather.result(core, rep)
        totals = [ring.result() for ring in sums]
        ratio = vector.shape[0]
        every = small.reshape((dp * rep,) + small.shape[2:])
        vector = jnp.sum(every[:, :ratio], 0)
        pooled_query = every[:, ratio : ratio + crops].reshape(-1, width)
        pooled_key = every[:, ratio + crops :].reshape(-1, width)
    else:
        totals = []
        for product in products:
            theirs, own = product(False, core_info), product(True, core_info)
            both = jnp.where(core == 0, jnp.stack([own, theirs]), jnp.stack([theirs, own]))
            totals.append(lax.psum(both.reshape(-1, own.shape[-1]), AXES).astype(F32))
        for number in late_keys:
            key_crop(number, info)
        vector = lax.psum(vector, AXES)
        pooled_query = lax.all_gather(picked(pools, section), AXES, axis=0, tiled=True)
        pooled_key = lax.all_gather(key_pool(), AXES, axis=0, tiled=True)
    ratio = hidden // width
    return (
        pooled_query[None],
        pooled_key[None],
        grads["ig"][None],
        totals[2][None, :, : 3 * width],
        totals[2][None, :, 3 * width :],
        totals[1][None],
        totals[0][None],
        vector[:ratio].reshape(1, hidden),
        vector[None, ratio : ratio + 6],
        vector[None, ratio + 6 : ratio + 8],
    )


def solution(mesh):
    placed = (
        P(("dp", "rep"), None, None),
        P(("dp", "rep"), None, None),
        P(("dp", "rep")),
        P(("dp", "rep")),
        P(("dp", "rep"), None, None),
        P("section", None, None, None),
        P("section", None, None, None),
        P("section", None, None, None),
        P("section", None, None, None),
        P("section", None, None),
        P("section", None, None, None),
        P("section", None, None, None),
    )
    return jax.shard_map(
        on_device,
        mesh=mesh,
        in_specs=placed,
        out_specs=(
            P("section", None, None),
            P("section", None, None),
            P("section", ("dp", "rep"), None, None),
            P("section", None, None),
            P("section", None, None),
            P("section", None, None),
            P("section", None, None),
            P("section", None),
            P("section", None, None),
            P("section", None, None),
        ),
        check_vma=False,
    )
```

```python
import functools
import math

import jax
import jax.numpy as jnp
from jax import lax
from jax.experimental import pallas as pl
from jax.experimental.pallas import tpu as pltpu
from jax.sharding import PartitionSpec as P

HEAD = 64
EPS = 1e-06
NEG = -1000000000.0
VMEM_LIMIT = 16 * 1024 * 1024
HELD_CROPS = 3
HELD_LIMIT = 10 * 1024 * 1024
PASS_LIMIT = 22 * 1024 * 1024
NT = (((1,), (1,)), ((), ()))
TN = (((0,), (0,)), ((), ()))
F32 = jnp.float32
BF16 = jnp.bfloat16
ANY = pl.BlockSpec(memory_space=pl.ANY)
SMEM = pl.BlockSpec(memory_space=pltpu.SMEM)


def mm(left, right, dims=(((1,), (0,)), ((), ()))):
    return lax.dot_general(left, right, dims, preferred_element_type=F32)


def row_variants(crop_len):
    return [crop_len]


def gelu_pair(values):
    cdf = 0.5 + 0.5 * lax.erf(values * (2.0**-0.5))
    density = jnp.exp(-0.5 * values * values) * (2.0 * math.pi) ** -0.5
    return values * cdf, cdf + values * density


def norm_forward(hidden):
    centred = hidden - jnp.mean(hidden, -1, keepdims=True)
    inverse = lax.rsqrt(jnp.mean(centred * centred, -1, keepdims=True) + EPS)
    return centred * inverse, inverse


def norm_backward(scaled, normed, inverse):
    return (
        scaled
        - jnp.mean(scaled, -1, keepdims=True)
        - normed * jnp.mean(scaled * normed, -1, keepdims=True)
    ) * inverse


def dispatch(length, crop_len, body):
    lower = 0
    for rows in row_variants(crop_len):
        pl.when((length > lower) & (length <= rows))(functools.partial(body, rows))
        lower = rows


VMEM_NAMES = ("qkv", "n1", "gp", "n2", "inv")
HBM_NAMES = ("att", "xs", "mix", "low", "act")


def save_shapes(crops, crop_len, width, hidden):
    heads = width // HEAD
    held = min(HELD_CROPS, crops)
    return {
        "qkv": ((held, crop_len, 3 * width), BF16),
        "att": ((crops + 1, heads, crop_len, crop_len), BF16),
        "n1": ((held, crop_len, width), BF16),
        "gp": ((held, crop_len, hidden), BF16),
        "n2": ((held, crop_len, width), BF16),
        "inv": ((held, crop_len, 128), F32),
        "xs": ((crops + 1, crop_len, width), BF16),
        "mix": ((crops + 1, crop_len, width), BF16),
        "low": ((crops + 1, crop_len, width), BF16),
        "act": ((crops + 1, crop_len, hidden), BF16),
    }


VMEM = pl.BlockSpec(memory_space=pltpu.VMEM)


def in_hbm(*values):
    return [pltpu.with_memory_space_constraint(value, pltpu.HBM) for value in values]


def in_vmem(*values):
    return [pltpu.with_memory_space_constraint(value, pltpu.VMEM) for value in values]


def each_lagged(count, first, second, third):
    ahead, waiting = first(0), None
    for number in range(count):
        current, ahead = ahead, first(number + 1) if number + 1 < count else None
        if waiting is not None:
            third(*waiting)
        waiting = (number, second(number, current))
    third(*waiting)


def assigned(crops, query_lengths, key_lengths):
    section = lax.axis_index("section")
    member = jnp.where(section == 0, crops[0][0], crops[1][0])
    crop = jnp.where(section == 0, crops[0][1], crops[1][1])
    live = crop >= 0
    crop = jnp.maximum(crop, 0)
    return section, live, member, crop, jnp.where(member == 0, query_lengths[crop], key_lengths[crop])


def head_masks():
    lane = lax.broadcasted_iota(jnp.int32, (1, 2 * HEAD), 1)
    return lane < HEAD, lane >= HEAD


def forward_kernel(mode, crops, first, n_alias, query_lengths, key_lengths, own, *refs):
    refs = list(refs)
    take = lambda count: [refs.pop(0) for _ in range(count)]
    recv = None if first else take(1)[0]
    weights = take(4)
    bup, biases, gains = take(3)
    take(n_alias)
    y_ref, pool_ref = take(2)
    save = mode != "pass"
    kept = dict(zip(VMEM_NAMES + HBM_NAMES, take(10))) if save else {}
    if mode == "held":
        held = weights
    else:
        held = take(4)
    if not save:
        kept["qkv"] = take(1)[0]
    batt = take(1)[0] if save else None
    bx, bmix, blow, bact, wsem, xsem, osem = refs
    wqkv, wout, wup, wdown = held
    crop_len, width = bx.shape
    hidden = bact.shape[1]
    heads = width // HEAD
    base = hidden // width
    section, live, member, crop, length = assigned(crops, query_lengths, key_lengths)
    which = member if save else 0
    place = jnp.where(member == 0, lax.rem(crop, HELD_CROPS), 1) if save else 0

    loaded = crops[0][0]

    def weight_copy(number):
        target = held[number].at[loaded if save else 0]
        return pltpu.make_async_copy(weights[number].at[0, loaded if save else 1], target, wsem.at[number])

    def weight_ready(number):
        if mode != "held":
            weight_copy(number).wait()

    def bias(row):
        return biases[0, member, row : row + 1, :]

    def gain(row):
        return gains[0, member, row : row + 1, :]

    def rise_bias(cols):
        return jnp.where(member == 0, bup[0, 0:1, cols], bup[0, 1:2, cols])

    def body(rows):
        keys = -(-rows // 128) * 128
        qkv = kept["qkv"]
        started = []

        def clear(ref, *index):
            if rows < crop_len:
                ref[(*index, slice(rows, crop_len))] = jnp.zeros((crop_len - rows, ref.shape[-1]), ref.dtype)

        def finish(number, name, buffer):
            if name != "att":
                clear(buffer)
            if save:
                slot = jnp.where(member == 0, crop, kept[name].shape[0] - 1)
                copy = pltpu.make_async_copy(buffer, kept[name].at[slot], osem.at[number])
                copy.start()
                started.append(copy)

        x = bx[:rows, :]
        finish(0, "xs", bx)
        weight_ready(0)
        for segment in range(3):
            cols = slice(segment * width, (segment + 1) * width)
            part = mm(x, wqkv[which, :, cols])
            if segment != 1:
                part = part + bias(segment // 2)
            qkv[place, :rows, cols] = part.astype(BF16)
        clear(qkv, place)
        masks = head_masks()
        key_valid = lax.broadcasted_iota(jnp.int32, (1, keys), 1) < length
        mixed = [None]

        def pair(part, head, row_count):
            start = part * width + head // 2 * 2 * HEAD
            return qkv[place, :row_count, start : start + 2 * HEAD]

        def score(head):
            return mm(pair(0, head, rows), jnp.where(masks[head % 2], pair(1, head, keys), 0), NT)

        def soften(head, scores):
            scores = jnp.where(key_valid, scores * HEAD**-0.5, NEG)
            weight = jnp.exp(scores - jnp.max(scores, -1, keepdims=True))
            weight = (weight * (1.0 / jnp.sum(weight, -1, keepdims=True))).astype(BF16)
            if save:
                batt[head, :rows, :keys] = weight
            return weight

        def mix(head, weight):
            part = mm(weight, jnp.where(masks[head % 2], pair(2, head, keys), 0))
            if head % 2 == 0:
                mixed[0] = part
            else:
                start = head // 2 * 2 * HEAD
                bmix[:rows, start : start + 2 * HEAD] = (mixed[0] + part).astype(BF16)

        each_lagged(heads, score, soften, mix)
        if save:
            finish(4, "att", batt)
        finish(1, "mix", bmix)
        weight_ready(1)
        attended = mm(bmix[:rows, :], wout[which]) + bias(2)
        n1, inv1 = norm_forward(x.astype(F32) + attended)
        after = n1 * gain(0) + bias(3)
        low = after.astype(BF16)
        blow[:rows, :] = low
        finish(2, "low", blow)
        weight_ready(2)
        weight_ready(3)
        branch = [after + bias(4)]

        def cols(part):
            return slice(part * width, (part + 1) * width)

        def rise(part):
            return mm(low, wup[which, :, cols(part)]) + rise_bias(cols(part))

        def activate(part, pre):
            act, slope = gelu_pair(pre)
            act = act.astype(BF16)
            bact[:rows, cols(part)] = act
            if save:
                kept["gp"][place, :rows, cols(part)] = slope.astype(BF16)
            return act

        def fall(part, act):
            branch[0] = branch[0] + mm(act, wdown[which, cols(part), :])

        each_lagged(base, rise, activate, fall)
        finish(3, "act", bact)
        n2, inv2 = norm_forward(branch[0])
        out = n2 * gain(1) + bias(5)
        y_ref[:rows, :] = out.astype(BF16)
        clear(y_ref)
        valid = lax.broadcasted_iota(jnp.int32, (rows, 1), 0) < length
        total = jnp.sum(jnp.where(valid, out, 0.0), 0, keepdims=True)
        pool_ref[...] = total / length.astype(F32)
        if save:
            kept["n1"][place, :rows, :] = n1.astype(BF16)
            kept["n2"][place, :rows, :] = n2.astype(BF16)
            wide = lax.broadcasted_iota(jnp.int32, (1, 128), 1)
            kept["inv"][place, :rows, :] = jnp.where(wide == 0, inv1, inv2)
        for copy in started:
            copy.wait()

    @pl.when(live)
    def _():
        @pl.when(section == 0)
        def _():
            copy = pltpu.make_async_copy(own.at[crop], bx, xsem)
            copy.start()

        if mode != "held":
            for number in range(4):
                weight_copy(number).start()

        @pl.when(section == 0)
        def _():
            pltpu.make_async_copy(own.at[crop], bx, xsem).wait()

        if recv is not None:

            @pl.when(section != 0)
            def _():
                bx[...] = recv[...]

        dispatch(length, crop_len, body)

    if mode == "load":

        @pl.when(jnp.logical_not(live))
        def _():
            for number in range(4):
                weight_copy(number).start()
            for number in range(4):
                weight_copy(number).wait()


def forward_call(mode, lengths, crops, own, recv, weights, held, state, order=()):
    crop_count, crop_len, width = own.shape
    hidden = weights[2].shape[-1]
    shapes = save_shapes(crop_count, crop_len, width, hidden)
    names = VMEM_NAMES + HBM_NAMES if mode != "pass" else ()
    pinned = lambda name, value: (in_vmem if name in VMEM_NAMES else in_hbm)(value)[0]
    aliased = [pinned(name, state[name]) for name in names] if state else []
    order = list(order)
    arrived = [] if recv is None else [recv]
    read = in_vmem(*held) if mode == "held" else in_hbm(*weights[:4])
    grown = in_vmem(*held) if mode == "load" and held else []
    operands = [*lengths, *in_hbm(own), *arrived, *read, *weights[4:], *order, *aliased, *grown]
    first = 10 + len(arrived) + len(order)
    shape_of = lambda name: (pltpu.VMEM if name in VMEM_NAMES else pltpu.HBM)(*shapes[name])
    spec_of = lambda name: VMEM if name in VMEM_NAMES else ANY
    copies = 1 if mode == "pass" else 2
    weight_shapes = [pltpu.VMEM((copies, *weight.shape[2:]), BF16) for weight in weights[:4]]
    outs = pl.pallas_call(
        functools.partial(forward_kernel, mode, crops, recv is None, len(order) + len(aliased) + len(grown)),
        out_shape=[
            jax.ShapeDtypeStruct((crop_len, width), BF16),
            jax.ShapeDtypeStruct((1, width), F32),
        ]
        + [shape_of(name) for name in names]
        + (weight_shapes if mode == "load" else []),
        in_specs=[SMEM, SMEM, ANY]
        + [VMEM] * len(arrived)
        + [VMEM if mode == "held" else ANY] * 4
        + [VMEM] * 3
        + [ANY] * len(order)
        + [spec_of(name) for name in names][: len(aliased)]
        + [VMEM] * len(grown),
        out_specs=[VMEM, VMEM] + [spec_of(name) for name in names] + ([VMEM] * 4 if mode == "load" else []),
        input_output_aliases={first + i: 2 + i for i in range(len(aliased) + len(grown))},
        scratch_shapes=(weight_shapes if mode == "pass" else [])
        + [
            pltpu.VMEM((1, crop_len, 3 * width), BF16)
            if mode == "pass"
            else pltpu.VMEM((width // HEAD, crop_len, crop_len), BF16)
        ]
        + [
            pltpu.VMEM((crop_len, width), BF16),
            pltpu.VMEM((crop_len, width), BF16),
            pltpu.VMEM((crop_len, width), BF16),
            pltpu.VMEM((crop_len, hidden), BF16),
            pltpu.SemaphoreType.DMA((4,)),
            pltpu.SemaphoreType.DMA,
            pltpu.SemaphoreType.DMA((5,)),
        ],
        compiler_params=pltpu.CompilerParams(vmem_limit_bytes=PASS_LIMIT if mode == "pass" else HELD_LIMIT),
        cost_estimate=crop_cost(weights, crop_len),
        name="forward_crop",
    )(*operands)
    return outs[0], outs[1], outs[2 + len(names) :], dict(zip(names, outs[2:]))


def crop_cost(weights, crop_len):
    size = sum(weight[0, 0].size for weight in weights[:4])
    return pl.CostEstimate(flops=2 * crop_len * size, bytes_accessed=8_000_000, transcendentals=0)


def backward_kernel(crops, first, n_alias, lengths, cot, *refs):
    refs = list(refs)
    take = lambda count: [refs.pop(0) for _ in range(count)]
    recv = None if first else take(1)[0]
    wqkv, wout, wup, wdown, gains = take(5)
    kept = dict(zip(VMEM_NAMES, take(len(VMEM_NAMES))))
    att = take(1)[0]
    take(n_alias)
    dx_ref, vec_ref, ig_ref, bg_ref, ug_ref, ag_ref, qg_ref = take(7)
    batt, bgin, bbg, bug, bag, bqg, bmg, bxg, asem, gsem, osem = refs
    crop_len, width = bbg.shape
    hidden = bug.shape[1]
    heads = width // HEAD
    base = hidden // width
    section, live, _, crop, length = assigned([(0, crop) for crop in crops], lengths, lengths)
    place = lax.rem(crop, HELD_CROPS)

    def gain(row):
        return gains[0, 0, row : row + 1, :]

    def att_copy():
        return pltpu.make_async_copy(att.at[crop], batt, asem)

    def body(rows):
        keys = -(-rows // 128) * 128
        started = []

        def clear(buffer):
            if rows < crop_len:
                buffer[rows:, :] = jnp.zeros((crop_len - rows, buffer.shape[1]), buffer.dtype)

        def finish(number, buffer, target):
            clear(buffer)
            copy = pltpu.make_async_copy(buffer, target, osem.at[number])
            copy.start()
            started.append(copy)

        def column(row, values, start=0):
            vec_ref[row : row + 1, start : start + values.shape[1]] = jnp.sum(values.astype(F32), 0, keepdims=True)

        valid = lax.broadcasted_iota(jnp.int32, (rows, 1), 0) < length
        g = jnp.where(valid, bgin[:rows, :].astype(F32), 0.0)
        n2 = kept["n2"][place, :rows, :].astype(F32)
        inv1 = kept["inv"][place, :rows, 0:1]
        inv2 = kept["inv"][place, :rows, 1:2]
        sum_two = norm_backward(g * gain(1), n2, inv2)
        bg = sum_two.astype(BF16)
        bbg[:rows, :] = bg
        finish(0, bbg, bg_ref.at[crop])
        column(base + 5, g)
        column(base + 7, g * n2)
        column(base + 4, bg)
        side = [sum_two]

        def cols(part):
            return slice(part * width, (part + 1) * width)

        def descend(part):
            return mm(bg, wdown[0, cols(part), :], NT)

        def slope(part, grad):
            grad = (grad * kept["gp"][place, :rows, cols(part)].astype(F32)).astype(BF16)
            bug[:rows, cols(part)] = grad
            column(part, grad)
            return grad

        def ascend(part, grad):
            side[0] = side[0] + mm(grad, wup[0, :, cols(part)], NT)

        each_lagged(base, descend, slope, ascend)
        finish(1, bug, ug_ref.at[crop])
        n1 = kept["n1"][place, :rows, :].astype(F32)
        side = side[0]
        sum_one = norm_backward(side * gain(0), n1, inv1)
        ag = sum_one.astype(BF16)
        bag[:rows, :] = ag
        finish(2, bag, ag_ref.at[crop])
        column(base + 3, side)
        column(base + 6, side * n1)
        column(base + 2, ag)
        bmg[:rows, :] = mm(ag, wout[0], NT).astype(BF16)
        att_copy().wait()
        masks = head_masks()
        scale = HEAD**-0.5
        sums = [None]

        def pair(part, head, row_count):
            start = part * width + head // 2 * 2 * HEAD
            return jnp.where(masks[head % 2], kept["qkv"][place, :row_count, start : start + 2 * HEAD], 0)

        def attention_grad(head):
            start = head // 2 * 2 * HEAD
            return mm(bmg[:rows, start : start + 2 * HEAD], pair(2, head, keys), NT)

        def score_grad(head, grad):
            wide = batt[head, :rows, :keys].astype(F32)
            both = wide * grad
            return (both - wide * jnp.sum(both, -1, keepdims=True)).astype(BF16)

        def spread(head, score):
            start = head // 2 * 2 * HEAD
            mg = jnp.where(masks[head % 2], bmg[:rows, start : start + 2 * HEAD], 0)
            parts = (
                mm(score, pair(1, head, keys)),
                mm(score, pair(0, head, rows), TN),
                mm(batt[head, :rows, :keys], mg, TN),
            )
            if head % 2 == 0:
                sums[0] = parts
                return
            dq, dk, dv = (old + new for old, new in zip(sums[0], parts))
            dq = (dq * scale).astype(BF16)
            dv = dv[:rows].astype(BF16)
            bqg[:rows, start : start + 2 * HEAD] = dq
            bqg[:rows, width + start : width + start + 2 * HEAD] = (dk[:rows] * scale).astype(BF16)
            bqg[:rows, 2 * width + start : 2 * width + start + 2 * HEAD] = dv
            column(base, dq, start)
            column(base + 1, dv, start)

        each_lagged(heads, attention_grad, score_grad, spread)
        finish(3, bqg, qg_ref.at[crop])
        xg = sum_one + mm(bqg[:rows, :], wqkv[0], NT)
        dx = xg.astype(BF16)
        dx_ref[:rows, :] = dx
        clear(dx_ref)
        bxg[:rows, :] = jnp.where(section == 0, xg, dx.astype(F32))
        finish(4, bxg, ig_ref.at[crop])
        for copy in started:
            copy.wait()

    @pl.when(jnp.logical_not(live))
    def _():
        vec_ref[...] = jnp.zeros(vec_ref.shape, F32)

    @pl.when(live)
    def _():
        if recv is not None:

            @pl.when(section == 0)
            def _():
                bgin[...] = recv[...]

        @pl.when(section != 0)
        def _():
            copy = pltpu.make_async_copy(cot.at[crop], bgin, gsem)
            copy.start()
            copy.wait()

        att_copy().start()
        dispatch(length, crop_len, body)


def backward_call(lengths, crops, cot, recv, weights, held, state, grads, order=()):
    crop_count, crop_len, width = cot.shape
    hidden = weights[2].shape[-1]
    shapes = {
        "ig": ((crop_count, crop_len, width), F32),
        "bg": ((crop_count, crop_len, width), BF16),
        "ug": ((crop_count, crop_len, hidden), BF16),
        "ag": ((crop_count, crop_len, width), BF16),
        "qg": ((crop_count, crop_len, 3 * width), BF16),
    }
    names = tuple(shapes)
    aliased = in_hbm(*[grads[name] for name in names]) if grads else []
    arrived = [] if recv is None else [recv]
    operands = [lengths, *in_hbm(cot), *arrived, *in_vmem(*held), weights[6]]
    order = list(order)
    operands += in_vmem(*[state[name] for name in VMEM_NAMES]) + in_hbm(state["att"]) + order + aliased
    first = 8 + len(arrived) + len(VMEM_NAMES) + len(order)
    outs = pl.pallas_call(
        functools.partial(backward_kernel, crops, recv is None, len(order) + len(aliased)),
        out_shape=[
            jax.ShapeDtypeStruct((crop_len, width), BF16),
            jax.ShapeDtypeStruct((hidden // width + 8, width), F32),
        ]
        + [pltpu.HBM(*shapes[name]) for name in names],
        in_specs=[SMEM, ANY] + [VMEM] * (len(arrived) + 5 + len(VMEM_NAMES)) + [ANY] * (1 + len(order) + len(aliased)),
        out_specs=[VMEM, VMEM] + [ANY] * len(names),
        input_output_aliases={first + i: 2 + i for i in range(len(aliased))},
        scratch_shapes=[
            pltpu.VMEM((width // HEAD, crop_len, crop_len), BF16),
            pltpu.VMEM((crop_len, width), BF16),
            pltpu.VMEM((crop_len, width), BF16),
            pltpu.VMEM((crop_len, hidden), BF16),
            pltpu.VMEM((crop_len, width), BF16),
            pltpu.VMEM((crop_len, 3 * width), BF16),
            pltpu.VMEM((crop_len, width), BF16),
            pltpu.VMEM((crop_len, width), F32),
            pltpu.SemaphoreType.DMA,
            pltpu.SemaphoreType.DMA,
            pltpu.SemaphoreType.DMA((5,)),
        ],
        compiler_params=pltpu.CompilerParams(vmem_limit_bytes=HELD_LIMIT),
        cost_estimate=crop_cost(weights, crop_len),
        name="backward_crop",
    )(*operands)
    return outs[0], outs[1], dict(zip(names, outs[2:]))


def weight_kernel(info, left, right, out):
    out[...] = mm(left[...], right[...], TN).astype(BF16)


def weight_call(info, left, right, mine):
    left = left.reshape(-1, left.shape[-1])
    right = right.reshape(-1, right.shape[-1])
    tokens, rows, columns = right.shape[0], left.shape[1] // 2, right.shape[1]
    half = lambda info: info[0] if mine else 1 - info[0]
    if rows >= columns:
        count = rows // 384
        tile = rows // count
        spec_left = pl.BlockSpec((tokens, tile), lambda i, info: (0, half(info) * count + i))
        spec_right = pl.BlockSpec((tokens, columns), lambda i, info: (0, 0))
        spec_out = pl.BlockSpec((tile, columns), lambda i, info: (i, 0))
    else:
        tile = 768
        count = columns // tile
        spec_left = pl.BlockSpec((tokens, rows), lambda i, info: (0, half(info)))
        spec_right = pl.BlockSpec((tokens, tile), lambda i, info: (0, i))
        spec_out = pl.BlockSpec((rows, tile), lambda i, info: (0, i))
    return pl.pallas_call(
        weight_kernel,
        out_shape=jax.ShapeDtypeStruct((rows, columns), BF16),
        grid_spec=pltpu.PrefetchScalarGridSpec(
            num_scalar_prefetch=1, grid=(count,), in_specs=[spec_left, spec_right], out_specs=spec_out
        ),
        compiler_params=pltpu.CompilerParams(vmem_limit_bytes=VMEM_LIMIT),
        cost_estimate=pl.CostEstimate(flops=2 * tokens * rows * columns, bytes_accessed=2 * tokens * (rows + columns) + 2 * rows * columns, transcendentals=0),
        name="weight_half",
    )(info, *in_hbm(left, right))


def last_weight_kernel(info, left, right, left_out, right_out, out):
    step = pl.program_id(0)

    @pl.when(step < pl.num_programs(0) - 1)
    def _():
        out[...] = mm(left[...], right[...], TN).astype(BF16)

    @pl.when(step == pl.num_programs(0) - 1)
    def _():
        out[...] = mm(left_out[...], right_out[...], TN).astype(BF16)


def last_weight_call(info, left, right, left_out, right_out, mine):
    left, right, left_out, right_out = (a.reshape(-1, a.shape[-1]) for a in (left, right, left_out, right_out))
    (tokens, columns), width = right.shape, left.shape[1]
    rows, parts = width // 2, columns // width
    half = lambda info: info[0] if mine else 1 - info[0]
    return pl.pallas_call(
        last_weight_kernel,
        out_shape=jax.ShapeDtypeStruct((rows, (parts + 1) * width), BF16),
        grid_spec=pltpu.PrefetchScalarGridSpec(
            num_scalar_prefetch=1,
            grid=(parts + 1,),
            in_specs=[
                pl.BlockSpec((tokens, rows), lambda i, info: (0, half(info))),
                pl.BlockSpec((tokens, width), lambda i, info: (0, jnp.minimum(i, parts - 1))),
                pl.BlockSpec((tokens, rows), lambda i, info: (0, half(info))),
                pl.BlockSpec((tokens, width), lambda i, info: (0, 0)),
            ],
            out_specs=pl.BlockSpec((rows, width), lambda i, info: (0, i)),
        ),
        compiler_params=pltpu.CompilerParams(vmem_limit_bytes=VMEM_LIMIT),
        cost_estimate=pl.CostEstimate(flops=2 * tokens * rows * width * (parts + 1), bytes_accessed=12_000_000, transcendentals=0),
        name="weight_half_two",
    )(info, *in_hbm(left, right, left_out, right_out))


def ring_plan(dp, rep):
    chips = [(0, z) for z in range(rep)] + [(1, z) for z in reversed(range(rep))]
    count = len(chips)
    position = [0] * (dp * rep)
    pairs = []
    for core in range(2):
        order = chips if core == 0 else chips[::-1]
        index = [(2 * y + core) * rep + z for y, z in order]
        for place, device in enumerate(index):
            position[device] = place
            pairs.append((device, index[(place + 1) % count]))
    return count, position, pairs


def place_kernel(info, half, *refs):
    outs = refs[len(refs) // 2 :]
    start = 0
    for out in outs:
        out[...] = half[:, start : start + out.shape[1]].astype(F32)
        start += out.shape[1]


def place_call(info, half, widths, outs):
    rows, columns = half.shape
    count = 4
    tile = rows // count
    return pl.pallas_call(
        place_kernel if outs else lambda info, half, *refs: place_kernel(info, half, *refs, *refs),
        out_shape=[jax.ShapeDtypeStruct((2 * rows, width), F32) for width in widths],
        grid_spec=pltpu.PrefetchScalarGridSpec(
            num_scalar_prefetch=1,
            grid=(count,),
            in_specs=[pl.BlockSpec((tile, columns), lambda i, info: (i, 0))] + [ANY] * len(outs),
            out_specs=[pl.BlockSpec((tile, width), lambda i, info: (info[0] * count + i, 0)) for width in widths],
        ),
        input_output_aliases={2 + n: n for n in range(len(outs))},
        compiler_params=pltpu.CompilerParams(vmem_limit_bytes=VMEM_LIMIT),
        cost_estimate=pl.CostEstimate(flops=0, bytes_accessed=6 * rows * columns, transcendentals=0),
        name="place_half",
    )(info, half, *outs)


def tied(value, *others):
    return lax.optimization_barrier((value, *others))[0]


class RingSum:
    def __init__(self, own, other, core, place, plan, swap, widths):
        self.count, _, self.pairs = plan
        self.own, self.other = (a.reshape(self.count, -1, a.shape[-1]) for a in (own, other))
        self.core, self.place, self.swap = core, place, swap
        self.moving = self.block(place).astype(BF16)
        self.step, self.half = 0, None
        self.widths, self.outs, self.finished = widths, [], False

    def block(self, number):
        number = jnp.mod(number, self.count)
        take = lambda a: lax.dynamic_index_in_dim(a, number, 0, keepdims=False).astype(F32)
        return take(self.own) + take(self.other)

    def done(self):
        return self.step == 2 * self.count - 2

    def put(self, number):
        self.half = lax.dynamic_update_index_in_dim(self.half, self.moving, jnp.mod(number, self.count), 0)

    def advance(self, last):
        self.step += 1
        moving = tied(lax.ppermute(self.moving, AXES, self.pairs), last)
        if self.step < self.count:
            self.moving = (moving.astype(F32) + self.block(self.place - self.step)).astype(BF16)
            if self.step == self.count - 1:
                self.half = jnp.zeros(self.own.shape, BF16)
                self.put(self.place + 1)
            return
        self.moving = moving
        self.put(self.place - (self.step - self.count))

    def finish(self, last):
        if not self.outs:
            self.half = self.half.reshape(-1, self.own.shape[-1])
            self.swapped = lax.ppermute(self.half, AXES, self.swap)
            self.outs = place_call(tied(self.core[None], last), self.half, self.widths, [])
        else:
            swapped = tied(self.swapped, last)
            self.outs = place_call((1 - self.core)[None], swapped, self.widths, self.outs)
            self.finished = True
        return self.outs[0]


class RingGather:
    def __init__(self, value, cuts, core, place, rep, plan, swap):
        self.cuts = cuts
        self.count, _, self.pairs = plan
        self.core, self.place, self.rep, self.swap = core, place, rep, swap
        self.moving = value
        self.parts = [value]
        self.finished = False

    def done(self):
        return len(self.parts) == self.count

    def advance(self, last):
        self.moving = tied(lax.ppermute(self.moving, AXES, self.pairs), last)
        self.parts.append(self.moving)

    def finish(self, last):
        core, rep = self.core, self.rep
        count = self.count
        own = jnp.stack(self.parts[::-1])
        own = jnp.roll(own, self.place + 1, 0)
        other = lax.ppermute(own, AXES, self.swap)
        first = jnp.where(core == 0, own, other)
        second = jnp.where(core == 0, other, own)[::-1]
        both = jnp.stack([first, second], 1)
        low, high = both[: count // 2], both[count // 2 :][::-1]
        whole = jnp.stack([low, high])
        whole = jnp.moveaxis(whole, 1, 2)
        whole = whole.reshape((2 * 2 * rep,) + whole.shape[3:])
        starts = [sum(self.cuts[:number]) for number in range(len(self.cuts))]
        parts = [whole[:, start : start + cut] for start, cut in zip(starts, self.cuts)]
        self.outs = [jnp.sum(parts[0], 0)] + [part.reshape(-1, part.shape[-1]) for part in parts[1:]]
        self.outs = lax.optimization_barrier((*self.outs, last))[:-1]
        self.finished = True
        return self.outs[-1]


AXES = ("dp", "rep")


def on_device(
    query_input,
    key_input,
    query_lengths,
    key_lengths,
    cotangent,
    w_qkv,
    w_out,
    w_up,
    w_down,
    b_up,
    biases,
    gains,
):
    section = lax.axis_index("section")
    dp, rep = lax.axis_size("dp"), lax.axis_size("rep")
    crops, crop_len, width = query_input.shape
    hidden = w_up.shape[-1]
    weights = (w_qkv, w_out, w_up, w_down, b_up, biases, gains)

    core = jnp.mod(lax.axis_index("dp"), 2).astype(jnp.int32)
    place = jnp.zeros((), jnp.int32)
    if dp == 4:
        plan = ring_plan(dp, rep)
        place = jnp.asarray(plan[1], jnp.int32)[lax.axis_index(AXES)]
    query_lengths, core, place, section = lax.optimization_barrier((query_lengths, core, place, section))

    def sum_of(vectors):
        return sum(lax.optimization_barrier(tuple(vectors)))

    def up(value):
        return lax.ppermute(value, "section", [(0, 1)])

    def down(value):
        return lax.ppermute(value, "section", [(1, 0)])

    state, grads = {}, {}
    vectors = []

    lengths = (query_lengths, key_lengths)
    idle = (0, -1)
    query = lambda crop: (0, crop) if 0 <= crop < crops else idle
    key = lambda crop: (1, crop) if 0 <= crop < crops else idle
    plan_of_calls = [(query(0), idle), (key(0), idle)]
    for crop in range(1, crops):
        plan_of_calls += [(query(crop), query(crop - 1)), None]
    plan_of_calls += [(key(1), query(crops - 1)), None, (key(2), key(0)), None]
    late_calls = [(key(crop), key(crop - 2)) for crop in range(3, crops + 2)]
    sent_on, pooled_rows = {}, {}

    def forward(mode, call, held, state, order, lengths=lengths):
        sent, pooled, loaded, state = forward_call(
            mode, lengths, call, key_input if call[0][0] else query_input, sent_on.get(call[1]), weights, held, state, order
        )
        for number, done in enumerate(call):
            if done[1] >= 0:
                pooled_rows[number, *done] = pooled
        if call[0][1] >= 0:
            sent_on[call[0]] = up(sent)
        return pooled, loaded or held, state

    def pool(member):
        first, second = (jnp.concatenate([pooled_rows[number, member, crop] for crop in range(crops)]) for number in range(2))
        return jnp.where(section == 0, first, second)

    returned = held = None
    order = []
    backs = 0
    for number, call in enumerate(plan_of_calls):
        if call is not None:
            pooled, held, state = forward("held" if number > 1 else "load", call, held, state, order)
            order = [pooled]
        else:
            assignment = (backs - 1, backs if backs < crops else -1)
            back, vector, grads = backward_call(
                query_lengths, assignment, cotangent, returned, weights, held, state, grads, order
            )
            order = [vector]
            vectors.append(vector)
            returned = down(back)
            backs += 1

    section, core, place, vector = lax.optimization_barrier((section, core, place, sum_of(vectors)))
    core_info = core[None]
    swap = [(d * rep + z, (d ^ 1) * rep + z) for d in range(dp) for z in range(rep)]
    products = (
        lambda mine, core_info: weight_call(core_info, state["act"], grads["bg"], mine),
        lambda mine, core_info: weight_call(core_info, state["low"], grads["ug"], mine),
        lambda mine, core_info: last_weight_call(
            core_info, state["xs"], grads["qg"], state["mix"], grads["ag"], mine
        ),
    )
    widths = [(width,), (hidden,), (3 * width, width)]
    if dp == 4:
        rings, last = [], vector

        def advance(last):
            for ring in rings:
                if not ring.done():
                    ring.advance(last)
                    last = ring.moving
                elif not ring.finished:
                    last = ring.finish(last)
            return last

        for product, cut in zip(products, widths):
            theirs = product(False, tied(core_info, last))
            last = advance(theirs)
            other = lax.ppermute(theirs, AXES, swap)
            own = product(True, tied(core_info, last))
            last = advance(own)
            rings.append(RingSum(own, other, core, place, plan, swap, cut))
            last = rings[-1].moving
        sums = list(rings)
        for call in late_calls:
            pooled, _, _ = forward("pass", call, None, {}, [], (query_lengths, tied(key_lengths, last)))
            last = advance(pooled)
        small = jnp.concatenate([vector, pool(0), pool(1)])
        gather = RingGather(small, (vector.shape[0], crops, crops), core, place, rep, plan, swap)
        rings.insert(0, gather)
        while not all(ring.finished for ring in rings):
            last = advance(last)
        totals = [out for ring in sums for out in ring.outs]
        vector, pooled_query, pooled_key = gather.outs
    else:
        totals = []
        for product in products:
            theirs, own = product(False, core_info), product(True, core_info)
            both = jnp.where(core == 0, jnp.stack([own, theirs]), jnp.stack([theirs, own]))
            totals.append(lax.psum(both.reshape(-1, own.shape[-1]), AXES).astype(F32))
        totals += [totals[2][:, 3 * width :]]
        totals[2] = totals[2][:, : 3 * width]
        for call in late_calls:
            forward("pass", call, None, {}, [])
        vector = lax.psum(vector, AXES)
        pooled_query = lax.all_gather(pool(0), AXES, axis=0, tiled=True)
        pooled_key = lax.all_gather(pool(1), AXES, axis=0, tiled=True)
    ratio = hidden // width
    return (
        pooled_query[None],
        pooled_key[None],
        grads["ig"][None],
        totals[2][None],
        totals[3][None],
        totals[1][None],
        totals[0][None],
        vector[:ratio].reshape(1, hidden),
        vector[None, ratio : ratio + 6],
        vector[None, ratio + 6 : ratio + 8],
    )


def solution(mesh):
    placed = (
        P(("dp", "rep"), None, None),
        P(("dp", "rep"), None, None),
        P(("dp", "rep")),
        P(("dp", "rep")),
        P(("dp", "rep"), None, None),
        P("section", None, None, None),
        P("section", None, None, None),
        P("section", None, None, None),
        P("section", None, None, None),
        P("section", None, None),
        P("section", None, None, None),
        P("section", None, None, None),
    )
    return jax.shard_map(
        on_device,
        mesh=mesh,
        in_specs=placed,
        out_specs=(
            P("section", None, None),
            P("section", None, None),
            P("section", ("dp", "rep"), None, None),
            P("section", None, None),
            P("section", None, None),
            P("section", None, None),
            P("section", None, None),
            P("section", None),
            P("section", None, None),
            P("section", None, None),
        ),
        check_vma=False,
    )
```

```python
import functools
import math

import jax
import jax.numpy as jnp
from jax import lax
from jax.experimental import pallas as pl
from jax.experimental.pallas import tpu as pltpu
from jax.sharding import PartitionSpec as P

HEAD = 64
EPS = 1e-06
NEG = -1000000000.0
HELD_CROPS = 3
HELD_LIMIT = 10 * 1024 * 1024
PASS_LIMIT = 22 * 1024 * 1024
WEIGHTS_LIMIT = 50 * 1024 * 1024
NT = (((1,), (1,)), ((), ()))
TN = (((0,), (0,)), ((), ()))
F32 = jnp.float32
BF16 = jnp.bfloat16
ANY = pl.BlockSpec(memory_space=pl.ANY)
SMEM = pl.BlockSpec(memory_space=pltpu.SMEM)


def mm(left, right, dims=(((1,), (0,)), ((), ()))):
    return lax.dot_general(left, right, dims, preferred_element_type=F32)


def row_variants(crop_len):
    return [crop_len]


def gelu_pair(values):
    cdf = 0.5 + 0.5 * lax.erf(values * (2.0**-0.5))
    density = jnp.exp(-0.5 * values * values) * (2.0 * math.pi) ** -0.5
    return values * cdf, cdf + values * density


def norm_forward(hidden):
    centred = hidden - jnp.mean(hidden, -1, keepdims=True)
    inverse = lax.rsqrt(jnp.mean(centred * centred, -1, keepdims=True) + EPS)
    return centred * inverse, inverse


def norm_backward(scaled, normed, inverse):
    return (
        scaled
        - jnp.mean(scaled, -1, keepdims=True)
        - normed * jnp.mean(scaled * normed, -1, keepdims=True)
    ) * inverse


def dispatch(length, crop_len, body):
    lower = 0
    for rows in row_variants(crop_len):
        pl.when((length > lower) & (length <= rows))(functools.partial(body, rows))
        lower = rows


VMEM_NAMES = ("qkv", "n1", "gp", "n2", "inv")
HBM_NAMES = ("att", "xs", "mix", "low", "act")


def save_shapes(crops, crop_len, width, hidden):
    heads = width // HEAD
    held = min(HELD_CROPS, crops)
    return {
        "qkv": ((held, crop_len, 3 * width), BF16),
        "att": ((crops + 1, heads, crop_len, crop_len), BF16),
        "n1": ((held, crop_len, width), BF16),
        "gp": ((held, crop_len, hidden), BF16),
        "n2": ((held, crop_len, width), BF16),
        "inv": ((held, crop_len, 128), F32),
        "xs": ((crops + 1, crop_len, width), BF16),
        "mix": ((crops + 1, crop_len, width), BF16),
        "low": ((crops + 1, crop_len, width), BF16),
        "act": ((crops + 1, crop_len, hidden), BF16),
    }


VMEM = pl.BlockSpec(memory_space=pltpu.VMEM)


def in_hbm(*values):
    return [pltpu.with_memory_space_constraint(value, pltpu.HBM) for value in values]


def in_vmem(*values):
    return [pltpu.with_memory_space_constraint(value, pltpu.VMEM) for value in values]


def each_lagged(count, first, second, third):
    ahead, waiting = first(0), None
    for number in range(count):
        current, ahead = ahead, first(number + 1) if number + 1 < count else None
        if waiting is not None:
            third(*waiting)
        waiting = (number, second(number, current))
    third(*waiting)


def assigned(crops, query_lengths, key_lengths):
    section = lax.axis_index("section")
    member = jnp.where(section == 0, crops[0][0], crops[1][0])
    crop = jnp.where(section == 0, crops[0][1], crops[1][1])
    live = crop >= 0
    crop = jnp.maximum(crop, 0)
    return section, live, member, crop, jnp.where(member == 0, query_lengths[crop], key_lengths[crop])


def head_masks():
    lane = lax.broadcasted_iota(jnp.int32, (1, 2 * HEAD), 1)
    return lane < HEAD, lane >= HEAD


def forward_kernel(mode, crops, first, n_alias, query_lengths, key_lengths, own, *refs):
    refs = list(refs)
    take = lambda count: [refs.pop(0) for _ in range(count)]
    recv = None if first else take(1)[0]
    weights = take(4)
    bup, biases, gains = take(3)
    take(n_alias)
    y_ref, pool_ref = take(2)
    save = mode != "pass"
    kept = dict(zip(VMEM_NAMES + HBM_NAMES, take(10))) if save else {}
    if mode == "held":
        held = weights
    else:
        held = take(4)
    if not save:
        kept["qkv"] = take(1)[0]
    batt = take(1)[0] if save else None
    bx, bmix, blow, bact, wsem, xsem, osem = refs
    wqkv, wout, wup, wdown = held
    crop_len, width = bx.shape
    hidden = bact.shape[1]
    heads = width // HEAD
    base = hidden // width
    section, live, member, crop, length = assigned(crops, query_lengths, key_lengths)
    which = member if save else 0
    place = jnp.where(member == 0, lax.rem(crop, HELD_CROPS), 1) if save else 0

    loaded = crops[0][0]

    def weight_copy(number):
        target = held[number].at[loaded if save else 0]
        return pltpu.make_async_copy(weights[number].at[0, loaded if save else 1], target, wsem.at[number])

    def weight_ready(number):
        if mode != "held":
            weight_copy(number).wait()

    def bias(row):
        return biases[0, member, row : row + 1, :]

    def gain(row):
        return gains[0, member, row : row + 1, :]

    def rise_bias(cols):
        return jnp.where(member == 0, bup[0, 0:1, cols], bup[0, 1:2, cols])

    def body(rows):
        keys = -(-rows // 128) * 128
        qkv = kept["qkv"]
        started = []

        def clear(ref, *index):
            if rows < crop_len:
                ref[(*index, slice(rows, crop_len))] = jnp.zeros((crop_len - rows, ref.shape[-1]), ref.dtype)

        def finish(number, name, buffer):
            if name != "att":
                clear(buffer)
            if save:
                slot = jnp.where(member == 0, crop, kept[name].shape[0] - 1)
                copy = pltpu.make_async_copy(buffer, kept[name].at[slot], osem.at[number])
                copy.start()
                started.append(copy)

        x = bx[:rows, :]
        finish(0, "xs", bx)
        weight_ready(0)
        for segment in range(3):
            cols = slice(segment * width, (segment + 1) * width)
            part = mm(x, wqkv[which, :, cols])
            if segment != 1:
                part = part + bias(segment // 2)
            qkv[place, :rows, cols] = part.astype(BF16)
        clear(qkv, place)
        masks = head_masks()
        key_valid = lax.broadcasted_iota(jnp.int32, (1, keys), 1) < length
        mixed = [None]

        def pair(part, head, row_count):
            start = part * width + head // 2 * 2 * HEAD
            return qkv[place, :row_count, start : start + 2 * HEAD]

        def score(head):
            return mm(pair(0, head, rows), jnp.where(masks[head % 2], pair(1, head, keys), 0), NT)

        def soften(head, scores):
            scores = jnp.where(key_valid, scores * HEAD**-0.5, NEG)
            weight = jnp.exp(scores - jnp.max(scores, -1, keepdims=True))
            weight = (weight * (1.0 / jnp.sum(weight, -1, keepdims=True))).astype(BF16)
            if save:
                batt[head, :rows, :keys] = weight
            return weight

        def mix(head, weight):
            part = mm(weight, jnp.where(masks[head % 2], pair(2, head, keys), 0))
            if head % 2 == 0:
                mixed[0] = part
            else:
                start = head // 2 * 2 * HEAD
                bmix[:rows, start : start + 2 * HEAD] = (mixed[0] + part).astype(BF16)

        each_lagged(heads, score, soften, mix)
        if save:
            finish(4, "att", batt)
        finish(1, "mix", bmix)
        weight_ready(1)
        attended = mm(bmix[:rows, :], wout[which]) + bias(2)
        n1, inv1 = norm_forward(x.astype(F32) + attended)
        after = n1 * gain(0) + bias(3)
        low = after.astype(BF16)
        blow[:rows, :] = low
        finish(2, "low", blow)
        weight_ready(2)
        weight_ready(3)
        branch = [after + bias(4)]

        def cols(part):
            return slice(part * width, (part + 1) * width)

        def rise(part):
            return mm(low, wup[which, :, cols(part)]) + rise_bias(cols(part))

        def activate(part, pre):
            act, slope = gelu_pair(pre)
            act = act.astype(BF16)
            bact[:rows, cols(part)] = act
            if save:
                kept["gp"][place, :rows, cols(part)] = slope.astype(BF16)
            return act

        def fall(part, act):
            branch[0] = branch[0] + mm(act, wdown[which, cols(part), :])

        each_lagged(base, rise, activate, fall)
        finish(3, "act", bact)
        n2, inv2 = norm_forward(branch[0])
        out = n2 * gain(1) + bias(5)
        y_ref[:rows, :] = out.astype(BF16)
        clear(y_ref)
        valid = lax.broadcasted_iota(jnp.int32, (rows, 1), 0) < length
        total = jnp.sum(jnp.where(valid, out, 0.0), 0, keepdims=True)
        pool_ref[...] = total / length.astype(F32)
        if save:
            kept["n1"][place, :rows, :] = n1.astype(BF16)
            kept["n2"][place, :rows, :] = n2.astype(BF16)
            wide = lax.broadcasted_iota(jnp.int32, (1, 128), 1)
            kept["inv"][place, :rows, :] = jnp.where(wide == 0, inv1, inv2)
        for copy in started:
            copy.wait()

    @pl.when(live)
    def _():
        @pl.when(section == 0)
        def _():
            copy = pltpu.make_async_copy(own.at[crop], bx, xsem)
            copy.start()

        if mode != "held":
            for number in range(4):
                weight_copy(number).start()

        @pl.when(section == 0)
        def _():
            pltpu.make_async_copy(own.at[crop], bx, xsem).wait()

        if recv is not None:

            @pl.when(section != 0)
            def _():
                bx[...] = recv[...]

        dispatch(length, crop_len, body)

    if mode == "load":

        @pl.when(jnp.logical_not(live))
        def _():
            for number in range(4):
                weight_copy(number).start()
            for number in range(4):
                weight_copy(number).wait()


def forward_call(mode, lengths, crops, own, recv, weights, held, state, order=()):
    crop_count, crop_len, width = own.shape
    hidden = weights[2].shape[-1]
    shapes = save_shapes(crop_count, crop_len, width, hidden)
    names = VMEM_NAMES + HBM_NAMES if mode != "pass" else ()
    pinned = lambda name, value: (in_vmem if name in VMEM_NAMES else in_hbm)(value)[0]
    aliased = [pinned(name, state[name]) for name in names] if state else []
    order = list(order)
    arrived = [] if recv is None else [recv]
    read = in_vmem(*held) if mode == "held" else in_hbm(*weights[:4])
    grown = in_vmem(*held) if mode == "load" and held else []
    operands = [*lengths, *in_hbm(own), *arrived, *read, *weights[4:], *order, *aliased, *grown]
    first = 10 + len(arrived) + len(order)
    shape_of = lambda name: (pltpu.VMEM if name in VMEM_NAMES else pltpu.HBM)(*shapes[name])
    spec_of = lambda name: VMEM if name in VMEM_NAMES else ANY
    copies = 1 if mode == "pass" else 2
    weight_shapes = [pltpu.VMEM((copies, *weight.shape[2:]), BF16) for weight in weights[:4]]
    outs = pl.pallas_call(
        functools.partial(forward_kernel, mode, crops, recv is None, len(order) + len(aliased) + len(grown)),
        out_shape=[
            jax.ShapeDtypeStruct((crop_len, width), BF16),
            jax.ShapeDtypeStruct((1, width), F32),
        ]
        + [shape_of(name) for name in names]
        + (weight_shapes if mode == "load" else []),
        in_specs=[SMEM, SMEM, ANY]
        + [VMEM] * len(arrived)
        + [VMEM if mode == "held" else ANY] * 4
        + [VMEM] * 3
        + [ANY] * len(order)
        + [spec_of(name) for name in names][: len(aliased)]
        + [VMEM] * len(grown),
        out_specs=[VMEM, VMEM] + [spec_of(name) for name in names] + ([VMEM] * 4 if mode == "load" else []),
        input_output_aliases={first + i: 2 + i for i in range(len(aliased) + len(grown))},
        scratch_shapes=(weight_shapes if mode == "pass" else [])
        + [
            pltpu.VMEM((1, crop_len, 3 * width), BF16)
            if mode == "pass"
            else pltpu.VMEM((width // HEAD, crop_len, crop_len), BF16)
        ]
        + [
            pltpu.VMEM((crop_len, width), BF16),
            pltpu.VMEM((crop_len, width), BF16),
            pltpu.VMEM((crop_len, width), BF16),
            pltpu.VMEM((crop_len, hidden), BF16),
            pltpu.SemaphoreType.DMA((4,)),
            pltpu.SemaphoreType.DMA,
            pltpu.SemaphoreType.DMA((5,)),
        ],
        compiler_params=pltpu.CompilerParams(vmem_limit_bytes=PASS_LIMIT if mode == "pass" else HELD_LIMIT),
        cost_estimate=crop_cost(weights, crop_len),
        name="forward_crop",
    )(*operands)
    return outs[0], outs[1], outs[2 + len(names) :], dict(zip(names, outs[2:]))


def crop_cost(weights, crop_len):
    size = sum(weight[0, 0].size for weight in weights[:4])
    return pl.CostEstimate(flops=2 * crop_len * size, bytes_accessed=8_000_000, transcendentals=0)


def backward_kernel(crops, first, n_alias, lengths, cot, *refs):
    refs = list(refs)
    take = lambda count: [refs.pop(0) for _ in range(count)]
    recv = None if first else take(1)[0]
    wqkv, wout, wup, wdown, gains = take(5)
    kept = dict(zip(VMEM_NAMES, take(len(VMEM_NAMES))))
    att = take(1)[0]
    take(n_alias)
    dx_ref, vec_ref, ig_ref, bg_ref, ug_ref, ag_ref, qg_ref = take(7)
    batt, bgin, bbg, bug, bag, bqg, bmg, bxg, asem, gsem, osem = refs
    crop_len, width = bbg.shape
    hidden = bug.shape[1]
    heads = width // HEAD
    base = hidden // width
    section, live, _, crop, length = assigned([(0, crop) for crop in crops], lengths, lengths)
    place = lax.rem(crop, HELD_CROPS)

    def gain(row):
        return gains[0, 0, row : row + 1, :]

    def att_copy():
        return pltpu.make_async_copy(att.at[crop], batt, asem)

    def body(rows):
        keys = -(-rows // 128) * 128
        started = []

        def clear(buffer):
            if rows < crop_len:
                buffer[rows:, :] = jnp.zeros((crop_len - rows, buffer.shape[1]), buffer.dtype)

        def finish(number, buffer, target):
            clear(buffer)
            copy = pltpu.make_async_copy(buffer, target, osem.at[number])
            copy.start()
            started.append(copy)

        def column(row, values, start=0):
            vec_ref[row : row + 1, start : start + values.shape[1]] = jnp.sum(values.astype(F32), 0, keepdims=True)

        valid = lax.broadcasted_iota(jnp.int32, (rows, 1), 0) < length
        g = jnp.where(valid, bgin[:rows, :].astype(F32), 0.0)
        n2 = kept["n2"][place, :rows, :].astype(F32)
        inv1 = kept["inv"][place, :rows, 0:1]
        inv2 = kept["inv"][place, :rows, 1:2]
        sum_two = norm_backward(g * gain(1), n2, inv2)
        bg = sum_two.astype(BF16)
        bbg[:rows, :] = bg
        finish(0, bbg, bg_ref.at[crop])
        column(base + 5, g)
        column(base + 7, g * n2)
        column(base + 4, bg)
        side = [sum_two]

        def cols(part):
            return slice(part * width, (part + 1) * width)

        def descend(part):
            return mm(bg, wdown[0, cols(part), :], NT)

        def slope(part, grad):
            grad = (grad * kept["gp"][place, :rows, cols(part)].astype(F32)).astype(BF16)
            bug[:rows, cols(part)] = grad
            column(part, grad)
            return grad

        def ascend(part, grad):
            side[0] = side[0] + mm(grad, wup[0, :, cols(part)], NT)

        each_lagged(base, descend, slope, ascend)
        finish(1, bug, ug_ref.at[crop])
        n1 = kept["n1"][place, :rows, :].astype(F32)
        side = side[0]
        sum_one = norm_backward(side * gain(0), n1, inv1)
        ag = sum_one.astype(BF16)
        bag[:rows, :] = ag
        finish(2, bag, ag_ref.at[crop])
        column(base + 3, side)
        column(base + 6, side * n1)
        column(base + 2, ag)
        bmg[:rows, :] = mm(ag, wout[0], NT).astype(BF16)
        att_copy().wait()
        masks = head_masks()
        scale = HEAD**-0.5
        sums = [None]

        def pair(part, head, row_count):
            start = part * width + head // 2 * 2 * HEAD
            return jnp.where(masks[head % 2], kept["qkv"][place, :row_count, start : start + 2 * HEAD], 0)

        def attention_grad(head):
            start = head // 2 * 2 * HEAD
            return mm(bmg[:rows, start : start + 2 * HEAD], pair(2, head, keys), NT)

        def score_grad(head, grad):
            wide = batt[head, :rows, :keys].astype(F32)
            both = wide * grad
            return (both - wide * jnp.sum(both, -1, keepdims=True)).astype(BF16)

        def spread(head, score):
            start = head // 2 * 2 * HEAD
            mg = jnp.where(masks[head % 2], bmg[:rows, start : start + 2 * HEAD], 0)
            parts = (
                mm(score, pair(1, head, keys)),
                mm(score, pair(0, head, rows), TN),
                mm(batt[head, :rows, :keys], mg, TN),
            )
            if head % 2 == 0:
                sums[0] = parts
                return
            dq, dk, dv = (old + new for old, new in zip(sums[0], parts))
            dq = (dq * scale).astype(BF16)
            dv = dv[:rows].astype(BF16)
            bqg[:rows, start : start + 2 * HEAD] = dq
            bqg[:rows, width + start : width + start + 2 * HEAD] = (dk[:rows] * scale).astype(BF16)
            bqg[:rows, 2 * width + start : 2 * width + start + 2 * HEAD] = dv
            column(base, dq, start)
            column(base + 1, dv, start)

        each_lagged(heads, attention_grad, score_grad, spread)
        finish(3, bqg, qg_ref.at[crop])
        xg = sum_one + mm(bqg[:rows, :], wqkv[0], NT)
        dx = xg.astype(BF16)
        dx_ref[:rows, :] = dx
        clear(dx_ref)
        bxg[:rows, :] = jnp.where(section == 0, xg, dx.astype(F32))
        finish(4, bxg, ig_ref.at[crop])
        for copy in started:
            copy.wait()

    @pl.when(jnp.logical_not(live))
    def _():
        vec_ref[...] = jnp.zeros(vec_ref.shape, F32)

    @pl.when(live)
    def _():
        if recv is not None:

            @pl.when(section == 0)
            def _():
                bgin[...] = recv[...]

        @pl.when(section != 0)
        def _():
            copy = pltpu.make_async_copy(cot.at[crop], bgin, gsem)
            copy.start()
            copy.wait()

        att_copy().start()
        dispatch(length, crop_len, body)


def backward_call(lengths, crops, cot, recv, weights, held, state, grads, order=()):
    crop_count, crop_len, width = cot.shape
    hidden = weights[2].shape[-1]
    shapes = {
        "ig": ((crop_count, crop_len, width), F32),
        "bg": ((crop_count, crop_len, width), BF16),
        "ug": ((crop_count, crop_len, hidden), BF16),
        "ag": ((crop_count, crop_len, width), BF16),
        "qg": ((crop_count, crop_len, 3 * width), BF16),
    }
    names = tuple(shapes)
    aliased = in_hbm(*[grads[name] for name in names]) if grads else []
    arrived = [] if recv is None else [recv]
    operands = [lengths, *in_hbm(cot), *arrived, *in_vmem(*held), weights[6]]
    order = list(order)
    operands += in_vmem(*[state[name] for name in VMEM_NAMES]) + in_hbm(state["att"]) + order + aliased
    first = 8 + len(arrived) + len(VMEM_NAMES) + len(order)
    outs = pl.pallas_call(
        functools.partial(backward_kernel, crops, recv is None, len(order) + len(aliased)),
        out_shape=[
            jax.ShapeDtypeStruct((crop_len, width), BF16),
            jax.ShapeDtypeStruct((hidden // width + 8, width), F32),
        ]
        + [pltpu.HBM(*shapes[name]) for name in names],
        in_specs=[SMEM, ANY] + [VMEM] * (len(arrived) + 5 + len(VMEM_NAMES)) + [ANY] * (1 + len(order) + len(aliased)),
        out_specs=[VMEM, VMEM] + [ANY] * len(names),
        input_output_aliases={first + i: 2 + i for i in range(len(aliased))},
        scratch_shapes=[
            pltpu.VMEM((width // HEAD, crop_len, crop_len), BF16),
            pltpu.VMEM((crop_len, width), BF16),
            pltpu.VMEM((crop_len, width), BF16),
            pltpu.VMEM((crop_len, hidden), BF16),
            pltpu.VMEM((crop_len, width), BF16),
            pltpu.VMEM((crop_len, 3 * width), BF16),
            pltpu.VMEM((crop_len, width), BF16),
            pltpu.VMEM((crop_len, width), F32),
            pltpu.SemaphoreType.DMA,
            pltpu.SemaphoreType.DMA,
            pltpu.SemaphoreType.DMA((5,)),
        ],
        compiler_params=pltpu.CompilerParams(vmem_limit_bytes=HELD_LIMIT),
        cost_estimate=crop_cost(weights, crop_len),
        name="backward_crop",
    )(*operands)
    return outs[0], outs[1], dict(zip(names, outs[2:]))


def ring_place(core, chip, count):
    return jnp.where(core == 0, chip, count - 1 - chip)


def chip_number(dp_index, rep_index, rep):
    return jnp.where(lax.div(dp_index, 2) == 0, rep_index, 2 * rep - 1 - rep_index)


def weights_kernel(groups, *refs):
    pairs = 1 + max(dot[0] for dots in groups for dot in dots)
    lefts, rights = refs[:pairs], refs[pairs : 2 * pairs]
    refs = refs[-(3 * len(groups) + 2 * pairs + 3) :]
    outs, refs = refs[: 2 * len(groups)], refs[2 * len(groups) :]
    held_lefts, held_rights, refs = refs[:pairs], refs[pairs : 2 * pairs], refs[2 * pairs :]
    held_outs, (lsem, rsem, osem) = refs[:-3], refs[-3:]
    count = lax.axis_size("rep") * 2
    core = lax.rem(lax.axis_index("dp"), 2)
    chip = chip_number(lax.axis_index("dp"), lax.axis_index("rep"), count // 2)
    place = ring_place(core, chip, count)
    tile, width = held_lefts[0].shape[2], held_rights[0].shape[2]

    def slot_of(number, half, part):
        return half * (held_lefts[number].shape[0] // 2) + part

    def left_copy(number, half, part):
        which = jnp.where(half == 0, 1 - core, core)
        start = pl.multiple_of(slot_of(number, which, part) * tile, 128)
        source = lefts[number].at[pl.ds(0, held_lefts[number].shape[1]), pl.ds(start, tile)]
        slot = slot_of(number, half, part)
        return pltpu.make_async_copy(source, held_lefts[number].at[slot], lsem.at[number, slot])

    def right_copy(number, part):
        source = rights[number].at[:, pl.ds(part * width, width)]
        return pltpu.make_async_copy(source, held_rights[number].at[part], rsem.at[number, part])

    def out_copy(group, half, step, target):
        rows = held_outs[group].shape[1] // count
        block = lax.rem(jnp.where(half == 0, count - 1 - place, place) - step + count, count)
        source = held_outs[group].at[half, pl.ds(pl.multiple_of(block * rows, 16), rows)]
        return pltpu.make_async_copy(source, outs[2 * group + target].at[step], osem.at[group, half, step])

    def firsts():
        seen = set()
        for group, dots in enumerate(groups):
            for step, (number, left, right) in enumerate(dots):
                fresh = [key not in seen for key in ((0, number, left), (1, number, right))]
                seen |= {(0, number, left), (1, number, right)}
                yield group, step, number, left, right, fresh

    for half in range(2):
        for _, _, number, left, right, fresh in firsts():
            if fresh[0]:
                left_copy(number, half, left).start()
            if fresh[1] and half == 0:
                right_copy(number, right).start()

    @pl.loop(0, 2)
    def _(half):
        for group, step, number, left, right, fresh in firsts():
            if fresh[0]:
                left_copy(number, half, left).wait()
            if fresh[1]:

                @pl.when(half == 0)
                def _():
                    right_copy(number, right).wait()

            product = mm(held_lefts[number][slot_of(number, half, left)], held_rights[number][right], TN).astype(BF16)
            if held_outs[group].shape[1] == tile:
                held_outs[group][half, :, step * width : (step + 1) * width] = product
            else:
                held_outs[group][half, step * tile : (step + 1) * tile, :] = product
            if step == len(groups[group]) - 1:
                for target in range(2):

                    @pl.when(half == target)
                    def _():
                        for number in range(count):
                            out_copy(group, half, number, target).start()

    for group in range(len(groups)):
        for half in range(2):
            for step in range(count):
                out_copy(group, half, step, half).wait()


def weights_call(pairs, groups, order=()):
    lefts, rights = ([array.reshape(-1, array.shape[-1]) for array in side] for side in zip(*pairs))
    tokens, width = rights[0].shape
    tile = width // 2
    left_parts = [left.shape[1] // tile for left in lefts]
    right_parts = [right.shape[1] // width for right in rights]
    count = lax.axis_size("rep") * 2
    shapes = []
    for dots in groups:
        down = left_parts[dots[0][0]] // 2
        shapes.append((down * tile, len(dots) // down * width))
    blocks = [(count, rows // count, columns) for rows, columns in shapes]
    outs = pl.pallas_call(
        functools.partial(weights_kernel, groups),
        out_shape=[pltpu.HBM(block, BF16) for block in blocks for _ in range(2)],
        in_specs=[ANY] * (2 * len(pairs) + len(order)),
        out_specs=[ANY] * (2 * len(groups)),
        scratch_shapes=[pltpu.VMEM((parts, tokens, tile), BF16) for parts in left_parts]
        + [pltpu.VMEM((parts, tokens, width), BF16) for parts in right_parts]
        + [pltpu.VMEM((2, *shape), BF16) for shape in shapes]
        + [
            pltpu.SemaphoreType.DMA((len(pairs), max(left_parts))),
            pltpu.SemaphoreType.DMA((len(pairs), max(right_parts))),
            pltpu.SemaphoreType.DMA((len(groups), 2, count)),
        ],
        compiler_params=pltpu.CompilerParams(vmem_limit_bytes=WEIGHTS_LIMIT),
        cost_estimate=pl.CostEstimate(
            flops=4 * tokens * sum(rows * columns for rows, columns in shapes), bytes_accessed=40_000_000, transcendentals=0
        ),
        name="weight_gradients",
    )(*in_hbm(*lefts, *rights), *order)
    return [(outs[2 * number], outs[2 * number + 1]) for number in range(len(groups))]


def write_kernel(mine, outs_count, *refs):
    value, refs = refs[0], refs[1 if mine else 1 + outs_count :]
    outs, wide, osem = refs[:-2], refs[-2], refs[-1]
    small = outs[-1] if outs[-1].dtype == BF16 else None
    targets = outs if small is None else outs[:-1]
    count, rows, _ = wide.shape
    core = lax.rem(lax.axis_index("dp"), 2)
    whose = core if mine else 1 - core
    copies = []
    for block in range(count):
        wide[block] = value[block, :rows, :].astype(F32)
        row = pl.multiple_of((whose * count + block) * rows, 16)
        start = 0
        for target in targets:
            part = wide.at[block, :, pl.ds(start, target.shape[1])]
            copies.append(pltpu.make_async_copy(part, target.at[pl.ds(row, rows)], osem.at[len(copies)]))
            copies[-1].start()
            start += target.shape[1]
        if small is not None:
            origin = ring_place(whose, (block - 1) % count, count)
            part = value.at[block, pl.ds(rows, value.shape[1] - rows)]
            copies.append(pltpu.make_async_copy(part, small.at[whose, origin], osem.at[len(copies)]))
            copies[-1].start()
    for copy in copies:
        copy.wait()


def write_call(mine, value, rows, widths, outs):
    count, all_rows, columns = value.shape
    shapes = [pltpu.HBM((2 * count * rows, width), F32) for width in widths]
    if all_rows > rows:
        shapes.append(pltpu.HBM((2, count, all_rows - rows, columns), BF16))
    return pl.pallas_call(
        functools.partial(write_kernel, mine, len(shapes)),
        out_shape=shapes,
        in_specs=[VMEM] + [ANY] * len(outs),
        out_specs=[ANY] * len(shapes),
        input_output_aliases={1 + n: n for n in range(len(outs))},
        scratch_shapes=[pltpu.VMEM((count, rows, columns), F32), pltpu.SemaphoreType.DMA((3 * count,))],
        compiler_params=pltpu.CompilerParams(vmem_limit_bytes=PASS_LIMIT),
        cost_estimate=pl.CostEstimate(flops=0, bytes_accessed=6 * value.size, transcendentals=0),
        name="write_half",
    )(value, *in_hbm(*outs))


def small_kernel(rep, crops, every, b_up, biases, gains, pooled_query, pooled_key):
    count = every.shape[1]
    fixed = b_up.shape[1] // every.shape[3] + 8
    total = None
    for core in range(2):
        for chip in range(count):
            rows = every[core, chip].astype(F32)
            total = rows[:fixed] if total is None else total + rows[:fixed]
            y, z = (0, chip) if chip < rep else (1, 2 * rep - 1 - chip)
            first = ((2 * y + core) * rep + z) * crops
            pooled_query[first : first + crops, :] = rows[fixed : fixed + crops]
            pooled_key[first : first + crops, :] = rows[fixed + crops : fixed + 2 * crops]
    width = every.shape[3]
    for row in range(fixed - 8):
        b_up[:, row * width : (row + 1) * width] = total[row : row + 1]
    biases[...] = total[fixed - 8 : fixed - 2]
    gains[...] = total[fixed - 2 :]


def small_call(every, hidden, rep, crops):
    width = every.shape[3]
    shapes = [(1, hidden), (6, width), (2, width), (4 * rep * crops, width), (4 * rep * crops, width)]
    return pl.pallas_call(
        functools.partial(small_kernel, rep, crops),
        out_shape=[jax.ShapeDtypeStruct(shape, F32) for shape in shapes],
        in_specs=[VMEM],
        out_specs=[VMEM] * 5,
        name="small_sums",
    )(every)


def ring_plan(dp, rep):
    chips = [(0, z) for z in range(rep)] + [(1, z) for z in reversed(range(rep))]
    count = len(chips)
    pairs = []
    for core in range(2):
        order = chips if core == 0 else chips[::-1]
        index = [(2 * y + core) * rep + z for y, z in order]
        pairs += [(device, index[(place + 1) % count]) for place, device in enumerate(index)]
    return count, pairs


def tied(value, *others):
    return lax.optimization_barrier((value, *others))[0]


class RingSum:
    def __init__(self, own, other, place, plan):
        self.count, self.pairs = plan
        self.own, self.other, self.place = own, other, place
        self.moving = self.block(0).astype(BF16)
        self.step, self.extra, self.half = 0, None, None

    def block(self, step):
        return self.own[step].astype(F32) + self.other[step].astype(F32)

    def done(self):
        return self.step == 2 * self.count - 2

    def advance(self, last):
        self.step += 1
        spread = self.step - self.count + 1
        moving = tied(lax.ppermute(self.moving, AXES, self.pairs), last)
        if spread <= 0:
            moving = moving.astype(F32) + self.block(self.step)
            moving = lax.reduce_precision(moving, 8, 7).astype(BF16)
            if spread == 0 and self.extra is not None:
                moving = jnp.concatenate([moving, self.extra])
            if spread == 0:
                self.half = jnp.zeros((self.count, *moving.shape), BF16)
        self.moving = moving
        if spread >= 0:
            number = jnp.mod(self.place + 1 - spread, self.count)
            self.half = lax.dynamic_update_index_in_dim(self.half, moving, number, 0)
        return moving


AXES = ("dp", "rep")


def on_device(
    query_input,
    key_input,
    query_lengths,
    key_lengths,
    cotangent,
    w_qkv,
    w_out,
    w_up,
    w_down,
    b_up,
    biases,
    gains,
):
    section = lax.axis_index("section")
    dp, rep = lax.axis_size("dp"), lax.axis_size("rep")
    crops, crop_len, width = query_input.shape
    hidden = w_up.shape[-1]
    weights = (w_qkv, w_out, w_up, w_down, b_up, biases, gains)

    core = lax.rem(lax.axis_index("dp"), 2)
    place = ring_place(core, chip_number(lax.axis_index("dp"), lax.axis_index("rep"), rep), 2 * rep)
    if dp == 4:
        plan = ring_plan(dp, rep)
    query_lengths, core, place, section = lax.optimization_barrier((query_lengths, core, place, section))

    def sum_of(vectors):
        return sum(lax.optimization_barrier(tuple(vectors)))

    def up(value):
        return lax.ppermute(value, "section", [(0, 1)])

    def down(value):
        return lax.ppermute(value, "section", [(1, 0)])

    state, grads = {}, {}
    vectors = []

    lengths = (query_lengths, key_lengths)
    idle = (0, -1)
    query = lambda crop: (0, crop) if 0 <= crop < crops else idle
    key = lambda crop: (1, crop) if 0 <= crop < crops else idle
    plan_of_calls = [(query(0), idle), (key(0), idle)]
    for crop in range(1, crops):
        plan_of_calls += [(query(crop), query(crop - 1)), None]
    plan_of_calls += [(key(1), query(crops - 1)), None, (key(2), key(0)), None]
    late_calls = [(key(crop), idle) for crop in range(3, crops)] + [(idle, key(crop)) for crop in range(1, crops)]
    sent_on, pooled_rows = {}, {}

    def forward(mode, call, held, state, order, lengths=lengths):
        sent, pooled, loaded, state = forward_call(
            mode, lengths, call, key_input if call[0][0] else query_input, sent_on.get(call[1]), weights, held, state, order
        )
        for number, done in enumerate(call):
            if done[1] >= 0:
                pooled_rows[number, *done] = pooled
        if call[0][1] >= 0:
            sent_on[call[0]] = up(sent)
        return pooled, loaded or held, state

    def pool(member):
        first, second = (jnp.concatenate([pooled_rows[number, member, crop] for crop in range(crops)]) for number in range(2))
        return jnp.where(section == 0, first, second)

    returned = held = None
    order = []
    backs = 0
    for number, call in enumerate(plan_of_calls):
        if call is not None:
            pooled, held, state = forward("held" if number > 1 else "load", call, held, state, order)
            order = [pooled]
        else:
            assignment = (backs - 1, backs if backs < crops else -1)
            back, vector, grads = backward_call(
                query_lengths, assignment, cotangent, returned, weights, held, state, grads, order
            )
            order = [vector]
            vectors.append(vector)
            returned = down(back)
            backs += 1

    section, core, place, vector = lax.optimization_barrier((section, core, place, sum_of(vectors)))
    swap = [(d * rep + z, (d ^ 1) * rep + z) for d in range(dp) for z in range(rep)]
    if dp == 4:
        count, ratio = 2 * rep, hidden // width
        small = jnp.concatenate([vector, pool(0)]).astype(BF16)
        used_rows = small.shape[0] + crops
        small_rows = -(-used_rows // 16) * 16
        widths = [(width,), (hidden,), (3 * width, width)]
        pairs = [(state["act"], grads["bg"]), (state["low"], grads["ug"]), (state["xs"], grads["qg"]), (state["mix"], grads["ag"])]
        groups = [
            [(0, part, 0) for part in range(ratio)],
            [(1, 0, part) for part in range(ratio)],
            [(2, 0, part) for part in range(3)] + [(3, 0, 0)],
        ]
        halves = weights_call(pairs, groups, [vector])
        waiting = [(own, lax.ppermute(theirs, AXES, swap)) for theirs, own in halves]
        rings, last = [], halves[0][1]

        def advance(last, begun=0):
            for ring in rings:
                if not ring.done():
                    last = ring.advance(last)
            while len(rings) < begun:
                rings.append(RingSum(*waiting[len(rings)], place, plan))
                last = rings[-1].moving
            return last

        last = advance(last, 1)
        for call in late_calls:
            pooled, _, _ = forward("pass", call, None, {}, [last])
            last = advance(pooled, 3)
        rings[0].extra = jnp.pad(
            jnp.concatenate([small, pool(1).astype(BF16)]), ((0, small_rows - used_rows), (0, 0))
        )
        while not all(ring.done() for ring in rings):
            last = advance(last)
        swapped = [lax.ppermute(ring.half, AXES, swap) for ring in rings]
        outs = [write_call(True, ring.half, ring.own.shape[1], cut, []) for ring, cut in zip(rings, widths)]
        outs = [
            write_call(False, other, ring.own.shape[1], cut, out)
            for ring, other, cut, out in zip(rings, swapped, widths, outs)
        ]
        (grad_down, every), grad_up, grad_last = outs
        totals = [grad_down, *grad_up, *grad_last]
        grad_b_up, grad_biases, grad_gains, pooled_query, pooled_key = small_call(every, hidden, rep, crops)
    else:
        totals = []
        for left, right in (("act", "bg"), ("low", "ug"), ("xs", "qg"), ("mix", "ag")):
            left, right = (a.reshape(-1, a.shape[-1]) for a in (state[left][:crops], grads[right]))
            totals.append(lax.psum(mm(left, right, TN), AXES))
        for call in late_calls:
            forward("pass", call, None, {}, [])
        vector = lax.psum(vector, AXES)
        ratio = hidden // width
        grad_b_up = vector[:ratio].reshape(1, hidden)
        grad_biases, grad_gains = vector[ratio : ratio + 6], vector[ratio + 6 :]
        pooled_query = lax.all_gather(pool(0), AXES, axis=0, tiled=True)
        pooled_key = lax.all_gather(pool(1), AXES, axis=0, tiled=True)
    return (
        pooled_query[None],
        pooled_key[None],
        grads["ig"][None],
        totals[2][None],
        totals[3][None],
        totals[1][None],
        totals[0][None],
        grad_b_up,
        grad_biases[None],
        grad_gains[None],
    )


def solution(mesh):
    placed = (
        P(("dp", "rep"), None, None),
        P(("dp", "rep"), None, None),
        P(("dp", "rep")),
        P(("dp", "rep")),
        P(("dp", "rep"), None, None),
        P("section", None, None, None),
        P("section", None, None, None),
        P("section", None, None, None),
        P("section", None, None, None),
        P("section", None, None),
        P("section", None, None, None),
        P("section", None, None, None),
    )
    return jax.shard_map(
        on_device,
        mesh=mesh,
        in_specs=placed,
        out_specs=(
            P("section", None, None),
            P("section", None, None),
            P("section", ("dp", "rep"), None, None),
            P("section", None, None),
            P("section", None, None),
            P("section", None, None),
            P("section", None, None),
            P("section", None),
            P("section", None, None),
            P("section", None, None),
        ),
        check_vma=False,
    )
```

```python
import functools
import math

import jax
import jax.numpy as jnp
from jax import lax
from jax.experimental import pallas as pl
from jax.experimental.pallas import tpu as pltpu
from jax.sharding import PartitionSpec as P

HEAD = 64
EPS = 1e-06
NEG = -1000000000.0
HELD_CROPS = 4
HELD_LIMIT = 12 * 1024 * 1024
PASS_LIMIT = 22 * 1024 * 1024
WEIGHTS_LIMIT = 50 * 1024 * 1024
NT = (((1,), (1,)), ((), ()))
TN = (((0,), (0,)), ((), ()))
F32 = jnp.float32
BF16 = jnp.bfloat16
ANY = pl.BlockSpec(memory_space=pl.ANY)
SMEM = pl.BlockSpec(memory_space=pltpu.SMEM)


def mm(left, right, dims=(((1,), (0,)), ((), ()))):
    return lax.dot_general(left, right, dims, preferred_element_type=F32)


def row_variants(crop_len):
    return [crop_len]


def gelu_pair(values):
    cdf = 0.5 + 0.5 * lax.erf(values * (2.0**-0.5))
    density = jnp.exp(-0.5 * values * values) * (2.0 * math.pi) ** -0.5
    return values * cdf, cdf + values * density


def norm_forward(hidden):
    centred = hidden - jnp.mean(hidden, -1, keepdims=True)
    inverse = lax.rsqrt(jnp.mean(centred * centred, -1, keepdims=True) + EPS)
    return centred * inverse, inverse


def norm_backward(scaled, normed, inverse):
    return (
        scaled
        - jnp.mean(scaled, -1, keepdims=True)
        - normed * jnp.mean(scaled * normed, -1, keepdims=True)
    ) * inverse


def dispatch(length, crop_len, body):
    lower = 0
    for rows in row_variants(crop_len):
        pl.when((length > lower) & (length <= rows))(functools.partial(body, rows))
        lower = rows


VMEM_NAMES = ("n1", "gp", "n2", "inv")
HBM_NAMES = ("qkv", "att", "xs", "mix", "low", "act")


def save_shapes(crops, crop_len, width, hidden):
    heads = width // HEAD
    held = min(HELD_CROPS, crops)
    return {
        "qkv": ((crops + 1, crop_len, 3 * width), BF16),
        "att": ((crops + 1, heads, crop_len, crop_len), BF16),
        "n1": ((held, crop_len, width), BF16),
        "gp": ((held, crop_len, hidden), BF16),
        "n2": ((held, crop_len, width), BF16),
        "inv": ((held, crop_len, 128), F32),
        "xs": ((crops + 1, crop_len, width), BF16),
        "mix": ((crops + 1, crop_len, width), BF16),
        "low": ((crops + 1, crop_len, width), BF16),
        "act": ((crops + 1, crop_len, hidden), BF16),
    }


VMEM = pl.BlockSpec(memory_space=pltpu.VMEM)


def in_hbm(*values):
    return [pltpu.with_memory_space_constraint(value, pltpu.HBM) for value in values]


def in_vmem(*values):
    return [pltpu.with_memory_space_constraint(value, pltpu.VMEM) for value in values]


def each_lagged(count, first, second, third):
    ahead, waiting = first(0), None
    for number in range(count):
        current, ahead = ahead, first(number + 1) if number + 1 < count else None
        if waiting is not None:
            third(*waiting)
        waiting = (number, second(number, current))
    third(*waiting)


def assigned(crops, query_lengths, key_lengths):
    section = lax.axis_index("section")
    member = jnp.where(section == 0, crops[0][0], crops[1][0])
    crop = jnp.where(section == 0, crops[0][1], crops[1][1])
    live = crop >= 0
    crop = jnp.maximum(crop, 0)
    return section, live, member, crop, jnp.where(member == 0, query_lengths[crop], key_lengths[crop])


def head_masks():
    lane = lax.broadcasted_iota(jnp.int32, (1, 2 * HEAD), 1)
    return lane < HEAD, lane >= HEAD


def forward_kernel(mode, crops, first, n_alias, query_lengths, key_lengths, own, *refs):
    refs = list(refs)
    take = lambda count: [refs.pop(0) for _ in range(count)]
    recv = None if first else take(1)[0]
    weights = take(4)
    bup, biases, gains = take(3)
    take(n_alias)
    y_ref, pool_ref = take(2)
    save = mode != "pass"
    kept = dict(zip(VMEM_NAMES + HBM_NAMES, take(10))) if save else {}
    if mode == "held":
        held = weights
    else:
        held = take(4)
    bqkv = take(1)[0]
    batt = take(1)[0] if save else None
    bx, bmix, blow, bact, wsem, xsem, osem = refs
    wqkv, wout, wup, wdown = held
    crop_len, width = bx.shape
    hidden = bact.shape[1]
    heads = width // HEAD
    base = hidden // width
    section, live, member, crop, length = assigned(crops, query_lengths, key_lengths)
    which = member if save else 0
    place = jnp.where(member == 0, lax.rem(crop, HELD_CROPS), 0) if save else 0

    loaded = crops[0][0]

    def weight_copy(number):
        target = held[number].at[loaded if save else 0]
        return pltpu.make_async_copy(weights[number].at[0, loaded if save else 1], target, wsem.at[number])

    def weight_ready(number):
        if mode == "pass":
            weight_copy(number).wait()
        if mode == "load":
            pl.when(member == loaded)(weight_copy(number).wait)

    def bias(row):
        return biases[0, member, row : row + 1, :]

    def gain(row):
        return gains[0, member, row : row + 1, :]

    def rise_bias(cols):
        return jnp.where(member == 0, bup[0, 0:1, cols], bup[0, 1:2, cols])

    def body(rows):
        keys = -(-rows // 128) * 128
        qkv = bqkv
        started = []

        def clear(ref, *index):
            if rows < crop_len:
                ref[(*index, slice(rows, crop_len))] = jnp.zeros((crop_len - rows, ref.shape[-1]), ref.dtype)

        def finish(number, name, buffer):
            if name != "att":
                clear(buffer)
            if save:
                slot = jnp.where(member == 0, crop, kept[name].shape[0] - 1)
                copy = pltpu.make_async_copy(buffer, kept[name].at[slot], osem.at[number])
                copy.start()
                started.append(copy)

        x = bx[:rows, :]
        finish(0, "xs", bx)
        weight_ready(0)
        for segment in range(3):
            cols = slice(segment * width, (segment + 1) * width)
            part = mm(x, wqkv[which, :, cols])
            if segment != 1:
                part = part + bias(segment // 2)
            qkv[:rows, cols] = part.astype(BF16)
        finish(5, "qkv", qkv)
        masks = head_masks()
        key_valid = lax.broadcasted_iota(jnp.int32, (1, keys), 1) < length
        mixed = [None]

        def pair(part, head, row_count):
            start = part * width + head // 2 * 2 * HEAD
            return qkv[:row_count, start : start + 2 * HEAD]

        def score(head):
            return mm(pair(0, head, rows), jnp.where(masks[head % 2], pair(1, head, keys), 0), NT)

        def soften(head, scores):
            scores = jnp.where(key_valid, scores * HEAD**-0.5, NEG)
            weight = jnp.exp(scores - jnp.max(scores, -1, keepdims=True))
            weight = (weight * (1.0 / jnp.sum(weight, -1, keepdims=True))).astype(BF16)
            if save:
                batt[head, :rows, :keys] = weight
            return weight

        def mix(head, weight):
            part = mm(weight, jnp.where(masks[head % 2], pair(2, head, keys), 0))
            if head % 2 == 0:
                mixed[0] = part
            else:
                start = head // 2 * 2 * HEAD
                bmix[:rows, start : start + 2 * HEAD] = (mixed[0] + part).astype(BF16)

        each_lagged(heads, score, soften, mix)
        if save:
            finish(4, "att", batt)
        finish(1, "mix", bmix)
        weight_ready(1)
        attended = mm(bmix[:rows, :], wout[which]) + bias(2)
        n1, inv1 = norm_forward(x.astype(F32) + attended)
        after = n1 * gain(0) + bias(3)
        low = after.astype(BF16)
        blow[:rows, :] = low
        finish(2, "low", blow)
        weight_ready(2)
        weight_ready(3)
        branch = [after + bias(4)]

        def cols(part):
            return slice(part * width, (part + 1) * width)

        def rise(part):
            return mm(low, wup[which, :, cols(part)]) + rise_bias(cols(part))

        def activate(part, pre):
            act, slope = gelu_pair(pre)
            act = act.astype(BF16)
            bact[:rows, cols(part)] = act
            if save:
                kept["gp"][place, :rows, cols(part)] = slope.astype(BF16)
            return act

        def fall(part, act):
            branch[0] = branch[0] + mm(act, wdown[which, cols(part), :])

        each_lagged(base, rise, activate, fall)
        finish(3, "act", bact)
        n2, inv2 = norm_forward(branch[0])
        out = n2 * gain(1) + bias(5)
        y_ref[:rows, :] = out.astype(BF16)
        clear(y_ref)
        valid = lax.broadcasted_iota(jnp.int32, (rows, 1), 0) < length
        total = jnp.sum(jnp.where(valid, out, 0.0), 0, keepdims=True)
        pool_ref[...] = total / length.astype(F32)
        if save:
            kept["n1"][place, :rows, :] = n1.astype(BF16)
            kept["n2"][place, :rows, :] = n2.astype(BF16)
            wide = lax.broadcasted_iota(jnp.int32, (1, 128), 1)
            kept["inv"][place, :rows, :] = jnp.where(wide == 0, inv1, inv2)
        for copy in started:
            copy.wait()

    @pl.when(live)
    def _():
        @pl.when(section == 0)
        def _():
            copy = pltpu.make_async_copy(own.at[crop], bx, xsem)
            copy.start()

        if mode != "held":
            for number in range(4):
                weight_copy(number).start()

        @pl.when(section == 0)
        def _():
            pltpu.make_async_copy(own.at[crop], bx, xsem).wait()

        if recv is not None:

            @pl.when(section != 0)
            def _():
                bx[...] = recv[...]

        dispatch(length, crop_len, body)
        if mode == "load":
            for number in range(4):
                pl.when(member != loaded)(weight_copy(number).wait)

    if mode == "load":

        @pl.when(jnp.logical_not(live))
        def _():
            for number in range(4):
                weight_copy(number).start()
            for number in range(4):
                weight_copy(number).wait()


def forward_call(mode, lengths, crops, own, recv, weights, held, state, order=()):
    crop_count, crop_len, width = own.shape
    hidden = weights[2].shape[-1]
    shapes = save_shapes(crop_count, crop_len, width, hidden)
    names = VMEM_NAMES + HBM_NAMES if mode != "pass" else ()
    pinned = lambda name, value: (in_vmem if name in VMEM_NAMES else in_hbm)(value)[0]
    aliased = [pinned(name, state[name]) for name in names] if state else []
    order = list(order)
    arrived = [] if recv is None else [recv]
    read = in_vmem(*held) if mode == "held" else in_hbm(*weights[:4])
    grown = in_vmem(*held) if mode == "load" and held else []
    operands = [*lengths, *in_hbm(own), *arrived, *read, *weights[4:], *order, *aliased, *grown]
    first = 10 + len(arrived) + len(order)
    shape_of = lambda name: (pltpu.VMEM if name in VMEM_NAMES else pltpu.HBM)(*shapes[name])
    spec_of = lambda name: VMEM if name in VMEM_NAMES else ANY
    copies = 1 if mode == "pass" else 2
    weight_shapes = [pltpu.VMEM((copies, *weight.shape[2:]), BF16) for weight in weights[:4]]
    outs = pl.pallas_call(
        functools.partial(forward_kernel, mode, crops, recv is None, len(order) + len(aliased) + len(grown)),
        out_shape=[
            jax.ShapeDtypeStruct((crop_len, width), BF16),
            jax.ShapeDtypeStruct((1, width), F32),
        ]
        + [shape_of(name) for name in names]
        + (weight_shapes if mode == "load" else []),
        in_specs=[SMEM, SMEM, ANY]
        + [VMEM] * len(arrived)
        + [VMEM if mode == "held" else ANY] * 4
        + [VMEM] * 3
        + [ANY] * len(order)
        + [spec_of(name) for name in names][: len(aliased)]
        + [VMEM] * len(grown),
        out_specs=[VMEM, VMEM] + [spec_of(name) for name in names] + ([VMEM] * 4 if mode == "load" else []),
        input_output_aliases={first + i: 2 + i for i in range(len(aliased) + len(grown))},
        scratch_shapes=(weight_shapes if mode == "pass" else [])
        + [
            pltpu.VMEM((crop_len, 3 * width), BF16),
            *([] if mode == "pass" else [pltpu.VMEM((width // HEAD, crop_len, crop_len), BF16)]),
        ]
        + [
            pltpu.VMEM((crop_len, width), BF16),
            pltpu.VMEM((crop_len, width), BF16),
            pltpu.VMEM((crop_len, width), BF16),
            pltpu.VMEM((crop_len, hidden), BF16),
            pltpu.SemaphoreType.DMA((4,)),
            pltpu.SemaphoreType.DMA,
            pltpu.SemaphoreType.DMA((6,)),
        ],
        compiler_params=pltpu.CompilerParams(vmem_limit_bytes=PASS_LIMIT if mode == "pass" else HELD_LIMIT),
        cost_estimate=crop_cost(weights, crop_len),
        name="forward_crop",
    )(*operands)
    return outs[0], outs[1], outs[2 + len(names) :], dict(zip(names, outs[2:]))


def crop_cost(weights, crop_len):
    size = sum(weight[0, 0].size for weight in weights[:4])
    return pl.CostEstimate(flops=2 * crop_len * size, bytes_accessed=8_000_000, transcendentals=0)


def backward_kernel(crops, first, n_alias, lengths, cot, sent, *refs):
    refs = list(refs)
    take = lambda count: [refs.pop(0) for _ in range(count)]
    recv = None if first else take(1)[0]
    wqkv, wout, wup, wdown, gains = take(5)
    kept = dict(zip(VMEM_NAMES, take(len(VMEM_NAMES))))
    att, qkv = take(2)
    take(n_alias)
    dx_ref, vec_ref, ig_ref, bg_ref, ug_ref, ag_ref, qg_ref = take(7)
    bqkv, batt, bgin, bbg, bug, bag, bqg, bmg, bxg, asem, osem = refs
    crop_len, width = bbg.shape
    hidden = bug.shape[1]
    heads = width // HEAD
    base = hidden // width
    section, live, _, crop, length = assigned([(0, crop) for crop in crops], lengths, lengths)
    place = lax.rem(crop, HELD_CROPS)

    def gain(row):
        return gains[0, 0, row : row + 1, :]

    def att_copy():
        return pltpu.make_async_copy(att.at[crop], batt, asem.at[0])

    def qkv_copy():
        return pltpu.make_async_copy(qkv.at[crop], bqkv, asem.at[1])

    def body(rows):
        keys = -(-rows // 128) * 128
        started = []

        def clear(buffer):
            if rows < crop_len:
                buffer[rows:, :] = jnp.zeros((crop_len - rows, buffer.shape[1]), buffer.dtype)

        def finish(number, buffer, target):
            clear(buffer)
            copy = pltpu.make_async_copy(buffer, target, osem.at[number])
            copy.start()
            started.append(copy)

        def column(row, values, start=0):
            vec_ref[row : row + 1, start : start + values.shape[1]] = jnp.sum(values.astype(F32), 0, keepdims=True)

        valid = lax.broadcasted_iota(jnp.int32, (rows, 1), 0) < length
        g = jnp.where(valid, bgin[:rows, :].astype(F32), 0.0)
        n2 = kept["n2"][place, :rows, :].astype(F32)
        inv1 = kept["inv"][place, :rows, 0:1]
        inv2 = kept["inv"][place, :rows, 1:2]
        sum_two = norm_backward(g * gain(1), n2, inv2)
        bg = sum_two.astype(BF16)
        bbg[:rows, :] = bg
        finish(0, bbg, bg_ref.at[crop])
        column(base + 5, g)
        column(base + 7, g * n2)
        column(base + 4, bg)
        side = [sum_two]

        def cols(part):
            return slice(part * width, (part + 1) * width)

        def descend(part):
            return mm(bg, wdown[0, cols(part), :], NT)

        def slope(part, grad):
            grad = (grad * kept["gp"][place, :rows, cols(part)].astype(F32)).astype(BF16)
            bug[:rows, cols(part)] = grad
            column(part, grad)
            return grad

        def ascend(part, grad):
            side[0] = side[0] + mm(grad, wup[0, :, cols(part)], NT)

        each_lagged(base, descend, slope, ascend)
        finish(1, bug, ug_ref.at[crop])
        n1 = kept["n1"][place, :rows, :].astype(F32)
        side = side[0]
        sum_one = norm_backward(side * gain(0), n1, inv1)
        ag = sum_one.astype(BF16)
        bag[:rows, :] = ag
        finish(2, bag, ag_ref.at[crop])
        column(base + 3, side)
        column(base + 6, side * n1)
        column(base + 2, ag)
        bmg[:rows, :] = mm(ag, wout[0], NT).astype(BF16)
        att_copy().wait()
        qkv_copy().wait()
        masks = head_masks()
        scale = HEAD**-0.5
        sums = [None]

        def pair(part, head, row_count):
            start = part * width + head // 2 * 2 * HEAD
            return jnp.where(masks[head % 2], bqkv[:row_count, start : start + 2 * HEAD], 0)

        def attention_grad(head):
            start = head // 2 * 2 * HEAD
            return mm(bmg[:rows, start : start + 2 * HEAD], pair(2, head, keys), NT)

        def score_grad(head, grad):
            wide = batt[head, :rows, :keys].astype(F32)
            both = wide * grad
            return (both - wide * jnp.sum(both, -1, keepdims=True)).astype(BF16)

        def spread(head, score):
            start = head // 2 * 2 * HEAD
            mg = jnp.where(masks[head % 2], bmg[:rows, start : start + 2 * HEAD], 0)
            parts = (
                mm(score, pair(1, head, keys)),
                mm(score, pair(0, head, rows), TN),
                mm(batt[head, :rows, :keys], mg, TN),
            )
            if head % 2 == 0:
                sums[0] = parts
                return
            dq, dk, dv = (old + new for old, new in zip(sums[0], parts))
            dq = (dq * scale).astype(BF16)
            dv = dv[:rows].astype(BF16)
            bqg[:rows, start : start + 2 * HEAD] = dq
            bqg[:rows, width + start : width + start + 2 * HEAD] = (dk[:rows] * scale).astype(BF16)
            bqg[:rows, 2 * width + start : 2 * width + start + 2 * HEAD] = dv
            column(base, dq, start)
            column(base + 1, dv, start)

        each_lagged(heads, attention_grad, score_grad, spread)
        finish(3, bqg, qg_ref.at[crop])
        xg = sum_one + mm(bqg[:rows, :], wqkv[0], NT)
        dx = xg.astype(BF16)
        dx_ref[:rows, :] = jnp.where(section == 0, sent[:rows, :], dx)
        if rows < crop_len:
            dx_ref[rows:, :] = jnp.where(section == 0, sent[rows:, :], 0)
        bxg[:rows, :] = jnp.where(section == 0, xg, dx.astype(F32))
        finish(4, bxg, ig_ref.at[crop])
        for copy in started:
            copy.wait()

    @pl.when(jnp.logical_not(live))
    def _():
        vec_ref[...] = jnp.zeros(vec_ref.shape, F32)
        dx_ref[...] = sent[...]

    @pl.when(live)
    def _():
        if recv is not None:

            @pl.when(section == 0)
            def _():
                bgin[...] = recv[...]

        @pl.when(section != 0)
        def _():
            bgin[...] = cot[crop]

        att_copy().start()
        qkv_copy().start()
        dispatch(length, crop_len, body)


def backward_call(lengths, crops, cot, sent, recv, weights, held, state, grads, order=()):
    crop_count, crop_len, width = cot.shape
    hidden = weights[2].shape[-1]
    shapes = {
        "ig": ((crop_count, crop_len, width), F32),
        "bg": ((crop_count, crop_len, width), BF16),
        "ug": ((crop_count, crop_len, hidden), BF16),
        "ag": ((crop_count, crop_len, width), BF16),
        "qg": ((crop_count, crop_len, 3 * width), BF16),
    }
    names = tuple(shapes)
    aliased = in_hbm(*[grads[name] for name in names]) if grads else []
    arrived = [] if recv is None else [recv]
    operands = [lengths, *in_vmem(cot), sent, *arrived, *in_vmem(*held), weights[6]]
    order = list(order)
    operands += in_vmem(*[state[name] for name in VMEM_NAMES]) + in_hbm(state["att"], state["qkv"]) + order + aliased
    first = 10 + len(arrived) + len(VMEM_NAMES) + len(order)
    outs = pl.pallas_call(
        functools.partial(backward_kernel, crops, recv is None, len(order) + len(aliased)),
        out_shape=[
            jax.ShapeDtypeStruct((crop_len, width), BF16),
            jax.ShapeDtypeStruct((hidden // width + 8, width), F32),
        ]
        + [pltpu.HBM(*shapes[name]) for name in names],
        in_specs=[SMEM] + [VMEM] * (len(arrived) + 7 + len(VMEM_NAMES)) + [ANY] * (2 + len(order) + len(aliased)),
        out_specs=[VMEM, VMEM] + [ANY] * len(names),
        input_output_aliases={first + i: 2 + i for i in range(len(aliased))},
        scratch_shapes=[
            pltpu.VMEM((crop_len, 3 * width), BF16),
            pltpu.VMEM((width // HEAD, crop_len, crop_len), BF16),
            pltpu.VMEM((crop_len, width), BF16),
            pltpu.VMEM((crop_len, width), BF16),
            pltpu.VMEM((crop_len, hidden), BF16),
            pltpu.VMEM((crop_len, width), BF16),
            pltpu.VMEM((crop_len, 3 * width), BF16),
            pltpu.VMEM((crop_len, width), BF16),
            pltpu.VMEM((crop_len, width), F32),
            pltpu.SemaphoreType.DMA((2,)),
            pltpu.SemaphoreType.DMA((5,)),
        ],
        compiler_params=pltpu.CompilerParams(vmem_limit_bytes=HELD_LIMIT),
        cost_estimate=crop_cost(weights, crop_len),
        name="backward_crop",
    )(*operands)
    return outs[0], outs[1], dict(zip(names, outs[2:]))


def ring_place(core, chip, count):
    return jnp.where(core == 0, chip, count - 1 - chip)


def chip_number(dp_index, rep_index, rep):
    return jnp.where(lax.div(dp_index, 2) == 0, rep_index, 2 * rep - 1 - rep_index)


def weights_kernel(groups, *refs):
    pairs = 1 + max(dot[0] for dots in groups for dot in dots)
    lefts, rights = refs[:pairs], refs[pairs : 2 * pairs]
    refs = refs[-(3 * len(groups) + 2 * pairs + 3) :]
    outs, refs = refs[: 2 * len(groups)], refs[2 * len(groups) :]
    held_lefts, held_rights, refs = refs[:pairs], refs[pairs : 2 * pairs], refs[2 * pairs :]
    held_outs, (lsem, rsem, osem) = refs[:-3], refs[-3:]
    count = lax.axis_size("rep") * 2
    core = lax.rem(lax.axis_index("dp"), 2)
    chip = chip_number(lax.axis_index("dp"), lax.axis_index("rep"), count // 2)
    place = ring_place(core, chip, count)
    tile, width = held_lefts[0].shape[2], held_rights[0].shape[2]

    def slot_of(number, half, part):
        return half * (held_lefts[number].shape[0] // 2) + part

    def left_copy(number, half, part):
        which = jnp.where(half == 0, 1 - core, core)
        start = pl.multiple_of(slot_of(number, which, part) * tile, 128)
        source = lefts[number].at[pl.ds(0, held_lefts[number].shape[1]), pl.ds(start, tile)]
        slot = slot_of(number, half, part)
        return pltpu.make_async_copy(source, held_lefts[number].at[slot], lsem.at[number, slot])

    def right_copy(number, part):
        source = rights[number].at[:, pl.ds(part * width, width)]
        return pltpu.make_async_copy(source, held_rights[number].at[part], rsem.at[number, part])

    def out_copy(group, half, step, target):
        rows = held_outs[group].shape[1] // count
        block = lax.rem(jnp.where(half == 0, count - 1 - place, place) - step + count, count)
        source = held_outs[group].at[half, pl.ds(pl.multiple_of(block * rows, 16), rows)]
        return pltpu.make_async_copy(source, outs[2 * group + target].at[step], osem.at[group, half, step])

    def firsts():
        seen = set()
        for group, dots in enumerate(groups):
            for step, (number, left, right) in enumerate(dots):
                fresh = [key not in seen for key in ((0, number, left), (1, number, right))]
                seen |= {(0, number, left), (1, number, right)}
                yield group, step, number, left, right, fresh

    for half in range(2):
        for _, _, number, left, right, fresh in firsts():
            if fresh[0]:
                left_copy(number, half, left).start()
            if fresh[1] and half == 0:
                right_copy(number, right).start()

    @pl.loop(0, 2)
    def _(half):
        for group, step, number, left, right, fresh in firsts():
            if fresh[0]:
                left_copy(number, half, left).wait()
            if fresh[1]:

                @pl.when(half == 0)
                def _():
                    right_copy(number, right).wait()

            product = mm(held_lefts[number][slot_of(number, half, left)], held_rights[number][right], TN).astype(BF16)
            if held_outs[group].shape[1] == tile:
                held_outs[group][half, :, step * width : (step + 1) * width] = product
            else:
                held_outs[group][half, step * tile : (step + 1) * tile, :] = product
            if step == len(groups[group]) - 1:
                for target in range(2):

                    @pl.when(half == target)
                    def _():
                        for number in range(count):
                            out_copy(group, half, number, target).start()

    for group in range(len(groups)):
        for half in range(2):
            for step in range(count):
                out_copy(group, half, step, half).wait()


def weights_call(pairs, groups, order=()):
    lefts, rights = ([array.reshape(-1, array.shape[-1]) for array in side] for side in zip(*pairs))
    tokens, width = rights[0].shape
    tile = width // 2
    left_parts = [left.shape[1] // tile for left in lefts]
    right_parts = [right.shape[1] // width for right in rights]
    count = lax.axis_size("rep") * 2
    shapes = []
    for dots in groups:
        down = left_parts[dots[0][0]] // 2
        shapes.append((down * tile, len(dots) // down * width))
    blocks = [(count, rows // count, columns) for rows, columns in shapes]
    outs = pl.pallas_call(
        functools.partial(weights_kernel, groups),
        out_shape=[pltpu.HBM(block, BF16) for block in blocks for _ in range(2)],
        in_specs=[ANY] * (2 * len(pairs) + len(order)),
        out_specs=[ANY] * (2 * len(groups)),
        scratch_shapes=[pltpu.VMEM((parts, tokens, tile), BF16) for parts in left_parts]
        + [pltpu.VMEM((parts, tokens, width), BF16) for parts in right_parts]
        + [pltpu.VMEM((2, *shape), BF16) for shape in shapes]
        + [
            pltpu.SemaphoreType.DMA((len(pairs), max(left_parts))),
            pltpu.SemaphoreType.DMA((len(pairs), max(right_parts))),
            pltpu.SemaphoreType.DMA((len(groups), 2, count)),
        ],
        compiler_params=pltpu.CompilerParams(vmem_limit_bytes=WEIGHTS_LIMIT),
        cost_estimate=pl.CostEstimate(
            flops=4 * tokens * sum(rows * columns for rows, columns in shapes), bytes_accessed=40_000_000, transcendentals=0
        ),
        name="weight_gradients",
    )(*in_hbm(*lefts, *rights), *order)
    return [(outs[2 * number], outs[2 * number + 1]) for number in range(len(groups))]


def write_kernel(mine, outs_count, *refs):
    value, refs = refs[0], refs[1 if mine else 1 + outs_count :]
    outs, wide, osem = refs[:-2], refs[-2], refs[-1]
    small = outs[-1] if outs[-1].dtype == BF16 else None
    targets = outs if small is None else outs[:-1]
    count, rows, _ = wide.shape
    core = lax.rem(lax.axis_index("dp"), 2)
    whose = core if mine else 1 - core
    copies = []
    for block in range(count):
        wide[block] = value[block, :rows, :].astype(F32)
        row = pl.multiple_of((whose * count + block) * rows, 16)
        start = 0
        for target in targets:
            part = wide.at[block, :, pl.ds(start, target.shape[1])]
            copies.append(pltpu.make_async_copy(part, target.at[pl.ds(row, rows)], osem.at[len(copies)]))
            copies[-1].start()
            start += target.shape[1]
        if small is not None:
            origin = ring_place(whose, (block - 1) % count, count)
            part = value.at[block, pl.ds(rows, value.shape[1] - rows)]
            copies.append(pltpu.make_async_copy(part, small.at[whose, origin], osem.at[len(copies)]))
            copies[-1].start()
    for copy in copies:
        copy.wait()


def write_call(mine, value, rows, widths, outs):
    count, all_rows, columns = value.shape
    shapes = [pltpu.HBM((2 * count * rows, width), F32) for width in widths]
    if all_rows > rows:
        shapes.append(pltpu.HBM((2, count, all_rows - rows, columns), BF16))
    return pl.pallas_call(
        functools.partial(write_kernel, mine, len(shapes)),
        out_shape=shapes,
        in_specs=[VMEM] + [ANY] * len(outs),
        out_specs=[ANY] * len(shapes),
        input_output_aliases={1 + n: n for n in range(len(outs))},
        scratch_shapes=[pltpu.VMEM((count, rows, columns), F32), pltpu.SemaphoreType.DMA((3 * count,))],
        compiler_params=pltpu.CompilerParams(vmem_limit_bytes=PASS_LIMIT),
        cost_estimate=pl.CostEstimate(flops=0, bytes_accessed=6 * value.size, transcendentals=0),
        name="write_half",
    )(value, *in_hbm(*outs))


def small_kernel(rep, crops, every, b_up, biases, gains, pooled_query, pooled_key):
    count = every.shape[1]
    fixed = b_up.shape[1] // every.shape[3] + 8
    total = None
    for core in range(2):
        for chip in range(count):
            rows = every[core, chip].astype(F32)
            total = rows[:fixed] if total is None else total + rows[:fixed]
            y, z = (0, chip) if chip < rep else (1, 2 * rep - 1 - chip)
            first = ((2 * y + core) * rep + z) * crops
            pooled_query[first : first + crops, :] = rows[fixed : fixed + crops]
            pooled_key[first : first + crops, :] = rows[fixed + crops : fixed + 2 * crops]
    width = every.shape[3]
    for row in range(fixed - 8):
        b_up[:, row * width : (row + 1) * width] = total[row : row + 1]
    biases[...] = total[fixed - 8 : fixed - 2]
    gains[...] = total[fixed - 2 :]


def small_call(every, hidden, rep, crops):
    width = every.shape[3]
    shapes = [(1, hidden), (6, width), (2, width), (4 * rep * crops, width), (4 * rep * crops, width)]
    return pl.pallas_call(
        functools.partial(small_kernel, rep, crops),
        out_shape=[jax.ShapeDtypeStruct(shape, F32) for shape in shapes],
        in_specs=[VMEM],
        out_specs=[VMEM] * 5,
        name="small_sums",
    )(every)


def ring_plan(dp, rep):
    chips = [(0, z) for z in range(rep)] + [(1, z) for z in reversed(range(rep))]
    count = len(chips)
    pairs = []
    for core in range(2):
        order = chips if core == 0 else chips[::-1]
        index = [(2 * y + core) * rep + z for y, z in order]
        pairs += [(device, index[(place + 1) % count]) for place, device in enumerate(index)]
    return count, pairs


def tied(value, *others):
    return lax.optimization_barrier((value, *others))[0]


class RingSum:
    def __init__(self, own, other, place, plan):
        self.count, self.pairs = plan
        self.own, self.other, self.place = own, other, place
        self.moving = self.block(0).astype(BF16)
        self.step, self.extra, self.half = 0, None, None

    def block(self, step):
        return self.own[step].astype(F32) + self.other[step].astype(F32)

    def done(self):
        return self.step == 2 * self.count - 2

    def advance(self, last):
        self.step += 1
        spread = self.step - self.count + 1
        moving = tied(lax.ppermute(self.moving, AXES, self.pairs), last)
        if spread <= 0:
            moving = moving.astype(F32) + self.block(self.step)
            moving = lax.reduce_precision(moving, 8, 7).astype(BF16)
            if spread == 0 and self.extra is not None:
                moving = jnp.concatenate([moving, self.extra])
            if spread == 0:
                self.half = jnp.zeros((self.count, *moving.shape), BF16)
        self.moving = moving
        if spread >= 0:
            number = jnp.mod(self.place + 1 - spread, self.count)
            self.half = lax.dynamic_update_index_in_dim(self.half, moving, number, 0)
        return moving


AXES = ("dp", "rep")


def on_device(
    query_input,
    key_input,
    query_lengths,
    key_lengths,
    cotangent,
    w_qkv,
    w_out,
    w_up,
    w_down,
    b_up,
    biases,
    gains,
):
    section = lax.axis_index("section")
    dp, rep = lax.axis_size("dp"), lax.axis_size("rep")
    crops, crop_len, width = query_input.shape
    hidden = w_up.shape[-1]
    weights = (w_qkv, w_out, w_up, w_down, b_up, biases, gains)

    core = lax.rem(lax.axis_index("dp"), 2)
    place = ring_place(core, chip_number(lax.axis_index("dp"), lax.axis_index("rep"), rep), 2 * rep)
    if dp == 4:
        plan = ring_plan(dp, rep)
    query_lengths, core, place, section = lax.optimization_barrier((query_lengths, core, place, section))

    def sum_of(vectors):
        return sum(lax.optimization_barrier(tuple(vectors)))

    def up(value):
        return lax.ppermute(value, "section", [(0, 1)])

    state, grads = {}, {}
    vectors = []

    lengths = (query_lengths, key_lengths)
    idle = (0, -1)
    query = lambda crop: (0, crop) if 0 <= crop < crops else idle
    key = lambda crop: (1, crop) if 0 <= crop < crops else idle
    plan_of_calls = [(query(0), idle), (query(1), idle)]
    for crop in range(crops):
        ahead = query(crop + 2) if crop + 2 < crops else key(crop + 2 - crops)
        plan_of_calls += [(ahead, query(crop)), None]
    plan_of_calls += [(key(2), key(0)), None]
    late_calls = [(key(crop), idle) for crop in range(3, crops)] + [(idle, key(crop)) for crop in range(1, crops)]
    sent_on, pooled_rows = {}, {}

    def forward(mode, call, held, state, order, later=False):
        sent, pooled, loaded, state = forward_call(
            mode, lengths, call, key_input if call[0][0] else query_input, sent_on.get(call[1]), weights, held, state, order
        )
        for number, done in enumerate(call):
            if done[1] >= 0:
                pooled_rows[number, *done] = pooled
        if call[0][1] >= 0 and not later:
            sent_on[call[0]] = up(sent)
        return sent, pooled, loaded or held, state

    def pool(member):
        first, second = (jnp.concatenate([pooled_rows[number, member, crop] for crop in range(crops)]) for number in range(2))
        return jnp.where(section == 0, first, second)

    returned = held = None
    order = []
    backs, encoders = 0, set()
    for number, call in enumerate(plan_of_calls):
        if call is not None:
            later = 2 <= number < 2 * crops + 2
            mode = "held" if call[0][0] in encoders else "load"
            encoders.add(call[0][0])
            sent, pooled, held, state = forward(mode, call, held, state, order, later)
            order = [pooled]
        else:
            assignment = (backs - 1, backs if backs < crops else -1)
            back, vector, grads = backward_call(
                query_lengths, assignment, cotangent, sent, returned, weights, held, state, grads, order
            )
            order = [vector]
            vectors.append(vector)
            if backs < crops:
                returned = lax.ppermute(back, "section", [(0, 1), (1, 0)])
                sent_on[plan_of_calls[number - 1][0]] = returned
            backs += 1

    section, core, place, vector = lax.optimization_barrier((section, core, place, sum_of(vectors)))
    swap = [(d * rep + z, (d ^ 1) * rep + z) for d in range(dp) for z in range(rep)]
    if dp == 4:
        count, ratio = 2 * rep, hidden // width
        small = jnp.concatenate([vector, pool(0)]).astype(BF16)
        used_rows = small.shape[0] + crops
        small_rows = -(-used_rows // 16) * 16
        widths = [(width,), (hidden,), (3 * width, width)]
        pairs = [(state["act"], grads["bg"]), (state["low"], grads["ug"]), (state["xs"], grads["qg"]), (state["mix"], grads["ag"])]
        groups = [
            [(0, part, 0) for part in range(ratio)],
            [(1, 0, part) for part in range(ratio)],
            [(2, 0, part) for part in range(3)] + [(3, 0, 0)],
        ]
        halves = weights_call(pairs, groups, [vector])
        waiting = [(own, lax.ppermute(theirs, AXES, swap)) for theirs, own in halves]
        rings, last = [], halves[0][1]

        def advance(last, begun=0):
            for ring in rings:
                if not ring.done():
                    last = ring.advance(last)
            while len(rings) < begun:
                rings.append(RingSum(*waiting[len(rings)], place, plan))
                last = rings[-1].moving
            return last

        last = advance(last, 1)
        for call in late_calls:
            _, pooled, _, _ = forward("pass", call, None, {}, [last])
            last = advance(pooled, 3)
        rings[0].extra = jnp.pad(
            jnp.concatenate([small, pool(1).astype(BF16)]), ((0, small_rows - used_rows), (0, 0))
        )
        while not all(ring.done() for ring in rings):
            last = advance(last)
        swapped = [lax.ppermute(ring.half, AXES, swap) for ring in rings]
        outs = [write_call(True, ring.half, ring.own.shape[1], cut, []) for ring, cut in zip(rings, widths)]
        outs = [
            write_call(False, other, ring.own.shape[1], cut, out)
            for ring, other, cut, out in zip(rings, swapped, widths, outs)
        ]
        (grad_down, every), grad_up, grad_last = outs
        totals = [grad_down, *grad_up, *grad_last]
        grad_b_up, grad_biases, grad_gains, pooled_query, pooled_key = small_call(every, hidden, rep, crops)
    else:
        totals = []
        for left, right in (("act", "bg"), ("low", "ug"), ("xs", "qg"), ("mix", "ag")):
            left, right = (a.reshape(-1, a.shape[-1]) for a in (state[left][:crops], grads[right]))
            totals.append(lax.psum(mm(left, right, TN), AXES))
        for call in late_calls:
            forward("pass", call, None, {}, [])
        vector = lax.psum(vector, AXES)
        ratio = hidden // width
        grad_b_up = vector[:ratio].reshape(1, hidden)
        grad_biases, grad_gains = vector[ratio : ratio + 6], vector[ratio + 6 :]
        pooled_query = lax.all_gather(pool(0), AXES, axis=0, tiled=True)
        pooled_key = lax.all_gather(pool(1), AXES, axis=0, tiled=True)
    return (
        pooled_query[None],
        pooled_key[None],
        grads["ig"][None],
        totals[2][None],
        totals[3][None],
        totals[1][None],
        totals[0][None],
        grad_b_up,
        grad_biases[None],
        grad_gains[None],
    )


def solution(mesh):
    placed = (
        P(("dp", "rep"), None, None),
        P(("dp", "rep"), None, None),
        P(("dp", "rep")),
        P(("dp", "rep")),
        P(("dp", "rep"), None, None),
        P("section", None, None, None),
        P("section", None, None, None),
        P("section", None, None, None),
        P("section", None, None, None),
        P("section", None, None),
        P("section", None, None, None),
        P("section", None, None, None),
    )
    return jax.shard_map(
        on_device,
        mesh=mesh,
        in_specs=placed,
        out_specs=(
            P("section", None, None),
            P("section", None, None),
            P("section", ("dp", "rep"), None, None),
            P("section", None, None),
            P("section", None, None),
            P("section", None, None),
            P("section", None, None),
            P("section", None),
            P("section", None, None),
            P("section", None, None),
        ),
        check_vma=False,
    )
```

```python
import functools
import math

import jax
import jax.numpy as jnp
from jax import lax
from jax.experimental import pallas as pl
from jax.experimental.pallas import tpu as pltpu
from jax.sharding import PartitionSpec as P

HEAD = 64
EPS = 1e-06
NEG = -1000000000.0
HELD_CROPS = 4
HELD_LIMIT = 12 * 1024 * 1024
PASS_LIMIT = 22 * 1024 * 1024
WEIGHTS_LIMIT = 50 * 1024 * 1024
NT = (((1,), (1,)), ((), ()))
TN = (((0,), (0,)), ((), ()))
F32 = jnp.float32
BF16 = jnp.bfloat16
ANY = pl.BlockSpec(memory_space=pl.ANY)
SMEM = pl.BlockSpec(memory_space=pltpu.SMEM)


def mm(left, right, dims=(((1,), (0,)), ((), ()))):
    return lax.dot_general(left, right, dims, preferred_element_type=F32)


def row_variants(crop_len):
    return [crop_len]


def gelu_pair(values):
    cdf = 0.5 + 0.5 * lax.erf(values * (2.0**-0.5))
    density = jnp.exp(-0.5 * values * values) * (2.0 * math.pi) ** -0.5
    return values * cdf, cdf + values * density


def norm_forward(hidden):
    centred = hidden - jnp.mean(hidden, -1, keepdims=True)
    inverse = lax.rsqrt(jnp.mean(centred * centred, -1, keepdims=True) + EPS)
    return centred * inverse, inverse


def norm_backward(scaled, normed, inverse):
    return (
        scaled
        - jnp.mean(scaled, -1, keepdims=True)
        - normed * jnp.mean(scaled * normed, -1, keepdims=True)
    ) * inverse


def dispatch(length, crop_len, body):
    lower = 0
    for rows in row_variants(crop_len):
        pl.when((length > lower) & (length <= rows))(functools.partial(body, rows))
        lower = rows


VMEM_NAMES = ("n1", "gp", "n2", "inv")
HBM_NAMES = ("qkv", "att", "xs", "mix", "low", "act")


def save_shapes(crops, crop_len, width, hidden):
    heads = width // HEAD
    held = min(HELD_CROPS, crops)
    return {
        "qkv": ((crops + 1, crop_len, 3 * width), BF16),
        "att": ((crops + 1, heads, crop_len, crop_len), BF16),
        "n1": ((held, crop_len, width), BF16),
        "gp": ((held, crop_len, hidden), BF16),
        "n2": ((held, crop_len, width), BF16),
        "inv": ((held, crop_len, 128), F32),
        "xs": ((crops + 1, crop_len, width), BF16),
        "mix": ((crops + 1, crop_len, width), BF16),
        "low": ((crops + 1, crop_len, width), BF16),
        "act": ((crops + 1, crop_len, hidden), BF16),
    }


VMEM = pl.BlockSpec(memory_space=pltpu.VMEM)


def in_hbm(*values):
    return [pltpu.with_memory_space_constraint(value, pltpu.HBM) for value in values]


def in_vmem(*values):
    return [pltpu.with_memory_space_constraint(value, pltpu.VMEM) for value in values]


def each_lagged(count, first, second, third):
    ahead, waiting = first(0), None
    for number in range(count):
        current, ahead = ahead, first(number + 1) if number + 1 < count else None
        if waiting is not None:
            third(*waiting)
        waiting = (number, second(number, current))
    third(*waiting)


def assigned(crops, query_lengths, key_lengths):
    section = lax.axis_index("section")
    member = jnp.where(section == 0, crops[0][0], crops[1][0])
    crop = jnp.where(section == 0, crops[0][1], crops[1][1])
    live = crop >= 0
    crop = jnp.maximum(crop, 0)
    return section, live, member, crop, jnp.where(member == 0, query_lengths[crop], key_lengths[crop])


def head_masks():
    lane = lax.broadcasted_iota(jnp.int32, (1, 2 * HEAD), 1)
    return lane < HEAD, lane >= HEAD


def forward_kernel(mode, near, crops, first, n_alias, query_lengths, key_lengths, own, *refs):
    refs = list(refs)
    take = lambda count: [refs.pop(0) for _ in range(count)]
    recv = None if first else take(1)[0]
    weights = take(4)
    bup, biases, gains = take(3)
    take(n_alias)
    y_ref, pool_ref = take(2)
    save = mode != "pass"
    kept = dict(zip(VMEM_NAMES + HBM_NAMES, take(10))) if save else {}
    if mode == "held":
        held = weights
    else:
        held = take(4)
    bqkv = take(1)[0]
    batt = take(1)[0] if save else None
    bx, bmix, blow, bact, wsem, xsem, osem = refs
    wqkv, wout, wup, wdown = held
    crop_len, width = bx.shape
    hidden = bact.shape[1]
    heads = width // HEAD
    base = hidden // width
    section, live, member, crop, length = assigned(crops, query_lengths, key_lengths)
    which = member if save else 0
    place = jnp.where(member == 0, lax.rem(crop, HELD_CROPS), 0) if save else 0

    loaded = crops[0][0]

    def weight_copy(number):
        target = held[number].at[loaded if save else 0]
        return pltpu.make_async_copy(weights[number].at[0, loaded if save else 1], target, wsem.at[number])

    def weight_ready(number):
        if mode == "pass":
            weight_copy(number).wait()
        if mode == "load":
            pl.when(member == loaded)(weight_copy(number).wait)

    def bias(row):
        return biases[0, member, row : row + 1, :]

    def gain(row):
        return gains[0, member, row : row + 1, :]

    def rise_bias(cols):
        return jnp.where(member == 0, bup[0, 0:1, cols], bup[0, 1:2, cols])

    def body(rows):
        keys = -(-rows // 128) * 128
        qkv = bqkv
        started = []

        def clear(ref, *index):
            if rows < crop_len:
                ref[(*index, slice(rows, crop_len))] = jnp.zeros((crop_len - rows, ref.shape[-1]), ref.dtype)

        def finish(number, name, buffer):
            if name != "att":
                clear(buffer)
            if save:
                slot = jnp.where(member == 0, crop, kept[name].shape[0] - 1)
                copy = pltpu.make_async_copy(buffer, kept[name].at[slot], osem.at[number])
                copy.start()
                started.append(copy)

        x = bx[:rows, :]
        finish(0, "xs", bx)
        weight_ready(0)
        for segment in range(3):
            cols = slice(segment * width, (segment + 1) * width)
            part = mm(x, wqkv[which, :, cols])
            if segment != 1:
                part = part + bias(segment // 2)
            qkv[:rows, cols] = part.astype(BF16)
        finish(5, "qkv", qkv)
        masks = head_masks()
        key_valid = lax.broadcasted_iota(jnp.int32, (1, keys), 1) < length
        mixed = [None]

        def pair(part, head, row_count):
            start = part * width + head // 2 * 2 * HEAD
            return qkv[:row_count, start : start + 2 * HEAD]

        def score(head):
            return mm(pair(0, head, rows), jnp.where(masks[head % 2], pair(1, head, keys), 0), NT)

        def soften(head, scores):
            scores = jnp.where(key_valid, scores * HEAD**-0.5, NEG)
            weight = jnp.exp(scores - jnp.max(scores, -1, keepdims=True))
            weight = (weight * (1.0 / jnp.sum(weight, -1, keepdims=True))).astype(BF16)
            if save:
                batt[head, :rows, :keys] = weight
            return weight

        def mix(head, weight):
            part = mm(weight, jnp.where(masks[head % 2], pair(2, head, keys), 0))
            if head % 2 == 0:
                mixed[0] = part
            else:
                start = head // 2 * 2 * HEAD
                bmix[:rows, start : start + 2 * HEAD] = (mixed[0] + part).astype(BF16)

        each_lagged(heads, score, soften, mix)
        if save:
            finish(4, "att", batt)
        finish(1, "mix", bmix)
        weight_ready(1)
        attended = mm(bmix[:rows, :], wout[which]) + bias(2)
        n1, inv1 = norm_forward(x.astype(F32) + attended)
        after = n1 * gain(0) + bias(3)
        low = after.astype(BF16)
        blow[:rows, :] = low
        finish(2, "low", blow)
        weight_ready(2)
        weight_ready(3)
        branch = [after + bias(4)]

        def cols(part):
            return slice(part * width, (part + 1) * width)

        def rise(part):
            return mm(low, wup[which, :, cols(part)]) + rise_bias(cols(part))

        def activate(part, pre):
            act, slope = gelu_pair(pre)
            act = act.astype(BF16)
            bact[:rows, cols(part)] = act
            if save:
                kept["gp"][place, :rows, cols(part)] = slope.astype(BF16)
            return act

        def fall(part, act):
            branch[0] = branch[0] + mm(act, wdown[which, cols(part), :])

        each_lagged(base, rise, activate, fall)
        finish(3, "act", bact)
        n2, inv2 = norm_forward(branch[0])
        out = n2 * gain(1) + bias(5)
        y_ref[:rows, :] = out.astype(BF16)
        clear(y_ref)
        valid = lax.broadcasted_iota(jnp.int32, (rows, 1), 0) < length
        total = jnp.sum(jnp.where(valid, out, 0.0), 0, keepdims=True)
        pool_ref[...] = total / length.astype(F32)
        if save:
            kept["n1"][place, :rows, :] = n1.astype(BF16)
            kept["n2"][place, :rows, :] = n2.astype(BF16)
            wide = lax.broadcasted_iota(jnp.int32, (1, 128), 1)
            kept["inv"][place, :rows, :] = jnp.where(wide == 0, inv1, inv2)
        for copy in started:
            copy.wait()

    @pl.when(live)
    def _():
        @pl.when(section == 0)
        def _():
            if near:
                bx[...] = own[crop]
            else:
                pltpu.make_async_copy(own.at[crop], bx, xsem).start()

        if mode != "held":
            for number in range(4):
                weight_copy(number).start()

        if not near:

            @pl.when(section == 0)
            def _():
                pltpu.make_async_copy(own.at[crop], bx, xsem).wait()

        if recv is not None:

            @pl.when(section != 0)
            def _():
                bx[...] = recv[...]

        dispatch(length, crop_len, body)
        if mode == "load":
            for number in range(4):
                pl.when(member != loaded)(weight_copy(number).wait)

    if mode == "load":

        @pl.when(jnp.logical_not(live))
        def _():
            for number in range(4):
                weight_copy(number).start()
            for number in range(4):
                weight_copy(number).wait()


def forward_call(mode, lengths, crops, own, recv, weights, held, state, order=()):
    crop_count, crop_len, width = own.shape
    hidden = weights[2].shape[-1]
    shapes = save_shapes(crop_count, crop_len, width, hidden)
    names = VMEM_NAMES + HBM_NAMES if mode != "pass" else ()
    pinned = lambda name, value: (in_vmem if name in VMEM_NAMES else in_hbm)(value)[0]
    aliased = [pinned(name, state[name]) for name in names] if state else []
    order = list(order)
    arrived = [] if recv is None else [recv]
    read = in_vmem(*held) if mode == "held" else in_hbm(*weights[:4])
    grown = in_vmem(*held) if mode == "load" and held else []
    near = mode == "held" and crops[0][0] == 0
    operands = [*lengths, *(in_vmem if near else in_hbm)(own), *arrived, *read, *weights[4:], *order, *aliased, *grown]
    first = 10 + len(arrived) + len(order)
    shape_of = lambda name: (pltpu.VMEM if name in VMEM_NAMES else pltpu.HBM)(*shapes[name])
    spec_of = lambda name: VMEM if name in VMEM_NAMES else ANY
    copies = 1 if mode == "pass" else 2
    weight_shapes = [pltpu.VMEM((copies, *weight.shape[2:]), BF16) for weight in weights[:4]]
    outs = pl.pallas_call(
        functools.partial(forward_kernel, mode, near, crops, recv is None, len(order) + len(aliased) + len(grown)),
        out_shape=[
            jax.ShapeDtypeStruct((crop_len, width), BF16),
            jax.ShapeDtypeStruct((1, width), F32),
        ]
        + [shape_of(name) for name in names]
        + (weight_shapes if mode == "load" else []),
        in_specs=[SMEM, SMEM, VMEM if near else ANY]
        + [VMEM] * len(arrived)
        + [VMEM if mode == "held" else ANY] * 4
        + [VMEM] * 3
        + [ANY] * len(order)
        + [spec_of(name) for name in names][: len(aliased)]
        + [VMEM] * len(grown),
        out_specs=[VMEM, VMEM] + [spec_of(name) for name in names] + ([VMEM] * 4 if mode == "load" else []),
        input_output_aliases={first + i: 2 + i for i in range(len(aliased) + len(grown))},
        scratch_shapes=(weight_shapes if mode == "pass" else [])
        + [
            pltpu.VMEM((crop_len, 3 * width), BF16),
            *([] if mode == "pass" else [pltpu.VMEM((width // HEAD, crop_len, crop_len), BF16)]),
        ]
        + [
            pltpu.VMEM((crop_len, width), BF16),
            pltpu.VMEM((crop_len, width), BF16),
            pltpu.VMEM((crop_len, width), BF16),
            pltpu.VMEM((crop_len, hidden), BF16),
            pltpu.SemaphoreType.DMA((4,)),
            pltpu.SemaphoreType.DMA,
            pltpu.SemaphoreType.DMA((6,)),
        ],
        compiler_params=pltpu.CompilerParams(vmem_limit_bytes=PASS_LIMIT if mode == "pass" else HELD_LIMIT),
        cost_estimate=crop_cost(weights, crop_len),
        name="forward_crop",
    )(*operands)
    return outs[0], outs[1], outs[2 + len(names) :], dict(zip(names, outs[2:]))


def crop_cost(weights, crop_len):
    size = sum(weight[0, 0].size for weight in weights[:4])
    return pl.CostEstimate(flops=2 * crop_len * size, bytes_accessed=8_000_000, transcendentals=0)


def backward_kernel(crops, first, n_alias, lengths, cot, sent, *refs):
    refs = list(refs)
    take = lambda count: [refs.pop(0) for _ in range(count)]
    recv = None if first else take(1)[0]
    wqkv, wout, wup, wdown, gains = take(5)
    kept = dict(zip(VMEM_NAMES, take(len(VMEM_NAMES))))
    att, qkv = take(2)
    take(n_alias)
    dx_ref, vec_ref, ig_ref, bg_ref, ug_ref, ag_ref, qg_ref = take(7)
    bqkv, batt, bgin, bbg, bug, bag, bqg, bmg, bxg, asem, osem = refs
    crop_len, width = bbg.shape
    hidden = bug.shape[1]
    heads = width // HEAD
    base = hidden // width
    section, live, _, crop, length = assigned([(0, crop) for crop in crops], lengths, lengths)
    place = lax.rem(crop, HELD_CROPS)

    def gain(row):
        return gains[0, 0, row : row + 1, :]

    def att_copy():
        return pltpu.make_async_copy(att.at[crop], batt, asem.at[0])

    def qkv_copy():
        return pltpu.make_async_copy(qkv.at[crop], bqkv, asem.at[1])

    def body(rows):
        keys = -(-rows // 128) * 128
        started = []

        def clear(buffer):
            if rows < crop_len:
                buffer[rows:, :] = jnp.zeros((crop_len - rows, buffer.shape[1]), buffer.dtype)

        def finish(number, buffer, target):
            clear(buffer)
            copy = pltpu.make_async_copy(buffer, target, osem.at[number])
            copy.start()
            started.append(copy)

        def column(row, values, start=0):
            vec_ref[row : row + 1, start : start + values.shape[1]] = jnp.sum(values.astype(F32), 0, keepdims=True)

        valid = lax.broadcasted_iota(jnp.int32, (rows, 1), 0) < length
        g = jnp.where(valid, bgin[:rows, :].astype(F32), 0.0)
        n2 = kept["n2"][place, :rows, :].astype(F32)
        inv1 = kept["inv"][place, :rows, 0:1]
        inv2 = kept["inv"][place, :rows, 1:2]
        sum_two = norm_backward(g * gain(1), n2, inv2)
        bg = sum_two.astype(BF16)
        bbg[:rows, :] = bg
        finish(0, bbg, bg_ref.at[crop])
        column(base + 5, g)
        column(base + 7, g * n2)
        column(base + 4, bg)
        side = [sum_two]

        def cols(part):
            return slice(part * width, (part + 1) * width)

        def descend(part):
            return mm(bg, wdown[0, cols(part), :], NT)

        def slope(part, grad):
            grad = (grad * kept["gp"][place, :rows, cols(part)].astype(F32)).astype(BF16)
            bug[:rows, cols(part)] = grad
            column(part, grad)
            return grad

        def ascend(part, grad):
            side[0] = side[0] + mm(grad, wup[0, :, cols(part)], NT)

        each_lagged(base, descend, slope, ascend)
        finish(1, bug, ug_ref.at[crop])
        n1 = kept["n1"][place, :rows, :].astype(F32)
        side = side[0]
        sum_one = norm_backward(side * gain(0), n1, inv1)
        ag = sum_one.astype(BF16)
        bag[:rows, :] = ag
        finish(2, bag, ag_ref.at[crop])
        column(base + 3, side)
        column(base + 6, side * n1)
        column(base + 2, ag)
        bmg[:rows, :] = mm(ag, wout[0], NT).astype(BF16)
        att_copy().wait()
        qkv_copy().wait()
        masks = head_masks()
        scale = HEAD**-0.5
        sums = [None]

        def pair(part, head, row_count):
            start = part * width + head // 2 * 2 * HEAD
            return jnp.where(masks[head % 2], bqkv[:row_count, start : start + 2 * HEAD], 0)

        def attention_grad(head):
            start = head // 2 * 2 * HEAD
            return mm(bmg[:rows, start : start + 2 * HEAD], pair(2, head, keys), NT)

        def score_grad(head, grad):
            wide = batt[head, :rows, :keys].astype(F32)
            both = wide * grad
            return (both - wide * jnp.sum(both, -1, keepdims=True)).astype(BF16)

        def spread(head, score):
            start = head // 2 * 2 * HEAD
            mg = jnp.where(masks[head % 2], bmg[:rows, start : start + 2 * HEAD], 0)
            parts = (
                mm(score, pair(1, head, keys)),
                mm(score, pair(0, head, rows), TN),
                mm(batt[head, :rows, :keys], mg, TN),
            )
            if head % 2 == 0:
                sums[0] = parts
                return
            dq, dk, dv = (old + new for old, new in zip(sums[0], parts))
            dq = (dq * scale).astype(BF16)
            dv = dv[:rows].astype(BF16)
            bqg[:rows, start : start + 2 * HEAD] = dq
            bqg[:rows, width + start : width + start + 2 * HEAD] = (dk[:rows] * scale).astype(BF16)
            bqg[:rows, 2 * width + start : 2 * width + start + 2 * HEAD] = dv
            column(base, dq, start)
            column(base + 1, dv, start)

        each_lagged(heads, attention_grad, score_grad, spread)
        finish(3, bqg, qg_ref.at[crop])
        xg = sum_one + mm(bqg[:rows, :], wqkv[0], NT)
        dx = xg.astype(BF16)
        dx_ref[:rows, :] = jnp.where(section == 0, sent[:rows, :], dx)
        if rows < crop_len:
            dx_ref[rows:, :] = jnp.where(section == 0, sent[rows:, :], 0)
        bxg[:rows, :] = jnp.where(section == 0, xg, dx.astype(F32))
        finish(4, bxg, ig_ref.at[crop])
        for copy in started:
            copy.wait()

    @pl.when(jnp.logical_not(live))
    def _():
        vec_ref[...] = jnp.zeros(vec_ref.shape, F32)
        dx_ref[...] = sent[...]

    @pl.when(live)
    def _():
        if recv is not None:

            @pl.when(section == 0)
            def _():
                bgin[...] = recv[...]

        @pl.when(section != 0)
        def _():
            bgin[...] = cot[crop]

        att_copy().start()
        qkv_copy().start()
        dispatch(length, crop_len, body)


def backward_call(lengths, crops, cot, sent, recv, weights, held, state, grads, order=()):
    crop_count, crop_len, width = cot.shape
    hidden = weights[2].shape[-1]
    shapes = {
        "ig": ((crop_count, crop_len, width), F32),
        "bg": ((crop_count, crop_len, width), BF16),
        "ug": ((crop_count, crop_len, hidden), BF16),
        "ag": ((crop_count, crop_len, width), BF16),
        "qg": ((crop_count, crop_len, 3 * width), BF16),
    }
    names = tuple(shapes)
    aliased = in_hbm(*[grads[name] for name in names]) if grads else []
    arrived = [] if recv is None else [recv]
    operands = [lengths, *in_vmem(cot), sent, *arrived, *in_vmem(*held), weights[6]]
    order = list(order)
    operands += in_vmem(*[state[name] for name in VMEM_NAMES]) + in_hbm(state["att"], state["qkv"]) + order + aliased
    first = 10 + len(arrived) + len(VMEM_NAMES) + len(order)
    outs = pl.pallas_call(
        functools.partial(backward_kernel, crops, recv is None, len(order) + len(aliased)),
        out_shape=[
            jax.ShapeDtypeStruct((crop_len, width), BF16),
            jax.ShapeDtypeStruct((hidden // width + 8, width), F32),
        ]
        + [pltpu.HBM(*shapes[name]) for name in names],
        in_specs=[SMEM] + [VMEM] * (len(arrived) + 7 + len(VMEM_NAMES)) + [ANY] * (2 + len(order) + len(aliased)),
        out_specs=[VMEM, VMEM] + [ANY] * len(names),
        input_output_aliases={first + i: 2 + i for i in range(len(aliased))},
        scratch_shapes=[
            pltpu.VMEM((crop_len, 3 * width), BF16),
            pltpu.VMEM((width // HEAD, crop_len, crop_len), BF16),
            pltpu.VMEM((crop_len, width), BF16),
            pltpu.VMEM((crop_len, width), BF16),
            pltpu.VMEM((crop_len, hidden), BF16),
            pltpu.VMEM((crop_len, width), BF16),
            pltpu.VMEM((crop_len, 3 * width), BF16),
            pltpu.VMEM((crop_len, width), BF16),
            pltpu.VMEM((crop_len, width), F32),
            pltpu.SemaphoreType.DMA((2,)),
            pltpu.SemaphoreType.DMA((5,)),
        ],
        compiler_params=pltpu.CompilerParams(vmem_limit_bytes=HELD_LIMIT),
        cost_estimate=crop_cost(weights, crop_len),
        name="backward_crop",
    )(*operands)
    return outs[0], outs[1], dict(zip(names, outs[2:]))


def ring_place(core, chip, count):
    return jnp.where(core == 0, chip, count - 1 - chip)


def chip_number(dp_index, rep_index, rep):
    return jnp.where(lax.div(dp_index, 2) == 0, rep_index, 2 * rep - 1 - rep_index)


def weights_kernel(groups, *refs):
    pairs = 1 + max(dot[0] for dots in groups for dot in dots)
    lefts, rights = refs[:pairs], refs[pairs : 2 * pairs]
    refs = refs[-(3 * len(groups) + 2 * pairs + 3) :]
    outs, refs = refs[: 2 * len(groups)], refs[2 * len(groups) :]
    held_lefts, held_rights, refs = refs[:pairs], refs[pairs : 2 * pairs], refs[2 * pairs :]
    held_outs, (lsem, rsem, osem) = refs[:-3], refs[-3:]
    count = lax.axis_size("rep") * 2
    core = lax.rem(lax.axis_index("dp"), 2)
    chip = chip_number(lax.axis_index("dp"), lax.axis_index("rep"), count // 2)
    place = ring_place(core, chip, count)
    tile, width = held_lefts[0].shape[2], held_rights[0].shape[2]

    def slot_of(number, half, part):
        return half * (held_lefts[number].shape[0] // 2) + part

    def left_copy(number, half, part):
        which = jnp.where(half == 0, 1 - core, core)
        start = pl.multiple_of(slot_of(number, which, part) * tile, 128)
        source = lefts[number].at[pl.ds(0, held_lefts[number].shape[1]), pl.ds(start, tile)]
        slot = slot_of(number, half, part)
        return pltpu.make_async_copy(source, held_lefts[number].at[slot], lsem.at[number, slot])

    def right_copy(number, part):
        source = rights[number].at[:, pl.ds(part * width, width)]
        return pltpu.make_async_copy(source, held_rights[number].at[part], rsem.at[number, part])

    def out_copy(group, half, step, target):
        rows = held_outs[group].shape[1] // count
        block = lax.rem(jnp.where(half == 0, count - 1 - place, place) - step + count, count)
        source = held_outs[group].at[half, pl.ds(pl.multiple_of(block * rows, 16), rows)]
        return pltpu.make_async_copy(source, outs[2 * group + target].at[step], osem.at[group, half, step])

    def firsts():
        seen = set()
        for group, dots in enumerate(groups):
            for step, (number, left, right) in enumerate(dots):
                fresh = [key not in seen for key in ((0, number, left), (1, number, right))]
                seen |= {(0, number, left), (1, number, right)}
                yield group, step, number, left, right, fresh

    for half in range(2):
        for _, _, number, left, right, fresh in firsts():
            if fresh[0]:
                left_copy(number, half, left).start()
            if fresh[1] and half == 0:
                right_copy(number, right).start()

    @pl.loop(0, 2)
    def _(half):
        for group, step, number, left, right, fresh in firsts():
            if fresh[0]:
                left_copy(number, half, left).wait()
            if fresh[1]:

                @pl.when(half == 0)
                def _():
                    right_copy(number, right).wait()

            product = mm(held_lefts[number][slot_of(number, half, left)], held_rights[number][right], TN).astype(BF16)
            if held_outs[group].shape[1] == tile:
                held_outs[group][half, :, step * width : (step + 1) * width] = product
            else:
                held_outs[group][half, step * tile : (step + 1) * tile, :] = product
            if step == len(groups[group]) - 1:
                for target in range(2):

                    @pl.when(half == target)
                    def _():
                        for number in range(count):
                            out_copy(group, half, number, target).start()

    for group in range(len(groups)):
        for half in range(2):
            for step in range(count):
                out_copy(group, half, step, half).wait()


def weights_call(pairs, groups, order=()):
    lefts, rights = ([array.reshape(-1, array.shape[-1]) for array in side] for side in zip(*pairs))
    tokens, width = rights[0].shape
    tile = width // 2
    left_parts = [left.shape[1] // tile for left in lefts]
    right_parts = [right.shape[1] // width for right in rights]
    count = lax.axis_size("rep") * 2
    shapes = []
    for dots in groups:
        down = left_parts[dots[0][0]] // 2
        shapes.append((down * tile, len(dots) // down * width))
    blocks = [(count, rows // count, columns) for rows, columns in shapes]
    outs = pl.pallas_call(
        functools.partial(weights_kernel, groups),
        out_shape=[pltpu.HBM(block, BF16) for block in blocks for _ in range(2)],
        in_specs=[ANY] * (2 * len(pairs) + len(order)),
        out_specs=[ANY] * (2 * len(groups)),
        scratch_shapes=[pltpu.VMEM((parts, tokens, tile), BF16) for parts in left_parts]
        + [pltpu.VMEM((parts, tokens, width), BF16) for parts in right_parts]
        + [pltpu.VMEM((2, *shape), BF16) for shape in shapes]
        + [
            pltpu.SemaphoreType.DMA((len(pairs), max(left_parts))),
            pltpu.SemaphoreType.DMA((len(pairs), max(right_parts))),
            pltpu.SemaphoreType.DMA((len(groups), 2, count)),
        ],
        compiler_params=pltpu.CompilerParams(vmem_limit_bytes=WEIGHTS_LIMIT),
        cost_estimate=pl.CostEstimate(
            flops=4 * tokens * sum(rows * columns for rows, columns in shapes), bytes_accessed=40_000_000, transcendentals=0
        ),
        name="weight_gradients",
    )(*in_hbm(*lefts, *rights), *order)
    return [(outs[2 * number], outs[2 * number + 1]) for number in range(len(groups))]


def write_kernel(mine, outs_count, *refs):
    value, refs = refs[0], refs[1 if mine else 1 + outs_count :]
    outs, wide, osem = refs[:-2], refs[-2], refs[-1]
    small = outs[-1] if outs[-1].dtype == BF16 else None
    targets = outs if small is None else outs[:-1]
    count, rows, _ = wide.shape
    core = lax.rem(lax.axis_index("dp"), 2)
    whose = core if mine else 1 - core
    copies = []
    for block in range(count):
        wide[block] = value[block, :rows, :].astype(F32)
        row = pl.multiple_of((whose * count + block) * rows, 16)
        start = 0
        for target in targets:
            part = wide.at[block, :, pl.ds(start, target.shape[1])]
            copies.append(pltpu.make_async_copy(part, target.at[pl.ds(row, rows)], osem.at[len(copies)]))
            copies[-1].start()
            start += target.shape[1]
        if small is not None:
            origin = ring_place(whose, (block - 1) % count, count)
            part = value.at[block, pl.ds(rows, value.shape[1] - rows)]
            copies.append(pltpu.make_async_copy(part, small.at[whose, origin], osem.at[len(copies)]))
            copies[-1].start()
    for copy in copies:
        copy.wait()


def write_call(mine, value, rows, widths, outs):
    count, all_rows, columns = value.shape
    shapes = [pltpu.HBM((2 * count * rows, width), F32) for width in widths]
    if all_rows > rows:
        shapes.append(pltpu.HBM((2, count, all_rows - rows, columns), BF16))
    return pl.pallas_call(
        functools.partial(write_kernel, mine, len(shapes)),
        out_shape=shapes,
        in_specs=[VMEM] + [ANY] * len(outs),
        out_specs=[ANY] * len(shapes),
        input_output_aliases={1 + n: n for n in range(len(outs))},
        scratch_shapes=[pltpu.VMEM((count, rows, columns), F32), pltpu.SemaphoreType.DMA((3 * count,))],
        compiler_params=pltpu.CompilerParams(vmem_limit_bytes=PASS_LIMIT),
        cost_estimate=pl.CostEstimate(flops=0, bytes_accessed=6 * value.size, transcendentals=0),
        name="write_half",
    )(value, *in_hbm(*outs))


def small_kernel(rep, crops, every, b_up, biases, gains, pooled_query, pooled_key):
    count = every.shape[1]
    fixed = b_up.shape[1] // every.shape[3] + 8
    total = None
    for core in range(2):
        for chip in range(count):
            rows = every[core, chip].astype(F32)
            total = rows[:fixed] if total is None else total + rows[:fixed]
            y, z = (0, chip) if chip < rep else (1, 2 * rep - 1 - chip)
            first = ((2 * y + core) * rep + z) * crops
            pooled_query[first : first + crops, :] = rows[fixed : fixed + crops]
            pooled_key[first : first + crops, :] = rows[fixed + crops : fixed + 2 * crops]
    width = every.shape[3]
    for row in range(fixed - 8):
        b_up[:, row * width : (row + 1) * width] = total[row : row + 1]
    biases[...] = total[fixed - 8 : fixed - 2]
    gains[...] = total[fixed - 2 :]


def small_call(every, hidden, rep, crops):
    width = every.shape[3]
    shapes = [(1, hidden), (6, width), (2, width), (4 * rep * crops, width), (4 * rep * crops, width)]
    return pl.pallas_call(
        functools.partial(small_kernel, rep, crops),
        out_shape=[jax.ShapeDtypeStruct(shape, F32) for shape in shapes],
        in_specs=[VMEM],
        out_specs=[VMEM] * 5,
        name="small_sums",
    )(every)


def ring_plan(dp, rep):
    chips = [(0, z) for z in range(rep)] + [(1, z) for z in reversed(range(rep))]
    count = len(chips)
    pairs = []
    for core in range(2):
        order = chips if core == 0 else chips[::-1]
        index = [(2 * y + core) * rep + z for y, z in order]
        pairs += [(device, index[(place + 1) % count]) for place, device in enumerate(index)]
    return count, pairs


def tied(value, *others):
    return lax.optimization_barrier((value, *others))[0]


class RingSum:
    def __init__(self, own, other, place, plan):
        self.count, self.pairs = plan
        self.own, self.other, self.place = own, other, place
        self.moving = self.block(0).astype(BF16)
        self.step, self.extra, self.half = 0, None, None

    def block(self, step):
        return self.own[step].astype(F32) + self.other[step].astype(F32)

    def done(self):
        return self.step == 2 * self.count - 2

    def advance(self, last):
        self.step += 1
        spread = self.step - self.count + 1
        moving = tied(lax.ppermute(self.moving, AXES, self.pairs), last)
        if spread <= 0:
            moving = moving.astype(F32) + self.block(self.step)
            moving = lax.reduce_precision(moving, 8, 7).astype(BF16)
            if spread == 0 and self.extra is not None:
                moving = jnp.concatenate([moving, self.extra])
            if spread == 0:
                self.half = jnp.zeros((self.count, *moving.shape), BF16)
        self.moving = moving
        if spread >= 0:
            number = jnp.mod(self.place + 1 - spread, self.count)
            self.half = lax.dynamic_update_index_in_dim(self.half, moving, number, 0)
        return moving


AXES = ("dp", "rep")


def on_device(
    query_input,
    key_input,
    query_lengths,
    key_lengths,
    cotangent,
    w_qkv,
    w_out,
    w_up,
    w_down,
    b_up,
    biases,
    gains,
):
    section = lax.axis_index("section")
    dp, rep = lax.axis_size("dp"), lax.axis_size("rep")
    crops, crop_len, width = query_input.shape
    hidden = w_up.shape[-1]
    weights = (w_qkv, w_out, w_up, w_down, b_up, biases, gains)

    core = lax.rem(lax.axis_index("dp"), 2)
    place = ring_place(core, chip_number(lax.axis_index("dp"), lax.axis_index("rep"), rep), 2 * rep)
    if dp == 4:
        plan = ring_plan(dp, rep)
    query_lengths, core, place, section = lax.optimization_barrier((query_lengths, core, place, section))

    def sum_of(vectors):
        return sum(lax.optimization_barrier(tuple(vectors)))

    def up(value):
        return lax.ppermute(value, "section", [(0, 1)])

    state, grads = {}, {}
    vectors = []

    lengths = (query_lengths, key_lengths)
    idle = (0, -1)
    query = lambda crop: (0, crop) if 0 <= crop < crops else idle
    key = lambda crop: (1, crop) if 0 <= crop < crops else idle
    plan_of_calls = [(query(0), idle), (query(1), idle)]
    for crop in range(crops):
        ahead = query(crop + 2) if crop + 2 < crops else key(crop + 2 - crops)
        plan_of_calls += [(ahead, query(crop)), None]
    plan_of_calls += [(key(2), key(0)), None]
    late_calls = [(key(crop), idle) for crop in range(3, crops)] + [(idle, key(crop)) for crop in range(1, crops)]
    sent_on, pooled_rows = {}, {}

    def forward(mode, call, held, state, order, later=False):
        sent, pooled, loaded, state = forward_call(
            mode, lengths, call, key_input if call[0][0] else query_input, sent_on.get(call[1]), weights, held, state, order
        )
        for number, done in enumerate(call):
            if done[1] >= 0:
                pooled_rows[number, *done] = pooled
        if call[0][1] >= 0 and not later:
            sent_on[call[0]] = up(sent)
        return sent, pooled, loaded or held, state

    def pool(member):
        first, second = (jnp.concatenate([pooled_rows[number, member, crop] for crop in range(crops)]) for number in range(2))
        return jnp.where(section == 0, first, second)

    returned = held = None
    order = []
    backs, encoders = 0, set()
    for number, call in enumerate(plan_of_calls):
        if call is not None:
            later = 2 <= number < 2 * crops + 2
            mode = "held" if call[0][0] in encoders else "load"
            encoders.add(call[0][0])
            sent, pooled, held, state = forward(mode, call, held, state, order, later)
            order = [pooled]
        else:
            assignment = (backs - 1, backs if backs < crops else -1)
            back, vector, grads = backward_call(
                query_lengths, assignment, cotangent, sent, returned, weights, held, state, grads, order
            )
            order = [vector]
            vectors.append(vector)
            if backs < crops:
                returned = lax.ppermute(back, "section", [(0, 1), (1, 0)])
                sent_on[plan_of_calls[number - 1][0]] = returned
            backs += 1

    section, core, place, vector = lax.optimization_barrier((section, core, place, sum_of(vectors)))
    swap = [(d * rep + z, (d ^ 1) * rep + z) for d in range(dp) for z in range(rep)]
    if dp == 4:
        count, ratio = 2 * rep, hidden // width
        small = jnp.concatenate([vector, pool(0)]).astype(BF16)
        used_rows = small.shape[0] + crops
        small_rows = -(-used_rows // 16) * 16
        widths = [(width,), (hidden,), (3 * width, width)]
        pairs = [(state["act"], grads["bg"]), (state["low"], grads["ug"]), (state["xs"], grads["qg"]), (state["mix"], grads["ag"])]
        groups = [
            [(0, part, 0) for part in range(ratio)],
            [(1, 0, part) for part in range(ratio)],
            [(2, 0, part) for part in range(3)] + [(3, 0, 0)],
        ]
        halves = weights_call(pairs, groups, [vector])
        waiting = [(own, lax.ppermute(theirs, AXES, swap)) for theirs, own in halves]
        rings, last = [], halves[0][1]

        def advance(last, begun=0):
            for ring in rings:
                if not ring.done():
                    last = ring.advance(last)
            while len(rings) < begun:
                rings.append(RingSum(*waiting[len(rings)], place, plan))
                last = rings[-1].moving
            return last

        last = advance(last, 1)
        for call in late_calls:
            _, pooled, _, _ = forward("pass", call, None, {}, [last])
            last = advance(pooled, 3)
        rings[0].extra = jnp.pad(
            jnp.concatenate([small, pool(1).astype(BF16)]), ((0, small_rows - used_rows), (0, 0))
        )
        while not all(ring.done() for ring in rings):
            last = advance(last)
        swapped = [lax.ppermute(ring.half, AXES, swap) for ring in rings]
        outs = [write_call(True, ring.half, ring.own.shape[1], cut, []) for ring, cut in zip(rings, widths)]
        outs = [
            write_call(False, other, ring.own.shape[1], cut, out)
            for ring, other, cut, out in zip(rings, swapped, widths, outs)
        ]
        (grad_down, every), grad_up, grad_last = outs
        totals = [grad_down, *grad_up, *grad_last]
        grad_b_up, grad_biases, grad_gains, pooled_query, pooled_key = small_call(every, hidden, rep, crops)
    else:
        totals = []
        for left, right in (("act", "bg"), ("low", "ug"), ("xs", "qg"), ("mix", "ag")):
            left, right = (a.reshape(-1, a.shape[-1]) for a in (state[left][:crops], grads[right]))
            totals.append(lax.psum(mm(left, right, TN), AXES))
        for call in late_calls:
            forward("pass", call, None, {}, [])
        vector = lax.psum(vector, AXES)
        ratio = hidden // width
        grad_b_up = vector[:ratio].reshape(1, hidden)
        grad_biases, grad_gains = vector[ratio : ratio + 6], vector[ratio + 6 :]
        pooled_query = lax.all_gather(pool(0), AXES, axis=0, tiled=True)
        pooled_key = lax.all_gather(pool(1), AXES, axis=0, tiled=True)
    return (
        pooled_query[None],
        pooled_key[None],
        grads["ig"][None],
        totals[2][None],
        totals[3][None],
        totals[1][None],
        totals[0][None],
        grad_b_up,
        grad_biases[None],
        grad_gains[None],
    )


def solution(mesh):
    placed = (
        P(("dp", "rep"), None, None),
        P(("dp", "rep"), None, None),
        P(("dp", "rep")),
        P(("dp", "rep")),
        P(("dp", "rep"), None, None),
        P("section", None, None, None),
        P("section", None, None, None),
        P("section", None, None, None),
        P("section", None, None, None),
        P("section", None, None),
        P("section", None, None, None),
        P("section", None, None, None),
    )
    return jax.shard_map(
        on_device,
        mesh=mesh,
        in_specs=placed,
        out_specs=(
            P("section", None, None),
            P("section", None, None),
            P("section", ("dp", "rep"), None, None),
            P("section", None, None),
            P("section", None, None),
            P("section", None, None),
            P("section", None, None),
            P("section", None),
            P("section", None, None),
            P("section", None, None),
        ),
        check_vma=False,
    )
```
